32 devices in a mesh: dp: 4 (over z), fsdp: 8 (over y, x, core).
Axes of the slice: x: 2, y: 2, z: 4, core: 2. Of those that a mesh axis runs over, the one named last changes fastest.
Arguments:
- tokens: bfloat16 [8192, 2048], P(('dp', 'fsdp')), may hold values from -6 to 6
- cotangent: bfloat16 [8192, 2048], P(('dp', 'fsdp')), may hold values from -6 to 6
- query_weight: bfloat16 [2048, 2048], P(('dp', 'fsdp')), may hold values from -0.5 to 0.5
- key_weight: bfloat16 [2048, 512], P(('dp', 'fsdp')), may hold values from -0.5 to 0.5
- value_weight: bfloat16 [2048, 512], P(('dp', 'fsdp')), may hold values from -0.125 to 0.125
- output_weight: bfloat16 [2048, 2048], P(('dp', 'fsdp')), may hold values from -1.5 to 1.5
- gate_weight: bfloat16 [2048, 8192], P(('dp', 'fsdp')), may hold values from -0.125 to 0.125
- up_weight: bfloat16 [2048, 8192], P(('dp', 'fsdp')), may hold values from -0.125 to 0.125
- down_weight: bfloat16 [8192, 2048], P(('dp', 'fsdp')), may hold values from -0.375 to 0.375
- attention_gain: bfloat16 [2048], P(('dp', 'fsdp')), may hold values from 0.099609375 to 1.8984375
- feedforward_gain: bfloat16 [2048], P(('dp', 'fsdp')), may hold values from 0.099609375 to 1.8984375
- lengths: int32 [4, 4], P('dp'), may hold values from 1 to 1024, as said below
Outputs:
- output: bfloat16 [8192, 2048], P(('dp', 'fsdp'))
- grad_input: bfloat16 [8192, 2048], P(('dp', 'fsdp'))
- grad_query: float32 [2048, 2048], P(('dp', 'fsdp'))
- grad_key: float32 [2048, 512], P(('dp', 'fsdp'))
- grad_value: float32 [2048, 512], P(('dp', 'fsdp'))
- grad_out: float32 [2048, 2048], P(('dp', 'fsdp'))
- grad_gate: float32 [2048, 8192], P(('dp', 'fsdp'))
- grad_up: float32 [2048, 8192], P(('dp', 'fsdp'))
- grad_down: float32 [8192, 2048], P(('dp', 'fsdp'))
- grad_attention_gain: float32 [2048], P(('dp', 'fsdp'))
- grad_feedforward_gain: float32 [2048], P(('dp', 'fsdp'))
The draws below stay inside these ranges and needn't reach their ends.
Inputs may be any that keep to these rules, and one draw needn't show every extreme that they name: Row g gives the lengths of the 4 sequences that fill group g's 2048 tokens one after another; every row sums to 2048, and its longest sequence has exactly 1024 tokens.
All inputs are finite; a program needn't handle non-finite values.
Results may differ from the reference program's by a relative error of at most 0.023.
Values may be sent and summed in bfloat16 or wider, within the bound.
A program may use at most 640 MiB of HBM per device.

```python
import jax
import jax.numpy as jnp
from jax import lax

D = 2048
NH = 32
KVH = 8
HD = 64
FF = 8192
KVW = 512
GROUP_TOK = 2048
TOKENS = 8192
MAXLEN = 1024
NSEQ = 4
N_DP = 4


def lengths_of_group(group_key):
    remaining = jnp.array(GROUP_TOK - MAXLEN, jnp.int32)
    pieces = [jnp.array(MAXLEN, jnp.int32)]
    for position in range(NSEQ - 2):
        later = NSEQ - 2 - position
        lowest = jnp.maximum(1, remaining - later * MAXLEN).astype(jnp.int32)
        highest = jnp.minimum(MAXLEN, remaining - later).astype(jnp.int32)
        chosen = jax.random.randint(jax.random.fold_in(group_key, position), (), lowest, highest + 1, dtype=jnp.int32)
        pieces.append(chosen)
        remaining = remaining - chosen
    pieces.append(remaining)
    stacked = jnp.stack(pieces).astype(jnp.int32)
    return jax.random.permutation(jax.random.fold_in(group_key, 1000), stacked)


def draw_lengths(key, part):
    group_keys = jax.random.split(jax.random.fold_in(key, 17), TOKENS // GROUP_TOK)
    return jax.vmap(lengths_of_group)(group_keys)


def level_of(key, dims, cuts, low, top_value):
    loudness = 1.0
    for dim, parts in cuts:
        heights = jax.random.uniform(jax.random.fold_in(jax.random.fold_in(key, 6), dim), (parts,), jnp.float32, low / len(cuts), top_value / len(cuts))
        loudness = loudness * jnp.repeat(jnp.exp(heights), dims[dim] // parts).reshape((-1,) + (1,) * (len(dims) - 1 - dim))
    return loudness


def normal_values(stream_key, extent, deviation, most, cuts=(), kind=jnp.bfloat16):
    factor_of = level_of(stream_key, extent, cuts, -0.22, 0.18) if cuts else 1.0
    entries = jax.random.normal(stream_key, extent, jnp.float32) * deviation * factor_of
    return jnp.minimum(jnp.maximum(entries, -most), most).astype(kind)


def setup_inputs(seed: int = 0) -> dict:
    key_list = jax.random.split(jax.random.key(seed), 13)
    return {
        "tokens": normal_values(key_list[0], (TOKENS, D), 1.0, 6.0, ((0, 32),)),
        "cotangent": normal_values(key_list[1], (TOKENS, D), 1.0, 6.0, ((0, 32),)),
        "query_weight": normal_values(key_list[2], (D, D), (D // 16) ** -0.5, 0.5, ((0, 32),)),
        "key_weight": normal_values(key_list[3], (D, KVW), (D // 16) ** -0.5, 0.5, ((0, 32),)),
        "value_weight": normal_values(key_list[4], (D, KVW), D ** -0.5, 0.125, ((0, 32),)),
        "output_weight": normal_values(key_list[5], (D, D), 16 ** -0.5, 1.5, ((0, 32),)),
        "gate_weight": normal_values(key_list[6], (D, FF), D ** -0.5, 0.125, ((0, 32),)),
        "up_weight": normal_values(key_list[7], (D, FF), D ** -0.5, 0.125, ((0, 32),)),
        "down_weight": normal_values(key_list[8], (FF, D), (FF // 32) ** -0.5, 0.375, ((0, 32),)),
        "attention_gain": jnp.clip(1.0 + 0.18 * jax.random.normal(key_list[9], (D,), jnp.float32), 0.099609375, 1.8984375).astype(jnp.bfloat16),
        "feedforward_gain": jnp.clip(1.0 + 0.18 * jax.random.normal(key_list[10], (D,), jnp.float32), 0.099609375, 1.8984375).astype(jnp.bfloat16),
        "lengths": draw_lengths(jax.random.fold_in(key_list[12], 71), 0),
    }


EPSILON = 1e-05
RESIDUAL_SCALE = 0.22
ATTENTION_SCALE = 0.015625
ROPE_BASE = 10000000.0
MASKED = -1e+30
PRECISION_MAX = lax.Precision.HIGHEST

@jax.custom_vjp
def low(v):
    return lax.optimization_barrier(v.astype(jnp.bfloat16)).astype(jnp.float32)

@jax.custom_vjp
def reduced_gradient(v):
    return v

def low_keep(v):
    return (low(v), None)

def low_pass(kept, grad):
    return (grad,)

def back_keep(v):
    return (v, None)

def back_low(kept, grad):
    return (low(grad),)
low.defvjp(low_keep, low_pass)
reduced_gradient.defvjp(back_keep, back_low)

def dense(left, right):
    return jnp.dot(left, right, precision=PRECISION_MAX, preferred_element_type=jnp.float32)

def rms_norm(values, gain):
    return values * lax.rsqrt(lax.optimization_barrier(jnp.mean(values * values, axis=1, keepdims=True)) + EPSILON) * gain[None, :]

def rotate(values, positions, head_count, direction):
    row_count = values.shape[0]
    head_width = values.shape[1] // head_count
    half_width = head_width // 2
    frequency = ROPE_BASE ** (-(2.0 * jnp.arange(half_width, dtype=jnp.float32)) / head_width)
    angles = positions.astype(jnp.float32)[:, None] * frequency[None, :]
    cosine = jnp.cos(angles)[:, None, :]
    sine_part = direction * jnp.sin(angles)[:, None, :]
    reshaped_rows = values.reshape(row_count, head_count, head_width)
    first_half = reshaped_rows[:, :, :half_width]
    second_half = reshaped_rows[:, :, half_width:]
    turned = jnp.concatenate([first_half * cosine - second_half * sine_part, second_half * cosine + first_half * sine_part], axis=2)
    return turned.reshape(row_count, head_count * head_width)

def sequence_tables(lengths_row, group_tokens):
    lengths_row = lengths_row.astype(jnp.int32)
    sequence_count = lengths_row.shape[0]
    finish = jnp.cumsum(lengths_row).astype(jnp.int32)
    opening = (finish - lengths_row).astype(jnp.int32)
    token_place = jnp.arange(group_tokens, dtype=jnp.int32)
    segment = lax.optimization_barrier(jnp.sum((token_place[:, None] >= finish[None, :]).astype(jnp.int32), axis=1)).astype(jnp.int32)
    member = segment[:, None] == jnp.arange(sequence_count, dtype=jnp.int32)[None, :]
    first_place = lax.optimization_barrier(jnp.sum(jnp.where(member, opening[None, :], 0), axis=1)).astype(jnp.int32)
    return (segment, (token_place - first_place).astype(jnp.int32))

def attention(queries, keys, values, segment, position):
    query_block = min(512, GROUP_TOK)
    block_count = GROUP_TOK // query_block
    group_size = NH // KVH
    gathered_keys = keys.reshape(GROUP_TOK, KVH, HD)
    gathered_values = values.reshape(GROUP_TOK, KVH, HD)

    def one_block(block_inputs):
        block_queries, query_segment, query_position = block_inputs
        reshaped_rows = block_queries.reshape(query_block, KVH, group_size, HD)
        unscaled_logits = reduced_gradient(jnp.einsum('akzv,ikv->kzai', reshaped_rows, gathered_keys, precision=PRECISION_MAX) * ATTENTION_SCALE)
        visible = (query_segment[:, None] == segment[None, :]) & (position[None, :] <= query_position[:, None])
        masked = jnp.where(visible[None, None], unscaled_logits, MASKED)
        peak_score = lax.optimization_barrier(jnp.max(masked, axis=3, keepdims=True))
        exponent = jnp.exp(masked - peak_score)
        probabilities = low(exponent / lax.optimization_barrier(jnp.sum(exponent, axis=3, keepdims=True)))
        merged_heads = jnp.einsum('ymqp,pyj->qymj', probabilities, gathered_values, precision=PRECISION_MAX)
        return merged_heads.reshape(query_block, NH * HD)
    stacked = lax.map(jax.checkpoint(one_block), (queries.reshape(block_count, query_block, NH * HD), segment.reshape(block_count, query_block), position.reshape(block_count, query_block)))
    return stacked.reshape(GROUP_TOK, NH * HD)

def layer(inputs, query_weight, key_weight, value_weight, output_weight, gate_weight, up_weight, down_weight, attention_gain, feedforward_gain, segment, position):
    normed_one = low(rms_norm(inputs, attention_gain))
    queries = low(rotate(reduced_gradient(dense(normed_one, query_weight)), position, NH, 1.0))
    keys = low(rotate(reduced_gradient(dense(normed_one, key_weight)), position, KVH, 1.0))
    values = low(reduced_gradient(dense(normed_one, value_weight)))
    mixed_low = low(reduced_gradient(attention(queries, keys, values, segment, position)))
    branch_one = reduced_gradient(dense(mixed_low, output_weight))
    residual = inputs + RESIDUAL_SCALE * branch_one
    normed_two = low(rms_norm(residual, feedforward_gain))
    gate = reduced_gradient(dense(normed_two, gate_weight))
    upward = reduced_gradient(dense(normed_two, up_weight))
    hidden = low(jax.nn.silu(gate) * upward)
    branch_two = reduced_gradient(dense(hidden, down_weight))
    return residual + RESIDUAL_SCALE * branch_two

def reference(tokens, cotangent, query_weight, key_weight, value_weight, output_weight, gate_weight, up_weight, down_weight, attention_gain, feedforward_gain, lengths):
    weights = tuple((weight_item.astype(jnp.float32) for weight_item in (query_weight, key_weight, value_weight, output_weight, gate_weight, up_weight, down_weight, attention_gain, feedforward_gain)))
    group_inputs = tokens.astype(jnp.float32).reshape(N_DP, GROUP_TOK, D)
    group_cotangents = cotangent.astype(jnp.float32).reshape(N_DP, GROUP_TOK, D)

    def one_group(totals, scanned):
        group_tokens, group_cotangent, lengths_row = scanned
        segment, position = sequence_tables(lengths_row, GROUP_TOK)

        def forward(group_values, *params):
            return layer(group_values, *params, segment, position)
        result, pullback = jax.vjp(forward, group_tokens, *weights)
        gradients = pullback(group_cotangent)
        totals = tuple((running + gradient for running, gradient in zip(totals, gradients[1:])))
        return (totals, (result.astype(jnp.bfloat16), gradients[0].astype(jnp.bfloat16)))
    starting = tuple((jnp.zeros(weight_item.shape, jnp.float32) for weight_item in weights))
    totals, (outputs, grad_inputs) = lax.scan(one_group, starting, (group_inputs, group_cotangents, lengths))
    return (outputs.reshape(TOKENS, D), grad_inputs.reshape(TOKENS, D), totals[0], totals[1], totals[2], totals[3], totals[4], totals[5], totals[6], totals[7], totals[8])
```

```python
import functools

import jax
import jax.numpy as jnp
from jax import lax
from jax.experimental import pallas as pl
from jax.experimental.pallas import tpu as pltpu
from jax.sharding import PartitionSpec as P

NH = 32
KVH = 8
HD = 64
HALF = HD // 2

EPSILON = 1e-05
RESIDUAL_SCALE = 0.22
ATTENTION_SCALE = 0.015625
ROPE_BASE = 10000000.0
MASKED = -1e30
BLOCK = 256
CHUNKS = 2
PIECES = 4
VMEM_BYTES = 58 * 1024 * 1024
MESH = pl.DeviceIdType.MESH
BF16 = jnp.bfloat16
F32 = jnp.float32


def dot_nn(left, right):
    return jnp.dot(left, right, preferred_element_type=F32)


def dot_nt(left, right):
    return lax.dot_general(left, right, (((1,), (1,)), ((), ())), preferred_element_type=F32)


def dot_tn(left, right):
    return lax.dot_general(left, right, (((0,), (0,)), ((), ())), preferred_element_type=F32)


def flip(index, mask):
    return index + mask * (1 - 2 * ((index // mask) % 2))


def plane_masks(member_count):
    masks = []
    mask = 2
    while mask < member_count:
        masks.append(mask)
        mask *= 2
    return masks


def hop(index, step, masks):
    core = index % 2
    return (1 - core) * flip(index, masks[step]) + core * flip(index, masks[-1 - step])


def walk(index, subset, masks):
    for step in range(len(masks)):
        if (subset >> step) & 1:
            index = hop(index, step, masks)
    return index


def greet(group, member, masks):
    barrier = pltpu.get_barrier_semaphore()
    partners = [hop(member, step, masks) for step in range(len(masks))] + [flip(member, 1)]
    for partner in partners:
        pl.semaphore_signal(barrier, inc=1, device_id=(group, partner), device_id_type=MESH)
    pl.semaphore_wait(barrier, len(partners))


def gather_kernel(
    member_count, own_ref, all_ref, link_send, link_recv, core_send, core_recv, local_sem
):
    group = lax.axis_index("dp")
    member = lax.axis_index("fsdp")
    masks = plane_masks(member_count)
    steps = len(masks)
    rows = own_ref.shape[0]
    piece = rows // PIECES
    greet(group, member, masks)

    def place(block, part):
        return all_ref.at[pl.ds(pl.multiple_of(block * rows + part * piece, piece), piece)]

    def link_copy(step, subset, part):
        number = (1 << step) - 1 + subset
        block = walk(member, subset, masks)
        source = own_ref.at[pl.ds(part * piece, piece)] if subset == 0 else place(block, part)
        return pltpu.make_async_remote_copy(
            source,
            place(block, part),
            link_send.at[number, part],
            link_recv.at[number, part],
            device_id=(group, hop(member, step, masks)),
            device_id_type=MESH,
        )

    def core_copy(subset, part):
        block = walk(member, subset, masks)
        source = own_ref.at[pl.ds(part * piece, piece)] if subset == 0 else place(block, part)
        return pltpu.make_async_remote_copy(
            source,
            place(block, part),
            core_send.at[subset, part],
            core_recv.at[subset, part],
            device_id=(group, flip(member, 1)),
            device_id_type=MESH,
        )

    for part in range(PIECES):
        for step in range(steps):
            link_copy(step, 0, part).start()
    keep = pltpu.make_async_copy(
        own_ref, all_ref.at[pl.ds(pl.multiple_of(member * rows, rows), rows)], local_sem
    )
    keep.start()
    for part in range(PIECES):
        core_copy(0, part).start()
    for step in range(steps):
        for part in range(PIECES):
            for subset in range(1 << step):
                link_copy(step, subset, part).wait_recv()
                arrived = subset | (1 << step)
                for later in range(step + 1, steps):
                    link_copy(later, arrived, part).start()
                core_copy(arrived, part).start()
    for part in range(PIECES):
        for subset in range(1 << steps):
            core_copy(subset, part).wait()
    for part in range(PIECES):
        for step in range(steps):
            for subset in range(1 << step):
                link_copy(step, subset, part).wait_send()
    keep.wait()


def plane_gather(own, member_count, collective_id):
    rows, width = own.shape
    steps = len(plane_masks(member_count))
    blocks = 1 << steps
    total = member_count * rows
    return pl.pallas_call(
        functools.partial(gather_kernel, member_count),
        out_shape=jax.ShapeDtypeStruct((total, width), own.dtype),
        in_specs=[pl.BlockSpec(memory_space=pl.ANY)],
        out_specs=pl.BlockSpec(memory_space=pl.ANY),
        scratch_shapes=[
            pltpu.SemaphoreType.DMA((blocks - 1, PIECES)),
            pltpu.SemaphoreType.DMA((blocks - 1, PIECES)),
            pltpu.SemaphoreType.DMA((blocks, PIECES)),
            pltpu.SemaphoreType.DMA((blocks, PIECES)),
            pltpu.SemaphoreType.DMA,
        ],
        compiler_params=pltpu.CompilerParams(collective_id=collective_id, has_side_effects=True),
        cost_estimate=pl.CostEstimate(
            flops=0, bytes_accessed=60 * total * width, transcendentals=0
        ),
        name="plane_gather",
    )(own)


def scatter_kernel(
    member_count,
    part_ref,
    sum_ref,
    core_buffer,
    link_buffer,
    held,
    link_send,
    link_recv,
    core_send,
    core_recv,
):
    group = lax.axis_index("dp")
    member = lax.axis_index("fsdp")
    sibling = flip(member, 1)
    masks = plane_masks(member_count)
    steps = len(masks)
    blocks = 1 << steps
    rows = sum_ref.shape[0]
    piece = rows // PIECES
    greet(group, member, masks)

    def source_rows(block, part):
        return pl.ds(pl.multiple_of(block * rows + part * piece, piece), piece)

    def core_copy(subset, part):
        block = walk(sibling, subset, masks)
        return pltpu.make_async_remote_copy(
            part_ref.at[source_rows(block, part)],
            core_buffer.at[subset, pl.ds(part * piece, piece)],
            core_send.at[subset, part],
            core_recv.at[subset, part],
            device_id=(group, sibling),
            device_id_type=MESH,
        )

    def slot(step, kept):
        return sum(blocks >> (s + 1) for s in range(step)) + (kept >> (step + 1))

    def link_copy(step, subset, part):
        kept = subset & ~(1 << step)
        number = slot(step, kept)
        return pltpu.make_async_remote_copy(
            held.at[subset, pl.ds(part * piece, piece)],
            link_buffer.at[number, pl.ds(part * piece, piece)],
            link_send.at[number, part],
            link_recv.at[number, part],
            device_id=(group, hop(member, step, masks)),
            device_id_type=MESH,
        )

    order = sorted(range(blocks), key=lambda s: (-(s & 1), -s))
    for part in range(PIECES):
        for subset in order:
            core_copy(subset, part).start()
    for part in range(PIECES):
        where = pl.ds(part * piece, piece)
        for subset in order:
            core_copy(subset, part).wait_recv()
            block = walk(member, subset, masks)
            total = part_ref[source_rows(block, part), :].astype(F32) + core_buffer[
                subset, where, :
            ].astype(F32)
            held[subset, where, :] = total.astype(BF16)
            if subset & 1:
                link_copy(0, subset, part).start()
    for step in range(steps):
        for part in range(PIECES):
            where = pl.ds(part * piece, piece)
            for kept in sorted(range(0, blocks, 2 << step), reverse=True):
                link_copy(step, kept | (1 << step), part).wait_recv()
                total = held[kept, where, :].astype(F32) + link_buffer[
                    slot(step, kept), where, :
                ].astype(F32)
                if kept == 0 and step == steps - 1:
                    sum_ref[where, :] = total
                else:
                    held[kept, where, :] = total.astype(BF16)
                if kept and (kept & (kept - 1)) != kept and (kept >> (step + 1)) & 1:
                    link_copy(step + 1, kept, part).start()
    for part in range(PIECES):
        for subset in range(blocks):
            core_copy(subset, part).wait_send()
        for step in range(steps):
            for kept in range(0, blocks, 2 << step):
                link_copy(step, kept | (1 << step), part).wait_send()


def plane_scatter(parts, member_count, collective_id):
    total, width = parts.shape
    rows = total // member_count
    steps = len(plane_masks(member_count))
    blocks = 1 << steps
    return pl.pallas_call(
        functools.partial(scatter_kernel, member_count),
        out_shape=jax.ShapeDtypeStruct((rows, width), F32),
        in_specs=[pl.BlockSpec(memory_space=pltpu.VMEM)],
        out_specs=pl.BlockSpec(memory_space=pltpu.VMEM),
        scratch_shapes=[
            pltpu.VMEM((blocks, rows, width), BF16),
            pltpu.VMEM((blocks - 1, rows, width), BF16),
            pltpu.VMEM((blocks, rows, width), BF16),
            pltpu.SemaphoreType.DMA((blocks - 1, PIECES)),
            pltpu.SemaphoreType.DMA((blocks - 1, PIECES)),
            pltpu.SemaphoreType.DMA((blocks, PIECES)),
            pltpu.SemaphoreType.DMA((blocks, PIECES)),
        ],
        compiler_params=pltpu.CompilerParams(
            collective_id=collective_id, has_side_effects=True, vmem_limit_bytes=VMEM_BYTES
        ),
        cost_estimate=pl.CostEstimate(
            flops=0, bytes_accessed=60 * total * width, transcendentals=0
        ),
        name="plane_scatter",
    )(parts)


def half_group(shape, heads):
    return (lax.broadcasted_iota(jnp.int32, shape, 1) // HALF) % heads


def full_group(shape):
    return lax.broadcasted_iota(jnp.int32, shape, 1) // HD


def forward_kernel(
    heads, first_ref, query_ref, key_ref, value_ref, start_ref, mixed_ref, lse_ref, top, total, acc
):
    step = pl.program_id(0)
    query = query_ref[...]
    start = start_ref[...]
    token = step * BLOCK + lax.broadcasted_iota(jnp.int32, (BLOCK, BLOCK), 1)
    within = lax.broadcasted_iota(jnp.int32, (BLOCK, BLOCK), 0)
    lane_head = half_group((BLOCK, query.shape[1]), heads)
    top[...] = jnp.full_like(top, MASKED)
    total[...] = jnp.zeros_like(total)
    acc[...] = jnp.zeros_like(acc)

    def one_block(block, carried):
        offset = pl.multiple_of(block * BLOCK, BLOCK)
        keys = key_ref[pl.ds(offset, BLOCK), :]
        values = value_ref[:, pl.ds(offset, BLOCK)]
        place = offset + within
        visible = (place >= start) & (place <= token)
        for head in range(heads):
            own_keys = jnp.where(lane_head == head, keys, jnp.zeros_like(keys))
            scores = jnp.where(visible, dot_nt(own_keys, query) * ATTENTION_SCALE, MASKED)
            old = top[head : head + 1, :]
            new = jnp.maximum(old, jnp.max(scores, axis=0, keepdims=True))
            weights = jnp.exp(scores - new)
            fade = jnp.exp(old - new)
            top[head : head + 1, :] = new
            total[head : head + 1, :] = total[head : head + 1, :] * fade + jnp.sum(
                weights, axis=0, keepdims=True
            )
            acc[head * HD : (head + 1) * HD, :] = acc[
                head * HD : (head + 1) * HD, :
            ] * fade + dot_nn(values, weights.astype(BF16))
        return carried

    lax.fori_loop(first_ref[step], step + 1, one_block, 0)
    for head in range(heads):
        acc[head * HD : (head + 1) * HD, :] = (
            acc[head * HD : (head + 1) * HD, :] / total[head : head + 1, :]
        )
    mixed_ref[...] = jnp.transpose(acc[...]).astype(BF16)
    lse_ref[...] = top[...] + jnp.log(total[...])


def attention_forward(first, query, keys, values, start):
    tokens, width = query.shape
    heads = width // HD
    return pl.pallas_call(
        functools.partial(forward_kernel, heads),
        grid_spec=pltpu.PrefetchScalarGridSpec(
            num_scalar_prefetch=1,
            grid=(tokens // BLOCK,),
            in_specs=[
                pl.BlockSpec((BLOCK, width), lambda i, first: (i, 0)),
                pl.BlockSpec((tokens, width), lambda i, first: (0, 0)),
                pl.BlockSpec((HD, tokens), lambda i, first: (0, 0)),
                pl.BlockSpec((1, BLOCK), lambda i, first: (0, i)),
            ],
            out_specs=[
                pl.BlockSpec((BLOCK, width), lambda i, first: (i, 0)),
                pl.BlockSpec((heads, BLOCK), lambda i, first: (0, i)),
            ],
            scratch_shapes=[
                pltpu.VMEM((heads, BLOCK), F32),
                pltpu.VMEM((heads, BLOCK), F32),
                pltpu.VMEM((width, BLOCK), F32),
            ],
        ),
        out_shape=[
            jax.ShapeDtypeStruct((tokens, width), BF16),
            jax.ShapeDtypeStruct((heads, tokens), F32),
        ],
        compiler_params=pltpu.CompilerParams(vmem_limit_bytes=VMEM_BYTES),
        cost_estimate=pl.CostEstimate(
            flops=8 * tokens * BLOCK * width * 8, bytes_accessed=8 * tokens * width, transcendentals=0
        ),
        name="attention_forward",
    )(first, query, keys, values, start)


def backward_kernel(
    heads,
    first_ref,
    query_ref,
    key_ref,
    value_ref,
    mixed_ref,
    grad_ref,
    lse_ref,
    start_ref,
    dquery_ref,
    dkey_ref,
    dvalue_ref,
):
    step = pl.program_id(0)
    query = query_ref[...]
    grad = grad_ref[...]
    start = start_ref[...]
    width = query.shape[1]
    token = step * BLOCK + lax.broadcasted_iota(jnp.int32, (BLOCK, BLOCK), 1)
    within = lax.broadcasted_iota(jnp.int32, (BLOCK, BLOCK), 0)
    half_head = half_group((BLOCK, width), heads)
    full_head = full_group((BLOCK, width))
    zero = jnp.zeros((BLOCK, width), BF16)
    product = grad.astype(F32) * mixed_ref[...].astype(F32)
    chooser = (
        lax.broadcasted_iota(jnp.int32, (8, width), 0)
        == lax.broadcasted_iota(jnp.int32, (8, width), 1) // HD
    ).astype(F32)
    correction = lax.dot_general(
        chooser,
        product,
        (((1,), (1,)), ((), ())),
        precision=lax.Precision.HIGHEST,
        preferred_element_type=F32,
    )

    @pl.when(step == 0)
    def _():
        dkey_ref[...] = jnp.zeros_like(dkey_ref)
        dvalue_ref[...] = jnp.zeros_like(dvalue_ref)

    dquery_ref[...] = jnp.zeros_like(dquery_ref)

    def one_block(block, carried):
        offset = pl.multiple_of(block * BLOCK, BLOCK)
        rows = pl.ds(offset, BLOCK)
        keys = key_ref[rows, :]
        values = value_ref[rows, :]
        place = offset + within
        visible = (place >= start) & (place <= token)
        dquery = dquery_ref[...]
        dkey = dkey_ref[rows, :]
        dvalue = dvalue_ref[rows, :]
        for head in range(heads):
            own_keys = jnp.where(half_head == head, keys, zero)
            own_values = jnp.where(full_head == head, values, zero)
            scores = dot_nt(own_keys, query) * ATTENTION_SCALE
            probs = jnp.where(visible, jnp.exp(scores - lse_ref[head : head + 1, :]), 0.0)
            pressure = dot_nt(own_values, grad)
            dscores = (probs * (pressure - correction[head : head + 1, :])).astype(BF16)
            dvalue = dvalue + dot_nn(probs.astype(BF16), jnp.where(full_head == head, grad, zero))
            dkey = dkey + dot_nn(dscores, jnp.where(half_head == head, query, zero))
            dquery = dquery + dot_tn(dscores, own_keys)
        dquery_ref[...] = dquery
        dkey_ref[rows, :] = dkey
        dvalue_ref[rows, :] = dvalue
        return carried

    lax.fori_loop(first_ref[step], step + 1, one_block, 0)


def attention_backward(first, query, keys, values, mixed, grad, lse, start):
    tokens, width = query.shape
    heads = width // HD
    by_block = pl.BlockSpec((BLOCK, width), lambda i, first: (i, 0))
    whole = pl.BlockSpec((tokens, width), lambda i, first: (0, 0))
    return pl.pallas_call(
        functools.partial(backward_kernel, heads),
        grid_spec=pltpu.PrefetchScalarGridSpec(
            num_scalar_prefetch=1,
            grid=(tokens // BLOCK,),
            in_specs=[
                by_block,
                whole,
                whole,
                by_block,
                by_block,
                pl.BlockSpec((heads, BLOCK), lambda i, first: (0, i)),
                pl.BlockSpec((1, BLOCK), lambda i, first: (0, i)),
            ],
            out_specs=[by_block, whole, whole],
        ),
        out_shape=[jax.ShapeDtypeStruct((tokens, width), F32)] * 3,
        compiler_params=pltpu.CompilerParams(vmem_limit_bytes=VMEM_BYTES),
        cost_estimate=pl.CostEstimate(
            flops=20 * tokens * BLOCK * width * 8,
            bytes_accessed=24 * tokens * width,
            transcendentals=0,
        ),
        name="attention_backward",
    )(first, query, keys, values, mixed, grad, lse, start)


def token_starts(lengths_row, group_tokens):
    count = lengths_row.shape[0]
    order = jnp.arange(count, dtype=jnp.int32)
    finish = jnp.sum(jnp.where(order[None, :] <= order[:, None], lengths_row[None, :], 0), axis=1)
    place = jnp.arange(group_tokens, dtype=jnp.int32)
    passed = place[:, None] >= finish[None, :]
    return jnp.max(jnp.where(passed, finish[None, :], 0), axis=1), place


def turn(values, cosine, sine):
    width = cosine.shape[1]
    first = values[:, :width]
    second = values[:, width:]
    return jnp.concatenate(
        [first * cosine - second * sine, second * cosine + first * sine], axis=1
    )


def inverse_norm(values):
    return lax.rsqrt(jnp.mean(values * values, axis=1, keepdims=True) + EPSILON)


def body(
    tokens,
    cotangent,
    query_weight,
    key_weight,
    value_weight,
    output_weight,
    gate_weight,
    up_weight,
    down_weight,
    attention_gain,
    feedforward_gain,
    lengths,
):
    members = lax.axis_size("fsdp")
    groups = lax.axis_size("dp")
    rows, model = tokens.shape
    group_tokens = rows * members
    shard = query_weight.shape[0]
    heads = NH // members
    width = heads * HD
    copies = members // KVH
    out_columns = model // members
    down_rows = down_weight.shape[0]
    chunk_rows = down_rows // CHUNKS
    gain_one = attention_gain.astype(F32)[:, None]
    gain_two = feedforward_gain.astype(F32)[:, None]

    scaled_query = (query_weight * gain_one).astype(BF16)
    scaled_key = (key_weight * gain_one).astype(BF16)
    scaled_value = (value_weight * gain_one).astype(BF16)
    packed = jnp.concatenate(
        [
            scaled_query.reshape(shard, members, heads, 2, HALF)
            .transpose(0, 1, 3, 2, 4)
            .reshape(shard, members, width),
            jnp.repeat(scaled_key.reshape(shard, KVH, HD), copies, axis=1),
            jnp.repeat(scaled_value.reshape(shard, KVH, HD), copies, axis=1),
            output_weight.reshape(shard, members, out_columns),
        ],
        axis=2,
    )
    packed = lax.all_to_all(packed, "fsdp", split_axis=1, concat_axis=0, tiled=True)
    packed = packed.reshape(members * shard, width + 2 * HD + out_columns)
    packed = lax.all_gather(packed, "dp", axis=0, tiled=True)

    gate_up = jnp.stack(
        [
            (weight * gain_two)
            .astype(BF16)
            .reshape(shard, groups, members, CHUNKS, chunk_rows)
            .transpose(0, 2, 3, 1, 4)
            for weight in (gate_weight, up_weight)
        ],
        axis=3,
    ).reshape(shard, members, CHUNKS * 2 * groups * chunk_rows)
    gate_up = lax.all_to_all(gate_up, "fsdp", split_axis=1, concat_axis=0, tiled=True)
    gate_up = gate_up.reshape(members * shard, CHUNKS, 2 * groups * chunk_rows)
    gate_up_chunks = []
    down_chunks = []
    for chunk in range(CHUNKS):
        gate_up_chunks.append(lax.all_gather(gate_up[:, chunk], "dp", axis=0, tiled=True))
        down_chunks.append(
            lax.all_gather(
                down_weight[chunk * chunk_rows : (chunk + 1) * chunk_rows], "dp", axis=0, tiled=True
            )
        )

    start, place = token_starts(lengths[0], group_tokens)
    first = start[::BLOCK] // BLOCK
    frequency = ROPE_BASE ** (-(2.0 * jnp.arange(HALF, dtype=F32)) / HD)
    angles = (place - start).astype(F32)[:, None] * frequency[None, :]
    cosine = jnp.tile(jnp.cos(angles), (1, heads))
    sine = jnp.tile(jnp.sin(angles), (1, heads))
    start = start[None, :]

    inputs = tokens.astype(F32)
    inverse_one = inverse_norm(inputs)
    normed_one = plane_gather((inputs * inverse_one).astype(BF16), members, 0)
    upstream = cotangent.astype(F32)
    grad_two = plane_gather((RESIDUAL_SCALE * upstream).astype(BF16), members, 1)

    key_part = packed[:, width : width + HD]
    value_part = packed[:, width + HD : width + 2 * HD]
    projection = jnp.concatenate(
        [
            packed[:, :width],
            jnp.tile(key_part[:, :HALF], (1, heads)),
            jnp.tile(key_part[:, HALF:], (1, heads)),
            jnp.tile(value_part, (1, heads)),
        ],
        axis=1,
    )
    out_piece = lax.all_to_all(
        packed[:, width + 2 * HD :], "fsdp", split_axis=0, concat_axis=1, tiled=True
    )
    projected = dot_nn(normed_one, projection)
    query = turn(projected[:, :width], cosine, sine).astype(BF16)
    keys = turn(projected[:, width : 2 * width], cosine, sine).astype(BF16)
    values = projected[:, 2 * width :].astype(BF16)
    mixed, lse = attention_forward(first, query, keys, values[:, :HD].T, start)
    branch_one = plane_scatter(dot_nn(mixed, out_piece).astype(BF16), members, 2)
    residual = inputs + RESIDUAL_SCALE * branch_one

    inverse_two = inverse_norm(residual)
    normed_two = plane_gather((residual * inverse_two).astype(BF16), members, 3)
    down_sum = 0.0
    grad_normed = 0.0
    down_grads = []
    gate_up_grads = []
    for chunk in range(CHUNKS):
        both_weight = gate_up_chunks[chunk]
        down_piece = down_chunks[chunk]
        units = down_piece.shape[0]
        both = dot_nn(normed_two, both_weight)
        gate = both[:, :units]
        up = both[:, units:]
        sigmoid = jax.nn.sigmoid(gate)
        hidden = (gate * sigmoid * up).astype(BF16)
        down_sum = down_sum + dot_nn(hidden, down_piece)
        grad_hidden = dot_nt(grad_two, down_piece)
        grad_both = jnp.concatenate(
            [
                (grad_hidden * up * sigmoid * (1.0 + gate * (1.0 - sigmoid))).astype(BF16),
                (grad_hidden * gate * sigmoid).astype(BF16),
            ],
            axis=1,
        )
        grad_normed = grad_normed + dot_nt(grad_both, both_weight)
        down_grads.append(
            lax.psum_scatter(
                dot_tn(hidden, grad_two).astype(BF16), "dp", scatter_dimension=0, tiled=True
            )
        )
        gate_up_grads.append(
            lax.psum_scatter(
                dot_tn(normed_two, grad_both).astype(BF16), "dp", scatter_dimension=0, tiled=True
            )
        )
    weighted_two = plane_scatter(grad_normed.astype(BF16), members, 4)
    grad_residual = (
        upstream
        + inverse_two * weighted_two
        - residual * inverse_two**3 * jnp.mean(weighted_two * residual, axis=1, keepdims=True)
    )
    gain_term_two = jnp.sum(weighted_two * residual * inverse_two, axis=0)

    grad_one = plane_gather((RESIDUAL_SCALE * grad_residual).astype(BF16), members, 5)
    grad_mixed = dot_nt(grad_one, out_piece).astype(BF16)
    out_grad = dot_tn(mixed, grad_one).astype(BF16)
    out_grad = lax.all_to_all(out_grad, "fsdp", split_axis=1, concat_axis=0, tiled=True)
    dquery, dkeys, dvalues = attention_backward(
        first, query, keys, values, mixed, grad_mixed, lse, start
    )
    grad_projected = jnp.concatenate(
        [
            (turn(dquery, cosine, -sine) * ATTENTION_SCALE).astype(BF16),
            (turn(dkeys, cosine, -sine) * ATTENTION_SCALE).astype(BF16),
            dvalues.astype(BF16),
        ],
        axis=1,
    )
    projection_grad = dot_tn(normed_one, grad_projected)
    key_grad = projection_grad[:, width : 2 * width].reshape(model, 2, heads, HALF).sum(axis=2)
    value_grad = projection_grad[:, 2 * width :].reshape(model, heads, HD).sum(axis=1)
    packed_grad = jnp.concatenate(
        [
            projection_grad[:, :width].astype(BF16),
            key_grad.reshape(model, HD).astype(BF16),
            value_grad.astype(BF16),
            out_grad,
        ],
        axis=1,
    )
    packed_grad = lax.psum_scatter(packed_grad, "dp", scatter_dimension=0, tiled=True)
    weighted_one = plane_scatter(dot_nt(grad_projected, projection).astype(BF16), members, 6)
    grad_inputs = (
        grad_residual
        + inverse_one * weighted_one
        - inputs * inverse_one**3 * jnp.mean(weighted_one * inputs, axis=1, keepdims=True)
    )
    gain_term_one = jnp.sum(weighted_one * inputs * inverse_one, axis=0)

    down_sum, _ = lax.optimization_barrier((down_sum.astype(BF16), weighted_one))
    branch_two = plane_scatter(down_sum, members, 7)
    output = residual + RESIDUAL_SCALE * branch_two

    both_grad = jnp.stack(gate_up_grads, axis=1).reshape(members, shard, -1)
    both_grad = lax.all_to_all(both_grad, "fsdp", split_axis=0, concat_axis=0, tiled=True)
    both_grad = (
        both_grad.reshape(members, shard, CHUNKS, 2, groups, chunk_rows)
        .transpose(3, 1, 4, 0, 2, 5)
        .reshape(2, shard, -1)
        .astype(F32)
    )
    packed_grad = lax.all_to_all(
        packed_grad.reshape(members, shard, -1), "fsdp", split_axis=0, concat_axis=0, tiled=True
    ).astype(F32)
    grad_query = (
        packed_grad[:, :, :width]
        .reshape(members, shard, 2, heads, HALF)
        .transpose(1, 0, 3, 2, 4)
        .reshape(shard, -1)
    )

    def folded(part):
        return (
            part.reshape(KVH, copies, shard, HD).sum(axis=1).transpose(1, 0, 2).reshape(shard, -1)
        )

    gains = jnp.stack([gain_term_one, gain_term_two], axis=1).reshape(-1, 2 * shard)
    gains = lax.psum_scatter(gains, ("dp", "fsdp"), scatter_dimension=0, tiled=True)
    gains = gains.reshape(shard, 2)
    return (
        output.astype(BF16),
        grad_inputs.astype(BF16),
        grad_query * gain_one,
        folded(packed_grad[:, :, width : width + HD]) * gain_one,
        folded(packed_grad[:, :, width + HD : width + 2 * HD]) * gain_one,
        packed_grad[:, :, width + 2 * HD :].transpose(1, 0, 2).reshape(shard, -1),
        both_grad[0] * gain_two,
        both_grad[1] * gain_two,
        jnp.concatenate(down_grads, axis=0).astype(F32),
        gains[:, 0] / gain_one[:, 0],
        gains[:, 1] / gain_two[:, 0],
    )


def solution(mesh):
    by_rows = P(("dp", "fsdp"), None)
    by_entries = P(("dp", "fsdp"))
    return jax.shard_map(
        body,
        mesh=mesh,
        in_specs=(by_rows,) * 9 + (by_entries,) * 2 + (P("dp", None),),
        out_specs=(by_rows,) * 9 + (by_entries,) * 2,
        check_vma=False,
    )
```

```python
import functools

import jax
import jax.numpy as jnp
from jax import lax
from jax.experimental import pallas as pl
from jax.experimental.pallas import tpu as pltpu
from jax.sharding import PartitionSpec as P

NH = 32
KVH = 8
HD = 64
HALF = HD // 2

EPSILON = 1e-05
RESIDUAL_SCALE = 0.22
ATTENTION_SCALE = 0.015625
ROPE_BASE = 10000000.0
MASKED = -1e30
BLOCK = 256
CHUNKS = 2
PIECES = 4
VMEM_BYTES = 58 * 1024 * 1024
MESH = pl.DeviceIdType.MESH
BF16 = jnp.bfloat16
F32 = jnp.float32


def dot_nn(left, right):
    return jnp.dot(left, right, preferred_element_type=F32)


def dot_nt(left, right):
    return lax.dot_general(left, right, (((1,), (1,)), ((), ())), preferred_element_type=F32)


def dot_tn(left, right):
    return lax.dot_general(left, right, (((0,), (0,)), ((), ())), preferred_element_type=F32)


def flip(index, mask):
    return index + mask * (1 - 2 * ((index // mask) % 2))


def plane_masks(member_count):
    masks = []
    mask = 2
    while mask < member_count:
        masks.append(mask)
        mask *= 2
    return masks


def hop(index, step, masks):
    core = index % 2
    return (1 - core) * flip(index, masks[step]) + core * flip(index, masks[-1 - step])


def walk(index, subset, masks):
    for step in range(len(masks)):
        if (subset >> step) & 1:
            index = hop(index, step, masks)
    return index


def greet(group, member, masks):
    barrier = pltpu.get_barrier_semaphore()
    partners = [hop(member, step, masks) for step in range(len(masks))] + [flip(member, 1)]
    for partner in partners:
        pl.semaphore_signal(barrier, inc=1, device_id=(group, partner), device_id_type=MESH)
    pl.semaphore_wait(barrier, len(partners))


def gather_kernel(
    member_count, in_order, own_ref, all_ref, link_send, link_recv, core_send, core_recv, local_sem
):
    group = lax.axis_index("dp")
    member = lax.axis_index("fsdp")
    masks = plane_masks(member_count)
    steps = len(masks)
    rows = own_ref.shape[0]
    piece = rows // PIECES
    greet(group, member, masks)

    blocks = 1 << steps

    def place(owner, subset, side, part):
        block = walk(owner, subset, masks) if in_order else subset + side * blocks
        return all_ref.at[pl.ds(pl.multiple_of(block * rows + part * piece, piece), piece)]

    def link_copy(step, subset, part):
        number = (1 << step) - 1 + subset
        here = place(member, subset, 0, part)
        there = here if in_order else place(member, subset | (1 << step), 0, part)
        return pltpu.make_async_remote_copy(
            own_ref.at[pl.ds(part * piece, piece)] if subset == 0 else here,
            there,
            link_send.at[number, part],
            link_recv.at[number, part],
            device_id=(group, hop(member, step, masks)),
            device_id_type=MESH,
        )

    def core_copy(subset, part):
        here = place(member, subset, 0, part)
        there = here if in_order else place(member, subset, 1, part)
        return pltpu.make_async_remote_copy(
            own_ref.at[pl.ds(part * piece, piece)] if subset == 0 else here,
            there,
            core_send.at[subset, part],
            core_recv.at[subset, part],
            device_id=(group, flip(member, 1)),
            device_id_type=MESH,
        )

    for part in range(PIECES):
        for step in range(steps):
            link_copy(step, 0, part).start()
    first = pl.multiple_of(member * rows, rows) if in_order else 0
    keep = pltpu.make_async_copy(own_ref, all_ref.at[pl.ds(first, rows)], local_sem)
    keep.start()
    for part in range(PIECES):
        core_copy(0, part).start()
    for step in range(steps):
        for part in range(PIECES):
            for subset in range(1 << step):
                link_copy(step, subset, part).wait_recv()
                arrived = subset | (1 << step)
                for later in range(step + 1, steps):
                    link_copy(later, arrived, part).start()
                core_copy(arrived, part).start()
    for part in range(PIECES):
        for subset in range(1 << steps):
            core_copy(subset, part).wait()
    for part in range(PIECES):
        for step in range(steps):
            for subset in range(1 << step):
                link_copy(step, subset, part).wait_send()
    keep.wait()


def plane_gather(own, member_count, collective_id, in_order):
    rows, width = own.shape
    steps = len(plane_masks(member_count))
    blocks = 1 << steps
    total = member_count * rows
    return pl.pallas_call(
        functools.partial(gather_kernel, member_count, in_order),
        out_shape=jax.ShapeDtypeStruct((total, width), own.dtype),
        in_specs=[pl.BlockSpec(memory_space=pl.ANY)],
        out_specs=pl.BlockSpec(memory_space=pl.ANY),
        scratch_shapes=[
            pltpu.SemaphoreType.DMA((blocks - 1, PIECES)),
            pltpu.SemaphoreType.DMA((blocks - 1, PIECES)),
            pltpu.SemaphoreType.DMA((blocks, PIECES)),
            pltpu.SemaphoreType.DMA((blocks, PIECES)),
            pltpu.SemaphoreType.DMA,
        ],
        compiler_params=pltpu.CompilerParams(collective_id=collective_id, has_side_effects=True),
        cost_estimate=pl.CostEstimate(
            flops=0, bytes_accessed=60 * total * width, transcendentals=0
        ),
        name="plane_gather",
    )(own)


def product_scatter_kernel(member_count, in_order, transposed, count, rows, *refs):
    lefts, rights, sum_ref = refs[:count], refs[count : 2 * count], refs[2 * count]
    held_lefts, held_rights = refs[2 * count + 1 : 3 * count + 1], refs[3 * count + 1 : 4 * count + 1]
    (
        outgoing,
        core_buffer,
        held,
        link_buffer,
        left_sem,
        right_sem,
        link_send,
        link_recv,
        core_send,
        core_recv,
    ) = refs[4 * count + 1 :]
    group = lax.axis_index("dp")
    member = lax.axis_index("fsdp")
    sibling = flip(member, 1)
    masks = plane_masks(member_count)
    steps = len(masks)
    blocks = 1 << steps
    piece = sum_ref.shape[1] // PIECES

    def left_copy(number, side, subset):
        owner = sibling if side else member
        block = walk(owner, subset, masks) if in_order else subset + side * blocks
        return pltpu.make_async_copy(
            lefts[number].at[pl.ds(pl.multiple_of(block * rows, rows), rows)],
            held_lefts[number].at[pl.ds((side * blocks + subset) * rows, rows)],
            left_sem.at[number, side, subset],
        )

    def right_copy(number):
        return pltpu.make_async_copy(rights[number], held_rights[number], right_sem.at[number])

    for number in range(count):
        right_copy(number).start()
        for side in (1, 0):
            for subset in range(blocks):
                left_copy(number, side, subset).start()
    greet(group, member, masks)

    def part(side, subset, where):
        where_rows = pl.ds((side * blocks + subset) * rows, rows)
        total = None
        for number in range(count):
            left = held_lefts[number][where_rows, :]
            if transposed:
                term = dot_nt(left, held_rights[number][where, :])
            else:
                term = dot_nn(left, held_rights[number][:, where])
            total = term if total is None else total + term
        return total

    def columns(index):
        return pl.ds(pl.multiple_of(index * piece, piece), piece)

    def core_copy(index):
        return pltpu.make_async_remote_copy(
            outgoing.at[:, columns(index)],
            core_buffer.at[:, columns(index)],
            core_send.at[index],
            core_recv.at[index],
            device_id=(group, sibling),
            device_id_type=MESH,
        )

    def slot(step, kept):
        return sum(blocks >> (s + 1) for s in range(step)) + (kept >> (step + 1))

    def link_copy(step, subset, index):
        number = slot(step, subset & ~(1 << step))
        return pltpu.make_async_remote_copy(
            held.at[pl.ds(subset * rows, rows), columns(index)],
            link_buffer.at[pl.ds(number * rows, rows), columns(index)],
            link_send.at[number, index],
            link_recv.at[number, index],
            device_id=(group, hop(member, step, masks)),
            device_id_type=MESH,
        )

    order = sorted(range(blocks), key=lambda s: (-(s & 1), -s))

    for number in range(count):
        right_copy(number).wait()
        for side in (1, 0):
            for subset in range(blocks):
                left_copy(number, side, subset).wait()

    def for_sibling(index, carried):
        where = columns(index)
        for subset in range(blocks):
            outgoing[pl.ds(subset * rows, rows), where] = part(1, subset, where).astype(BF16)
        core_copy(index).start()
        return carried

    lax.fori_loop(0, PIECES, for_sibling, 0)

    def for_links(index, carried):
        where = columns(index)
        core_copy(index).wait_recv()
        for subset in order:
            where_rows = pl.ds(subset * rows, rows)
            total = part(0, subset, where) + core_buffer[where_rows, where].astype(F32)
            if subset == 0:
                sum_ref[:, where] = total
            else:
                held[where_rows, where] = total.astype(BF16)
            if subset & 1:
                link_copy(0, subset, index).start()
        return carried

    lax.fori_loop(0, PIECES, for_links, 0)

    for step in range(steps):

        def one_step(index, carried, step=step):
            where = columns(index)
            for kept in sorted(range(0, blocks, 2 << step), reverse=True):
                link_copy(step, kept | (1 << step), index).wait_recv()
                arrived = link_buffer[pl.ds(slot(step, kept) * rows, rows), where].astype(F32)
                if kept == 0:
                    sum_ref[:, where] += arrived
                else:
                    where_rows = pl.ds(kept * rows, rows)
                    held[where_rows, where] = (
                        held[where_rows, where].astype(F32) + arrived
                    ).astype(BF16)
                if (kept >> (step + 1)) & 1:
                    link_copy(step + 1, kept, index).start()
            return carried

        lax.fori_loop(0, PIECES, one_step, 0)

    def finish(index, carried):
        core_copy(index).wait_send()
        for step in range(steps):
            for kept in range(0, blocks, 2 << step):
                link_copy(step, kept | (1 << step), index).wait_send()
        return carried

    lax.fori_loop(0, PIECES, finish, 0)


def product_scatter(lefts, rights, transposed, member_count, collective_id, in_order):
    count = len(lefts)
    total = lefts[0].shape[0]
    width = rights[0].shape[0 if transposed else 1]
    rows = total // member_count
    blocks = 1 << len(plane_masks(member_count))
    depth = sum(left.shape[1] for left in lefts)
    return pl.pallas_call(
        functools.partial(product_scatter_kernel, member_count, in_order, transposed, count, rows),
        out_shape=jax.ShapeDtypeStruct((rows, width), F32),
        in_specs=[pl.BlockSpec(memory_space=pl.ANY)] * (2 * count),
        out_specs=pl.BlockSpec(memory_space=pltpu.VMEM),
        scratch_shapes=[pltpu.VMEM(left.shape, BF16) for left in lefts]
        + [pltpu.VMEM(right.shape, BF16) for right in rights]
        + [
            pltpu.VMEM((blocks * rows, width), BF16),
            pltpu.VMEM((blocks * rows, width), BF16),
            pltpu.VMEM((blocks * rows, width), BF16),
            pltpu.VMEM(((blocks - 1) * rows, width), BF16),
            pltpu.SemaphoreType.DMA((count, 2, blocks)),
            pltpu.SemaphoreType.DMA((count,)),
            pltpu.SemaphoreType.DMA((blocks - 1, PIECES)),
            pltpu.SemaphoreType.DMA((blocks - 1, PIECES)),
            pltpu.SemaphoreType.DMA((PIECES,)),
            pltpu.SemaphoreType.DMA((PIECES,)),
        ],
        compiler_params=pltpu.CompilerParams(
            collective_id=collective_id, has_side_effects=True, vmem_limit_bytes=VMEM_BYTES
        ),
        cost_estimate=pl.CostEstimate(
            flops=2 * total * depth * width, bytes_accessed=60 * total * width, transcendentals=0
        ),
        name="product_scatter",
    )(*lefts, *rights)


def total_kernel(
    member_count, group_count, part_ref, sum_ref, near, held, far, near_send, near_recv, far_send, far_recv
):
    group = lax.axis_index("dp")
    member = lax.axis_index("fsdp")
    barrier = pltpu.get_barrier_semaphore()
    for away in range(1, member_count):
        pl.semaphore_signal(
            barrier,
            inc=1,
            device_id=(group, (member + away) % member_count),
            device_id_type=MESH,
        )
    for away in range(1, group_count):
        pl.semaphore_signal(
            barrier, inc=1, device_id=((group + away) % group_count, member), device_id_type=MESH
        )
    pl.semaphore_wait(barrier, member_count + group_count - 2)

    def near_copy(away):
        target = (member + away) % member_count
        return pltpu.make_async_remote_copy(
            part_ref.at[target],
            near.at[away],
            near_send.at[away],
            near_recv.at[away],
            device_id=(group, target),
            device_id_type=MESH,
        )

    def far_copy(away):
        return pltpu.make_async_remote_copy(
            held,
            far.at[away],
            far_send.at[away],
            far_recv.at[away],
            device_id=((group + away) % group_count, member),
            device_id_type=MESH,
        )

    for away in range(1, member_count):
        near_copy(away).start()
    total = part_ref[member]
    for away in range(1, member_count):
        near_copy(away).wait_recv()
        total = total + near[away]
    held[...] = total
    for away in range(1, group_count):
        far_copy(away).start()
    for away in range(1, group_count):
        far_copy(away).wait_recv()
        total = total + far[away]
    sum_ref[...] = total
    for away in range(1, member_count):
        near_copy(away).wait_send()
    for away in range(1, group_count):
        far_copy(away).wait_send()


def total_over_all(parts, group_count, collective_id):
    member_count, rows, lanes = parts.shape
    return pl.pallas_call(
        functools.partial(total_kernel, member_count, group_count),
        out_shape=jax.ShapeDtypeStruct((rows, lanes), F32),
        in_specs=[pl.BlockSpec(memory_space=pltpu.VMEM)],
        out_specs=pl.BlockSpec(memory_space=pltpu.VMEM),
        scratch_shapes=[
            pltpu.VMEM((member_count, rows, lanes), F32),
            pltpu.VMEM((rows, lanes), F32),
            pltpu.VMEM((group_count, rows, lanes), F32),
            pltpu.SemaphoreType.DMA((member_count,)),
            pltpu.SemaphoreType.DMA((member_count,)),
            pltpu.SemaphoreType.DMA((group_count,)),
            pltpu.SemaphoreType.DMA((group_count,)),
        ],
        compiler_params=pltpu.CompilerParams(collective_id=collective_id, has_side_effects=True),
        name="total_over_all",
    )(parts)


def half_group(shape, heads):
    return (lax.broadcasted_iota(jnp.int32, shape, 1) // HALF) % heads


def full_group(shape):
    return lax.broadcasted_iota(jnp.int32, shape, 1) // HD


def spread_keys(width):
    heads = width // HD
    row = lax.broadcasted_iota(jnp.int32, (2 * HD, width), 0)
    column = lax.broadcasted_iota(jnp.int32, (2 * HD, width), 1)
    source = column // (HALF * heads) * HALF + column % HALF
    return (row == source).astype(F32)


def spread_values(width):
    row = lax.broadcasted_iota(jnp.int32, (2 * HD, width), 0)
    column = lax.broadcasted_iota(jnp.int32, (2 * HD, width), 1)
    return (row == HD + column % HD).astype(F32)


def exact(left, right, dims):
    return lax.dot_general(
        left,
        right,
        (dims, ((), ())),
        precision=lax.Precision.HIGHEST,
        preferred_element_type=F32,
    )


def turn(values, cosine, sine):
    half = cosine.shape[1]
    first = values[:, :half]
    second = values[:, half:]
    return jnp.concatenate([first * cosine - second * sine, second * cosine + first * sine], axis=1)


def forward_kernel(
    heads,
    first_ref,
    projected_ref,
    cosine_ref,
    sine_ref,
    start_ref,
    query_ref,
    key_ref,
    value_ref,
    mixed_ref,
    lse_ref,
    value_columns,
    top,
    total,
    acc,
):
    step = pl.program_id(0)
    width = heads * HD
    start = start_ref[...]
    cosine = cosine_ref[...]
    sine = sine_ref[...]
    query = turn(projected_ref[:, :width], cosine, sine).astype(BF16)
    pair = projected_ref[:, width:]
    keys_here = turn(exact(pair, spread_keys(width), ((1,), (0,))), cosine, sine).astype(BF16)
    own_rows = pl.ds(pl.multiple_of(step * BLOCK, BLOCK), BLOCK)
    query_ref[...] = query
    key_ref[own_rows, :] = keys_here
    value_ref[...] = exact(pair, spread_values(width), ((1,), (0,))).astype(BF16)
    value_columns[:, own_rows] = jnp.transpose(pair)[HD:, :].astype(BF16)
    token = step * BLOCK + lax.broadcasted_iota(jnp.int32, (BLOCK, BLOCK), 1)
    within = lax.broadcasted_iota(jnp.int32, (BLOCK, BLOCK), 0)
    lane_head = half_group((BLOCK, width), heads)
    top[...] = jnp.full_like(top, MASKED)
    total[...] = jnp.zeros_like(total)
    acc[...] = jnp.zeros_like(acc)

    def one_block(block, carried):
        offset = pl.multiple_of(block * BLOCK, BLOCK)
        keys = key_ref[pl.ds(offset, BLOCK), :]
        values = value_columns[:, pl.ds(offset, BLOCK)]
        place = offset + within
        visible = (place >= start) & (place <= token)
        for head in range(heads):
            own_keys = jnp.where(lane_head == head, keys, jnp.zeros_like(keys))
            scores = jnp.where(visible, dot_nt(own_keys, query) * ATTENTION_SCALE, MASKED)
            old = top[head : head + 1, :]
            new = jnp.maximum(old, jnp.max(scores, axis=0, keepdims=True))
            weights = jnp.exp(scores - new)
            fade = jnp.exp(old - new)
            top[head : head + 1, :] = new
            total[head : head + 1, :] = total[head : head + 1, :] * fade + jnp.sum(
                weights, axis=0, keepdims=True
            )
            acc[head * HD : (head + 1) * HD, :] = acc[
                head * HD : (head + 1) * HD, :
            ] * fade + dot_nn(values, weights.astype(BF16))
        return carried

    lax.fori_loop(first_ref[step], step + 1, one_block, 0)
    for head in range(heads):
        acc[head * HD : (head + 1) * HD, :] = (
            acc[head * HD : (head + 1) * HD, :] / total[head : head + 1, :]
        )
    mixed_ref[...] = jnp.transpose(acc[...]).astype(BF16)
    lse_ref[...] = top[...] + jnp.log(total[...])


def attention_forward(first, projected, cosine, sine, start):
    tokens, columns = projected.shape
    width = columns - 2 * HD
    heads = width // HD
    by_block = pl.BlockSpec((BLOCK, width), lambda i, first: (i, 0))
    by_half = pl.BlockSpec((BLOCK, width // 2), lambda i, first: (i, 0))
    whole = pl.BlockSpec((tokens, width), lambda i, first: (0, 0))
    return pl.pallas_call(
        functools.partial(forward_kernel, heads),
        grid_spec=pltpu.PrefetchScalarGridSpec(
            num_scalar_prefetch=1,
            grid=(tokens // BLOCK,),
            in_specs=[
                pl.BlockSpec((BLOCK, columns), lambda i, first: (i, 0)),
                by_half,
                by_half,
                pl.BlockSpec((1, BLOCK), lambda i, first: (0, i)),
            ],
            out_specs=[
                by_block,
                whole,
                by_block,
                by_block,
                pl.BlockSpec((heads, BLOCK), lambda i, first: (0, i)),
            ],
            scratch_shapes=[
                pltpu.VMEM((HD, tokens), BF16),
                pltpu.VMEM((heads, BLOCK), F32),
                pltpu.VMEM((heads, BLOCK), F32),
                pltpu.VMEM((width, BLOCK), F32),
            ],
        ),
        out_shape=[jax.ShapeDtypeStruct((tokens, width), BF16)] * 4
        + [jax.ShapeDtypeStruct((heads, tokens), F32)],
        compiler_params=pltpu.CompilerParams(vmem_limit_bytes=VMEM_BYTES),
        cost_estimate=pl.CostEstimate(
            flops=64 * tokens * BLOCK * width, bytes_accessed=8 * tokens * width, transcendentals=0
        ),
        name="attention_forward",
    )(first, projected, cosine, sine, start)


def backward_kernel(
    heads,
    first_ref,
    query_ref,
    key_ref,
    value_ref,
    mixed_ref,
    grad_ref,
    lse_ref,
    start_ref,
    cosine_ref,
    sine_ref,
    out_ref,
    dquery,
    dkey,
    dvalue,
):
    step = pl.program_id(0)
    query = query_ref[...]
    grad = grad_ref[...]
    start = start_ref[...]
    width = query.shape[1]
    token = step * BLOCK + lax.broadcasted_iota(jnp.int32, (BLOCK, BLOCK), 1)
    within = lax.broadcasted_iota(jnp.int32, (BLOCK, BLOCK), 0)
    half_head = half_group((BLOCK, width), heads)
    full_head = full_group((BLOCK, width))
    zero = jnp.zeros((BLOCK, width), BF16)
    product = grad.astype(F32) * mixed_ref[...].astype(F32)
    chooser = (
        lax.broadcasted_iota(jnp.int32, (8, width), 0)
        == lax.broadcasted_iota(jnp.int32, (8, width), 1) // HD
    ).astype(F32)
    correction = exact(chooser, product, ((1,), (1,)))

    @pl.when(step == 0)
    def _():
        dkey[...] = jnp.zeros_like(dkey)
        dvalue[...] = jnp.zeros_like(dvalue)

    dquery[...] = jnp.zeros_like(dquery)

    def one_block(block, carried):
        offset = pl.multiple_of(block * BLOCK, BLOCK)
        rows = pl.ds(offset, BLOCK)
        keys = key_ref[rows, :]
        values = value_ref[rows, :]
        place = offset + within
        visible = (place >= start) & (place <= token)
        new_query = dquery[...]
        new_key = dkey[rows, :]
        new_value = dvalue[rows, :]
        for head in range(heads):
            own_keys = jnp.where(half_head == head, keys, zero)
            own_values = jnp.where(full_head == head, values, zero)
            scores = dot_nt(own_keys, query) * ATTENTION_SCALE
            probs = jnp.where(visible, jnp.exp(scores - lse_ref[head : head + 1, :]), 0.0)
            pressure = dot_nt(own_values, grad)
            dscores = (probs * (pressure - correction[head : head + 1, :])).astype(BF16)
            new_value = new_value + dot_nn(
                probs.astype(BF16), jnp.where(full_head == head, grad, zero)
            )
            new_key = new_key + dot_nn(dscores, jnp.where(half_head == head, query, zero))
            new_query = new_query + dot_tn(dscores, own_keys)
        dquery[...] = new_query
        dkey[rows, :] = new_key
        dvalue[rows, :] = new_value
        return carried

    lax.fori_loop(first_ref[step], step + 1, one_block, 0)
    own_rows = pl.ds(pl.multiple_of(step * BLOCK, BLOCK), BLOCK)
    out_ref[own_rows, :width] = (
        turn(dquery[...], cosine_ref[own_rows, :], -sine_ref[own_rows, :]) * ATTENTION_SCALE
    ).astype(BF16)

    @pl.when(step == pl.num_programs(0) - 1)
    def _():
        def fold(block, carried):
            rows = pl.ds(pl.multiple_of(block * BLOCK, BLOCK), BLOCK)
            turned = turn(dkey[rows, :], cosine_ref[rows, :], -sine_ref[rows, :]) * ATTENTION_SCALE
            out_ref[rows, width:] = (
                exact(turned, spread_keys(width), ((1,), (1,)))
                + exact(dvalue[rows, :], spread_values(width), ((1,), (1,)))
            ).astype(BF16)
            return carried

        lax.fori_loop(0, pl.num_programs(0), fold, 0)


def attention_backward(first, query, keys, values, mixed, grad, lse, start, cosine, sine):
    tokens, width = query.shape
    heads = width // HD
    columns = width + 2 * HD
    by_block = pl.BlockSpec((BLOCK, width), lambda i, first: (i, 0))
    whole = pl.BlockSpec((tokens, width), lambda i, first: (0, 0))
    whole_half = pl.BlockSpec((tokens, width // 2), lambda i, first: (0, 0))
    return pl.pallas_call(
        functools.partial(backward_kernel, heads),
        grid_spec=pltpu.PrefetchScalarGridSpec(
            num_scalar_prefetch=1,
            grid=(tokens // BLOCK,),
            in_specs=[
                by_block,
                whole,
                whole,
                by_block,
                by_block,
                pl.BlockSpec((heads, BLOCK), lambda i, first: (0, i)),
                pl.BlockSpec((1, BLOCK), lambda i, first: (0, i)),
                whole_half,
                whole_half,
            ],
            out_specs=pl.BlockSpec((tokens, columns), lambda i, first: (0, 0)),
            scratch_shapes=[
                pltpu.VMEM((BLOCK, width), F32),
                pltpu.VMEM((tokens, width), F32),
                pltpu.VMEM((tokens, width), F32),
            ],
        ),
        out_shape=jax.ShapeDtypeStruct((tokens, columns), BF16),
        compiler_params=pltpu.CompilerParams(vmem_limit_bytes=VMEM_BYTES),
        cost_estimate=pl.CostEstimate(
            flops=160 * tokens * BLOCK * width,
            bytes_accessed=24 * tokens * width,
            transcendentals=0,
        ),
        name="attention_backward",
    )(first, query, keys, values, mixed, grad, lse, start, cosine, sine)


def token_starts(lengths_row, group_tokens):
    count = lengths_row.shape[0]
    order = jnp.arange(count, dtype=jnp.int32)
    finish = jnp.sum(jnp.where(order[None, :] <= order[:, None], lengths_row[None, :], 0), axis=1)
    place = jnp.arange(group_tokens, dtype=jnp.int32)
    passed = place[:, None] >= finish[None, :]
    return jnp.max(jnp.where(passed, finish[None, :], 0), axis=1), place


def inverse_norm(values):
    return lax.rsqrt(jnp.mean(values * values, axis=1, keepdims=True) + EPSILON)


def after(value, *earlier):
    return lax.optimization_barrier((value, *earlier))[0]


def sum_over_groups(value):
    return lax.psum_scatter(value, "dp", scatter_dimension=0, tiled=True)


def gather_groups(value):
    return lax.all_gather(value, "dp", axis=0, tiled=True)


def send_to(value, member_count, partner):
    return lax.ppermute(value, "fsdp", [(m, partner(m)) for m in range(member_count)])


def permuted_swap(value):
    member_count = value.shape[0]
    member = lax.axis_index("fsdp")
    return [value] + [
        send_to(
            lax.dynamic_slice_in_dim(value, member ^ away, 1, 0),
            member_count,
            lambda m, away=away: m ^ away,
        )
        for away in range(1, member_count)
    ]


def joined(pieces):
    member = lax.axis_index("fsdp")
    result = pieces[0]
    for away in range(1, len(pieces)):
        result = lax.dynamic_update_slice_in_dim(result, pieces[away], member ^ away, 0)
    return result


def swap_members(value):
    return lax.all_to_all(value, "fsdp", split_axis=0, concat_axis=0, tiled=True)


def body(
    tokens,
    cotangent,
    query_weight,
    key_weight,
    value_weight,
    output_weight,
    gate_weight,
    up_weight,
    down_weight,
    attention_gain,
    feedforward_gain,
    lengths,
):
    members = lax.axis_size("fsdp")
    groups = lax.axis_size("dp")
    rows, model = tokens.shape
    group_tokens = rows * members
    shard = query_weight.shape[0]
    heads = NH // members
    width = heads * HD
    columns = width + 2 * HD
    copies = members // KVH
    out_columns = model // members
    down_rows = down_weight.shape[0]
    chunk_rows = down_rows // CHUNKS
    units = groups * chunk_rows
    gain_one = attention_gain.astype(F32)[:, None]
    gain_two = feedforward_gain.astype(F32)[:, None]

    scaled_query = (query_weight * gain_one).astype(BF16)
    scaled_key = (key_weight * gain_one).astype(BF16)
    scaled_value = (value_weight * gain_one).astype(BF16)
    packed = jnp.concatenate(
        [
            scaled_query.reshape(shard, members, heads, 2, HALF)
            .transpose(1, 0, 3, 2, 4)
            .reshape(members, shard, width),
            jnp.repeat(
                scaled_key.reshape(shard, KVH, HD).transpose(1, 0, 2), copies, axis=0
            ),
            jnp.repeat(
                scaled_value.reshape(shard, KVH, HD).transpose(1, 0, 2), copies, axis=0
            ),
            output_weight.reshape(shard, members, out_columns).transpose(1, 0, 2),
        ],
        axis=2,
    )
    packed = swap_members(packed).reshape(members * shard, columns + out_columns)
    inputs = tokens.astype(F32)
    inverse_one = inverse_norm(inputs)
    normed_one = plane_gather(after((inputs * inverse_one).astype(BF16), packed), members, 0, True)
    packed = after(gather_groups(packed), normed_one)
    upstream = cotangent.astype(F32)
    down_chunks = []
    for chunk in range(CHUNKS):
        part = down_weight[chunk * chunk_rows : (chunk + 1) * chunk_rows]
        down_chunks.append(gather_groups(after(part, normed_one)))
    gate_up = jnp.stack(
        [
            (weight * gain_two)
            .astype(BF16)
            .reshape(shard, groups, members, CHUNKS, chunk_rows)
            .transpose(2, 0, 3, 1, 4)
            for weight in (gate_weight, up_weight)
        ],
        axis=3,
    ).reshape(members, shard, CHUNKS * 2 * units)
    gate_up = permuted_swap(after(gate_up, normed_one))

    start, place = token_starts(lengths[0], group_tokens)
    first = start[::BLOCK] // BLOCK
    frequency = ROPE_BASE ** (-(2.0 * jnp.arange(HALF, dtype=F32)) / HD)
    angles = (place - start).astype(F32)[:, None] * frequency[None, :]
    cosine = jnp.tile(jnp.cos(angles), (1, heads))
    sine = jnp.tile(jnp.sin(angles), (1, heads))
    start = start[None, :]

    projection = packed[:, :columns]
    out_piece = lax.all_to_all(
        packed[:, columns:], "fsdp", split_axis=0, concat_axis=1, tiled=True
    )
    projected = dot_nn(normed_one, projection)
    query, keys, values, mixed, lse = attention_forward(first, projected, cosine, sine, start)
    mixed_then, down_chunks[0], *gate_up = lax.optimization_barrier(
        (mixed, down_chunks[0], *gate_up)
    )
    gate_up = joined(gate_up).reshape(members * shard, CHUNKS * 2 * units)
    gate_up_chunks = [
        gather_groups(gate_up[:, chunk * 2 * units : (chunk + 1) * 2 * units])
        for chunk in range(CHUNKS)
    ]
    branch_one = product_scatter(
        [after(mixed_then, gate_up)], [out_piece], False, members, 2, True
    )
    residual = inputs + RESIDUAL_SCALE * branch_one

    inverse_two = inverse_norm(residual)
    normed_two = plane_gather((residual * inverse_two).astype(BF16), members, 3, False)
    grad_two = plane_gather(
        after((RESIDUAL_SCALE * upstream).astype(BF16), normed_two), members, 1, False
    )
    hiddens = []
    grad_boths = []
    down_grads = []
    gate_up_grads = []
    for chunk in range(CHUNKS):
        both_weight = gate_up_chunks[chunk]
        down_piece = down_chunks[chunk]
        both = dot_nn(normed_two, both_weight)
        gate = both[:, :units]
        up = both[:, units:]
        sigmoid = jax.nn.sigmoid(gate)
        hidden = (gate * sigmoid * up).astype(BF16)
        grad_hidden = dot_nt(grad_two, down_piece)
        grad_both = jnp.concatenate(
            [
                (grad_hidden * up * sigmoid * (1.0 + gate * (1.0 - sigmoid))).astype(BF16),
                (grad_hidden * gate * sigmoid).astype(BF16),
            ],
            axis=1,
        )
        gate_up_grad = dot_tn(normed_two, grad_both).astype(BF16)
        down_grad = dot_tn(hidden, grad_two).astype(BF16)
        gate_up_grads.append(sum_over_groups(gate_up_grad))
        down_grads.append(sum_over_groups(down_grad))
        normed_two, grad_two, hidden, grad_both, _ = lax.optimization_barrier(
            (normed_two, grad_two, hidden, grad_both, gate_up_grad)
        )
        hiddens.append(hidden)
        grad_boths.append(grad_both)
    weighted_two = product_scatter(grad_boths, gate_up_chunks, True, members, 4, False)
    grad_residual = (
        upstream
        + inverse_two * weighted_two
        - residual * inverse_two**3 * jnp.mean(weighted_two * residual, axis=1, keepdims=True)
    )
    gain_term_two = jnp.sum(weighted_two * residual * inverse_two, axis=0)

    grad_one, gate_up_grads[0] = lax.optimization_barrier(
        ((RESIDUAL_SCALE * grad_residual).astype(BF16), gate_up_grads[0])
    )
    grad_one = plane_gather(grad_one, members, 5, True)
    grad_mixed = dot_nt(grad_one, out_piece).astype(BF16)
    out_grad = dot_tn(mixed, grad_one).astype(BF16)
    out_grad = lax.all_to_all(out_grad, "fsdp", split_axis=1, concat_axis=0, tiled=True)
    grad_mixed, gate_up_grads[-1] = lax.optimization_barrier((grad_mixed, gate_up_grads[-1]))
    grad_projected = attention_backward(
        first, query, keys, values, mixed, grad_mixed, lse, start, cosine, sine
    )
    packed_grad = jnp.concatenate(
        [dot_tn(normed_one, grad_projected).astype(BF16), out_grad], axis=1
    )
    grad_projected, packed_grad, down_grads[0] = lax.optimization_barrier(
        (grad_projected, packed_grad, down_grads[0])
    )
    packed_grad = sum_over_groups(packed_grad)
    weighted_one = product_scatter([grad_projected], [projection], True, members, 6, True)
    grad_inputs = (
        grad_residual
        + inverse_one * weighted_one
        - inputs * inverse_one**3 * jnp.mean(weighted_one * inputs, axis=1, keepdims=True)
    )
    gain_term_one = jnp.sum(weighted_one * inputs * inverse_one, axis=0)

    hiddens[-1] = after(hiddens[-1], weighted_one)
    branch_two = product_scatter(hiddens, down_chunks, False, members, 7, False)
    branch_two, down_grads[-1] = lax.optimization_barrier((branch_two, down_grads[-1]))
    output = residual + RESIDUAL_SCALE * branch_two

    gains = jnp.stack(
        [
            gain_term_one.reshape(groups, members, shard),
            gain_term_two.reshape(groups, members, shard),
        ],
        axis=2,
    ).reshape(groups, members, 2 * shard)
    gains = jnp.pad(
        gains.transpose(1, 0, 2), ((0, 0), (0, (-groups) % 8), (0, (-2 * shard) % 128))
    )
    gains = total_over_all(after(gains, branch_two), groups, 8)
    gains = lax.dynamic_slice_in_dim(gains, lax.axis_index("dp"), 1, 0)[0, : 2 * shard]
    gains = gains.reshape(2, shard)

    gate_up_grads = [
        swap_members(after(part.reshape(members, shard, 2 * units), branch_two))
        .reshape(members, shard, 2, groups, chunk_rows)
        for part in gate_up_grads
    ]
    both_grad = [
        jnp.stack([part[:, :, side] for part in gate_up_grads], axis=3)
        .transpose(1, 2, 0, 3, 4)
        .reshape(shard, -1)
        .astype(F32)
        * gain_two
        for side in range(2)
    ]
    packed_grad = swap_members(packed_grad.reshape(members, shard, -1)).astype(F32)
    grad_query = (
        packed_grad[:, :, :width]
        .reshape(members, shard, 2, heads, HALF)
        .transpose(1, 0, 3, 2, 4)
        .reshape(shard, -1)
    )

    def folded(part):
        return (
            part.reshape(KVH, copies, shard, HD).sum(axis=1).transpose(1, 0, 2).reshape(shard, -1)
        )

    return (
        output.astype(BF16),
        grad_inputs.astype(BF16),
        grad_query * gain_one,
        folded(packed_grad[:, :, width : width + HD]) * gain_one,
        folded(packed_grad[:, :, width + HD : columns]) * gain_one,
        packed_grad[:, :, columns:].transpose(1, 0, 2).reshape(shard, -1),
        both_grad[0],
        both_grad[1],
        jnp.concatenate(down_grads, axis=0).astype(F32),
        gains[0] / gain_one[:, 0],
        gains[1] / gain_two[:, 0],
    )


def solution(mesh):
    by_rows = P(("dp", "fsdp"), None)
    by_entries = P(("dp", "fsdp"))
    return jax.shard_map(
        body,
        mesh=mesh,
        in_specs=(by_rows,) * 9 + (by_entries,) * 2 + (P("dp", None),),
        out_specs=(by_rows,) * 9 + (by_entries,) * 2,
        check_vma=False,
    )
```

```python
import functools

import jax
import jax.numpy as jnp
from jax import lax
from jax.experimental import pallas as pl
from jax.experimental.pallas import tpu as pltpu
from jax.sharding import PartitionSpec as P

NH = 32
KVH = 8
HD = 64
HALF = HD // 2

EPSILON = 1e-05
RESIDUAL_SCALE = 0.22
ATTENTION_SCALE = 0.015625
ROPE_BASE = 10000000.0
MASKED = -1e30
BLOCK = 256
CHUNKS = 2
PIECES = 4
VMEM_BYTES = 58 * 1024 * 1024
MESH = pl.DeviceIdType.MESH
BF16 = jnp.bfloat16
F32 = jnp.float32


def dot_nn(left, right):
    return jnp.dot(left, right, preferred_element_type=F32)


def dot_nt(left, right):
    return lax.dot_general(left, right, (((1,), (1,)), ((), ())), preferred_element_type=F32)


def dot_tn(left, right):
    return lax.dot_general(left, right, (((0,), (0,)), ((), ())), preferred_element_type=F32)


def flip(index, mask):
    return index + mask * (1 - 2 * ((index // mask) % 2))


def plane_masks(member_count):
    masks = []
    mask = 2
    while mask < member_count:
        masks.append(mask)
        mask *= 2
    return masks


def hop(index, step, masks):
    core = index % 2
    return (1 - core) * flip(index, masks[step]) + core * flip(index, masks[-1 - step])


def walk(index, subset, masks):
    for step in range(len(masks)):
        if (subset >> step) & 1:
            index = hop(index, step, masks)
    return index


def greet(group, member, masks):
    barrier = pltpu.get_barrier_semaphore()
    partners = [hop(member, step, masks) for step in range(len(masks))] + [flip(member, 1)]
    for partner in partners:
        pl.semaphore_signal(barrier, inc=1, device_id=(group, partner), device_id_type=MESH)
    pl.semaphore_wait(barrier, len(partners))


def gather_kernel(member_count, in_order, count, own_ref, *refs):
    operands = refs[: count + 2] if count else ()
    refs = refs[len(operands) :]
    all_ref, results, refs = refs[0], refs[1 : 4 if count else 1], refs[4 if count else 1 :]
    link_send, link_recv, core_send, core_recv, local_sem = refs[:5]
    group = lax.axis_index("dp")
    member = lax.axis_index("fsdp")
    masks = plane_masks(member_count)
    steps = len(masks)
    rows = own_ref.shape[0]
    piece = rows // PIECES
    greet(group, member, masks)

    blocks = 1 << steps

    def place(owner, subset, side, part):
        block = walk(owner, subset, masks) if in_order else subset + side * blocks
        return all_ref.at[pl.ds(pl.multiple_of(block * rows + part * piece, piece), piece)]

    def link_copy(step, subset, part):
        number = (1 << step) - 1 + subset
        here = place(member, subset, 0, part)
        there = here if in_order else place(member, subset | (1 << step), 0, part)
        return pltpu.make_async_remote_copy(
            own_ref.at[pl.ds(part * piece, piece)] if subset == 0 else here,
            there,
            link_send.at[number, part],
            link_recv.at[number, part],
            device_id=(group, hop(member, step, masks)),
            device_id_type=MESH,
        )

    def core_copy(subset, part):
        here = place(member, subset, 0, part)
        there = here if in_order else place(member, subset, 1, part)
        return pltpu.make_async_remote_copy(
            own_ref.at[pl.ds(part * piece, piece)] if subset == 0 else here,
            there,
            core_send.at[subset, part],
            core_recv.at[subset, part],
            device_id=(group, flip(member, 1)),
            device_id_type=MESH,
        )

    for part in range(PIECES):
        for step in range(steps):
            link_copy(step, 0, part).start()
    first = pl.multiple_of(member * rows, rows) if in_order else 0
    keep = pltpu.make_async_copy(own_ref, all_ref.at[pl.ds(first, rows)], local_sem)
    keep.start()
    for part in range(PIECES):
        core_copy(0, part).start()
    tiles = []
    if count:
        helds = refs[5 : 7 + count]
        down_grad, out_sibling, out_own = refs[7 + count : 10 + count]
        load_sem, store_sem = refs[10 + count :]
        hiddens, gradient, down = helds[:count], helds[count], helds[count + 1]
        units = hiddens[0].shape[1]
        loads = [
            pltpu.make_async_copy(source, target, load_sem.at[number])
            for number, (source, target) in enumerate(zip(operands, helds))
        ]
        stores = [
            pltpu.make_async_copy(source, target, store_sem.at[number])
            for number, (source, target) in enumerate(
                zip((down_grad, out_sibling, out_own), results)
            )
        ]
        for load in loads:
            load.start()
        half = out_own.shape[0]
        height = min(256, half)
        width = down.shape[1] // 4

        def out_tile(target, base, row):
            def one_part(index, carried):
                columns = pl.ds(pl.multiple_of(index * width, width), width)
                total = None
                for number in range(count):
                    term = dot_nn(
                        hiddens[number][base + row : base + row + height, :],
                        down[number * units : (number + 1) * units, columns],
                    )
                    total = term if total is None else total + term
                target[row : row + height, columns] = total.astype(BF16)
                return carried

            lax.fori_loop(0, 4, one_part, 0)

        tile = min(256, units)

        def grad_tile(number, column):
            def one_part(index, carried):
                columns = pl.ds(pl.multiple_of(index * width, width), width)
                first = number * units + column
                down_grad[first : first + tile, columns] = dot_tn(
                    hiddens[number][:, column : column + tile], gradient[:, columns]
                ).astype(BF16)
                return carried

            lax.fori_loop(0, 4, one_part, 0)

        for load in loads[:count] + loads[count + 1 :]:
            tiles.append(load.wait)
        for target, base, store in (
            (out_sibling, half, stores[1]),
            (out_own, 0, stores[2]),
        ):
            for row in range(0, half, height):
                tiles.append(functools.partial(out_tile, target, base, row))
            tiles.append(store.start)
        tiles.append(loads[count].wait)
        for number in range(count):
            for column in range(0, units, tile):
                tiles.append(functools.partial(grad_tile, number, column))
        tiles.append(stores[0].start)
    share = -(-len(tiles) // (steps * PIECES))

    turn = 0
    for step in range(steps):
        for part in range(PIECES):
            for subset in range(1 << step):
                link_copy(step, subset, part).wait_recv()
                arrived = subset | (1 << step)
                for later in range(step + 1, steps):
                    link_copy(later, arrived, part).start()
                core_copy(arrived, part).start()
            for run in tiles[turn * share : (turn + 1) * share]:
                run()
            turn += 1
    for part in range(PIECES):
        for subset in range(1 << steps):
            core_copy(subset, part).wait()
    for part in range(PIECES):
        for step in range(steps):
            for subset in range(1 << step):
                link_copy(step, subset, part).wait_send()
    keep.wait()
    if count:
        for store in stores:
            store.wait()


def plane_gather(own, member_count, collective_id, in_order, extras=None):
    rows, width = own.shape
    steps = len(plane_masks(member_count))
    blocks = 1 << steps
    total = member_count * rows
    any_space = pl.BlockSpec(memory_space=pl.ANY)
    scratch = [
        pltpu.SemaphoreType.DMA((blocks - 1, PIECES)),
        pltpu.SemaphoreType.DMA((blocks - 1, PIECES)),
        pltpu.SemaphoreType.DMA((blocks, PIECES)),
        pltpu.SemaphoreType.DMA((blocks, PIECES)),
        pltpu.SemaphoreType.DMA,
    ]
    operands = [own]
    out_shape = [jax.ShapeDtypeStruct((total, width), own.dtype)]
    count = 0
    if extras:
        hiddens, gradient, down = extras
        count = len(hiddens)
        operands += [*hiddens, gradient, down]
        scratch += [pltpu.VMEM(value.shape, BF16) for value in operands[1:]]
        out_shape += [
            jax.ShapeDtypeStruct((down.shape[0], gradient.shape[1]), BF16),
            jax.ShapeDtypeStruct((total // 2, down.shape[1]), BF16),
            jax.ShapeDtypeStruct((total // 2, down.shape[1]), BF16),
        ]
        scratch += [pltpu.VMEM(value.shape, BF16) for value in out_shape[1:]]
        scratch += [pltpu.SemaphoreType.DMA((count + 2,)), pltpu.SemaphoreType.DMA((3,))]
    result = pl.pallas_call(
        functools.partial(gather_kernel, member_count, in_order, count),
        out_shape=out_shape,
        in_specs=[any_space] * len(operands),
        out_specs=[any_space] * len(out_shape),
        scratch_shapes=scratch,
        compiler_params=pltpu.CompilerParams(
            collective_id=collective_id, has_side_effects=True, vmem_limit_bytes=VMEM_BYTES
        ),
        cost_estimate=pl.CostEstimate(
            flops=0, bytes_accessed=60 * total * width, transcendentals=0
        ),
        name="plane_gather",
    )(*operands)
    return result if extras else result[0]


def swap_kernel(member_count, count, *refs):
    sources, targets = refs[:count], refs[count : 2 * count]
    send_sem, recv_sem, local_sem = refs[2 * count :]
    group = lax.axis_index("dp")
    member = lax.axis_index("fsdp")
    barrier = pltpu.get_barrier_semaphore()
    for away in range(1, member_count):
        pl.semaphore_signal(
            barrier,
            inc=1,
            device_id=(group, (member + away) % member_count),
            device_id_type=MESH,
        )
    pl.semaphore_wait(barrier, member_count - 1)

    def copy(number, away):
        target = (member + away) % member_count
        return pltpu.make_async_remote_copy(
            sources[number].at[target],
            targets[number].at[member],
            send_sem.at[number, away],
            recv_sem.at[number, away],
            device_id=(group, target),
            device_id_type=MESH,
        )

    def keep(number):
        return pltpu.make_async_copy(
            sources[number].at[member], targets[number].at[member], local_sem.at[number]
        )

    for number in range(count):
        for away in range(1, member_count):
            copy(number, away).start()
        keep(number).start()
    for number in range(count):
        for away in range(1, member_count):
            copy(number, away).wait()
        keep(number).wait()


def plane_swap(values, member_count, collective_id):
    count = len(values)
    any_space = pl.BlockSpec(memory_space=pl.ANY)
    return pl.pallas_call(
        functools.partial(swap_kernel, member_count, count),
        out_shape=[jax.ShapeDtypeStruct(value.shape, value.dtype) for value in values],
        in_specs=[any_space] * count,
        out_specs=[any_space] * count,
        scratch_shapes=[
            pltpu.SemaphoreType.DMA((count, member_count)),
            pltpu.SemaphoreType.DMA((count, member_count)),
            pltpu.SemaphoreType.DMA((count,)),
        ],
        compiler_params=pltpu.CompilerParams(collective_id=collective_id, has_side_effects=True),
        cost_estimate=pl.CostEstimate(
            flops=0,
            bytes_accessed=60 * sum(value.size for value in values),
            transcendentals=0,
        ),
        name="plane_swap",
    )(*values)


def product_scatter_kernel(member_count, in_order, transposed, count, rows, *refs):
    lefts, rights, sum_ref = refs[:count], refs[count : 2 * count], refs[2 * count]
    held_lefts, held_rights = refs[2 * count + 1 : 3 * count + 1], refs[3 * count + 1 : 4 * count + 1]
    (
        outgoing,
        core_buffer,
        held,
        link_buffer,
        left_sem,
        right_sem,
        link_send,
        link_recv,
        core_send,
        core_recv,
    ) = refs[4 * count + 1 :]
    group = lax.axis_index("dp")
    member = lax.axis_index("fsdp")
    sibling = flip(member, 1)
    masks = plane_masks(member_count)
    steps = len(masks)
    blocks = 1 << steps
    piece = sum_ref.shape[1] // PIECES

    def left_copy(number, side, subset):
        owner = sibling if side else member
        block = walk(owner, subset, masks) if in_order else subset + side * blocks
        return pltpu.make_async_copy(
            lefts[number].at[pl.ds(pl.multiple_of(block * rows, rows), rows)],
            held_lefts[number].at[pl.ds((side * blocks + subset) * rows, rows)],
            left_sem.at[number, side, subset],
        )

    def right_copy(number):
        return pltpu.make_async_copy(rights[number], held_rights[number], right_sem.at[number])

    for number in range(count):
        right_copy(number).start()
        for side in (1, 0):
            for subset in range(blocks):
                left_copy(number, side, subset).start()
    greet(group, member, masks)

    def part(side, subset, where):
        where_rows = pl.ds((side * blocks + subset) * rows, rows)
        total = None
        for number in range(count):
            left = held_lefts[number][where_rows, :]
            if transposed:
                term = dot_nt(left, held_rights[number][where, :])
            else:
                term = dot_nn(left, held_rights[number][:, where])
            total = term if total is None else total + term
        return total

    def columns(index):
        return pl.ds(pl.multiple_of(index * piece, piece), piece)

    def core_copy(index):
        return pltpu.make_async_remote_copy(
            outgoing.at[:, columns(index)],
            core_buffer.at[:, columns(index)],
            core_send.at[index],
            core_recv.at[index],
            device_id=(group, sibling),
            device_id_type=MESH,
        )

    def slot(step, kept):
        return sum(blocks >> (s + 1) for s in range(step)) + (kept >> (step + 1))

    def link_copy(step, subset, index):
        number = slot(step, subset & ~(1 << step))
        return pltpu.make_async_remote_copy(
            held.at[pl.ds(subset * rows, rows), columns(index)],
            link_buffer.at[pl.ds(number * rows, rows), columns(index)],
            link_send.at[number, index],
            link_recv.at[number, index],
            device_id=(group, hop(member, step, masks)),
            device_id_type=MESH,
        )

    order = sorted(range(blocks), key=lambda s: (-(s & 1), -s))

    for number in range(count):
        right_copy(number).wait()
        for side in (1, 0):
            for subset in range(blocks):
                left_copy(number, side, subset).wait()

    def for_sibling(index, carried):
        where = columns(index)
        for subset in range(blocks):
            outgoing[pl.ds(subset * rows, rows), where] = part(1, subset, where).astype(BF16)
        core_copy(index).start()
        return carried

    lax.fori_loop(0, PIECES, for_sibling, 0)

    def for_links(index, carried):
        where = columns(index)
        core_copy(index).wait_recv()
        for subset in order:
            where_rows = pl.ds(subset * rows, rows)
            total = part(0, subset, where) + core_buffer[where_rows, where].astype(F32)
            if subset == 0:
                sum_ref[:, where] = total
            else:
                held[where_rows, where] = total.astype(BF16)
            if subset & 1:
                link_copy(0, subset, index).start()
        return carried

    lax.fori_loop(0, PIECES, for_links, 0)

    for step in range(steps):

        def one_step(index, carried, step=step):
            where = columns(index)
            for kept in sorted(range(0, blocks, 2 << step), reverse=True):
                link_copy(step, kept | (1 << step), index).wait_recv()
                arrived = link_buffer[pl.ds(slot(step, kept) * rows, rows), where].astype(F32)
                if kept == 0:
                    sum_ref[:, where] += arrived
                else:
                    where_rows = pl.ds(kept * rows, rows)
                    held[where_rows, where] = (
                        held[where_rows, where].astype(F32) + arrived
                    ).astype(BF16)
                if (kept >> (step + 1)) & 1:
                    link_copy(step + 1, kept, index).start()
            return carried

        lax.fori_loop(0, PIECES, one_step, 0)

    def finish(index, carried):
        core_copy(index).wait_send()
        for step in range(steps):
            for kept in range(0, blocks, 2 << step):
                link_copy(step, kept | (1 << step), index).wait_send()
        return carried

    lax.fori_loop(0, PIECES, finish, 0)


def product_scatter(lefts, rights, transposed, member_count, collective_id, in_order):
    count = len(lefts)
    total = lefts[0].shape[0]
    width = rights[0].shape[0 if transposed else 1]
    rows = total // member_count
    blocks = 1 << len(plane_masks(member_count))
    depth = sum(left.shape[1] for left in lefts)
    scratch = (
        [pltpu.VMEM(left.shape, BF16) for left in lefts]
        + [pltpu.VMEM(right.shape, BF16) for right in rights]
        + [
            pltpu.VMEM((blocks * rows, width), BF16),
            pltpu.VMEM((blocks * rows, width), BF16),
            pltpu.VMEM((blocks * rows, width), BF16),
            pltpu.VMEM(((blocks - 1) * rows, width), BF16),
            pltpu.SemaphoreType.DMA((count, 2, blocks)),
            pltpu.SemaphoreType.DMA((count,)),
            pltpu.SemaphoreType.DMA((blocks - 1, PIECES)),
            pltpu.SemaphoreType.DMA((blocks - 1, PIECES)),
            pltpu.SemaphoreType.DMA((PIECES,)),
            pltpu.SemaphoreType.DMA((PIECES,)),
        ]
    )
    any_space = pl.BlockSpec(memory_space=pl.ANY)
    in_vmem = pl.BlockSpec(memory_space=pltpu.VMEM)
    return pl.pallas_call(
        functools.partial(product_scatter_kernel, member_count, in_order, transposed, count, rows),
        out_shape=jax.ShapeDtypeStruct((rows, width), F32),
        in_specs=[any_space] * (2 * count),
        out_specs=in_vmem,
        scratch_shapes=scratch,
        compiler_params=pltpu.CompilerParams(
            collective_id=collective_id, has_side_effects=True, vmem_limit_bytes=VMEM_BYTES
        ),
        cost_estimate=pl.CostEstimate(
            flops=2 * total * depth * width, bytes_accessed=60 * total * width, transcendentals=0
        ),
        name="product_scatter",
    )(*lefts, *rights)


def total_steps(
    member_count, group_count, part_ref, sum_ref, near, held, far, near_send, near_recv, far_send, far_recv
):
    group = lax.axis_index("dp")
    member = lax.axis_index("fsdp")
    barrier = pltpu.get_barrier_semaphore()
    for away in range(1, member_count):
        pl.semaphore_signal(
            barrier,
            inc=1,
            device_id=(group, (member + away) % member_count),
            device_id_type=MESH,
        )
    for away in range(1, group_count):
        pl.semaphore_signal(
            barrier, inc=1, device_id=((group + away) % group_count, member), device_id_type=MESH
        )
    pl.semaphore_wait(barrier, member_count + group_count - 2)

    def near_copy(away):
        target = (member + away) % member_count
        return pltpu.make_async_remote_copy(
            part_ref.at[target],
            near.at[away],
            near_send.at[away],
            near_recv.at[away],
            device_id=(group, target),
            device_id_type=MESH,
        )

    def far_copy(away):
        return pltpu.make_async_remote_copy(
            held,
            far.at[away],
            far_send.at[away],
            far_recv.at[away],
            device_id=((group + away) % group_count, member),
            device_id_type=MESH,
        )

    def near_step():
        for away in range(1, member_count):
            near_copy(away).start()

    def far_step():
        total = part_ref[member]
        for away in range(1, member_count):
            near_copy(away).wait_recv()
            total = total + near[away]
        held[...] = total
        for away in range(1, group_count):
            far_copy(away).start()

    def end_step():
        total = held[...]
        for away in range(1, group_count):
            far_copy(away).wait_recv()
            total = total + far[away]
        sum_ref[...] = total
        for away in range(1, member_count):
            near_copy(away).wait_send()
        for away in range(1, group_count):
            far_copy(away).wait_send()

    near_step()
    far_step()
    end_step()


def total_over_all(parts, group_count, collective_id):
    member_count, rows, lanes = parts.shape
    return pl.pallas_call(
        functools.partial(total_steps, member_count, group_count),
        out_shape=jax.ShapeDtypeStruct((rows, lanes), F32),
        in_specs=[pl.BlockSpec(memory_space=pltpu.VMEM)],
        out_specs=pl.BlockSpec(memory_space=pltpu.VMEM),
        scratch_shapes=[
            pltpu.VMEM((member_count, rows, lanes), F32),
            pltpu.VMEM((rows, lanes), F32),
            pltpu.VMEM((group_count, rows, lanes), F32),
            pltpu.SemaphoreType.DMA((member_count,)),
            pltpu.SemaphoreType.DMA((member_count,)),
            pltpu.SemaphoreType.DMA((group_count,)),
            pltpu.SemaphoreType.DMA((group_count,)),
        ],
        compiler_params=pltpu.CompilerParams(collective_id=collective_id, has_side_effects=True),
        cost_estimate=pl.CostEstimate(flops=0, bytes_accessed=40000000, transcendentals=0),
        name="total_over_all",
    )(parts)


def local_call(kernel, name, out_shape, *operands):
    in_vmem = pl.BlockSpec(memory_space=pltpu.VMEM)
    size = sum(value.size * value.dtype.itemsize for value in operands[1:])
    size += sum(value.size * value.dtype.itemsize for value in out_shape)
    return pl.pallas_call(
        kernel,
        grid_spec=pltpu.PrefetchScalarGridSpec(
            num_scalar_prefetch=1,
            in_specs=[in_vmem] * (len(operands) - 1),
            out_specs=[in_vmem] * len(out_shape),
            grid=(),
        ),
        out_shape=out_shape,
        compiler_params=pltpu.CompilerParams(vmem_limit_bytes=VMEM_BYTES),
        cost_estimate=pl.CostEstimate(flops=0, bytes_accessed=size, transcendentals=0),
        name=name,
    )(*operands)


def rows_apart(member, value, member_count):
    rows = value.shape[0] // member_count

    def kernel(member_ref, value_ref, *out_refs):
        for away, out_ref in enumerate(out_refs):
            other = member_ref[0] ^ away
            out_ref[...] = value_ref[pl.ds(pl.multiple_of(other * rows, rows), rows), :]

    shape = jax.ShapeDtypeStruct((rows, value.shape[1]), value.dtype)
    return local_call(kernel, "rows_apart", [shape] * member_count, member, value)


def rows_together(member, blocks, chunks):
    rows, width = blocks[0].shape
    part = width // chunks
    count = len(blocks)

    def kernel(member_ref, *refs):
        for away in range(count):
            where = pl.ds(pl.multiple_of((member_ref[0] ^ away) * rows, rows), rows)
            for chunk in range(chunks):
                refs[count + chunk][where, :] = refs[away][:, chunk * part : (chunk + 1) * part]

    shape = jax.ShapeDtypeStruct((count * rows, part), blocks[0].dtype)
    return local_call(kernel, "rows_together", [shape] * chunks, member, *blocks)


def columns_together(member, blocks):
    rows, width = blocks[0].shape
    count = len(blocks)

    def kernel(member_ref, *refs):
        for away in range(count):
            where = pl.ds(pl.multiple_of((member_ref[0] ^ away) * width, width), width)
            refs[count][:, where] = refs[away][...]

    shape = jax.ShapeDtypeStruct((rows, count * width), blocks[0].dtype)
    return local_call(kernel, "columns_together", [shape], member, *blocks)[0]


def exchanged(blocks):
    return [blocks[0]] + [
        lax.ppermute(blocks[away], "fsdp", [(m, m ^ away) for m in range(len(blocks))])
        for away in range(1, len(blocks))
    ]


def added(left, right):
    return left.astype(F32) + right.astype(F32)


def send_to(value, member_count, partner):
    return lax.ppermute(value, "fsdp", [(m, partner(m)) for m in range(member_count)])


def hopped(step, member_count):
    masks = plane_masks(member_count)
    return lambda m: (m ^ masks[step]) if m % 2 == 0 else (m ^ masks[-1 - step])


def unit_strips(member_count, group_count, chunks, per):
    share = group_count // chunks
    for chunk in range(chunks):
        for side in range(2):
            for place in range(share):
                group = chunk * share + place
                yield chunk, side, (side * share + place) * per, group * member_count * per


def units_apart(member, gate, up, gain, member_count, group_count, chunks):
    shard, width = gate.shape
    per = width // (member_count * group_count)
    columns = 2 * group_count * per
    strips = list(unit_strips(member_count, group_count, chunks, per))
    shape = jax.ShapeDtypeStruct((shard, columns), BF16)
    if per % 128:
        scaled = [(value * gain).astype(BF16) for value in (gate, up)]

        def block(away):
            other = member[0] ^ away
            return jnp.concatenate(
                [
                    lax.dynamic_slice_in_dim(scaled[side], base + other * per, per, 1)
                    for chunk, side, column, base in strips
                ],
                axis=1,
            )

        return [block(away) for away in range(member_count)]

    def kernel(member_ref, gate_ref, up_ref, gain_ref, *out_refs):
        for away, out_ref in enumerate(out_refs):
            other = member_ref[0] ^ away
            for chunk, side, column, base in strips:
                where = pl.ds(pl.multiple_of(base + other * per, per), per)
                source = (gate_ref, up_ref)[side][:, where].astype(F32)
                column += chunk * (columns // chunks)
                out_ref[:, column : column + per] = (source * gain_ref[...]).astype(BF16)

    return local_call(kernel, "units_apart", [shape] * member_count, member, gate, up, gain)


def units_together(member, chunk_blocks, gain, member_count, group_count):
    chunks = len(chunk_blocks)
    shard, columns = chunk_blocks[0][0].shape
    per = columns * chunks // (2 * group_count)
    width = per * member_count * group_count
    strips = list(unit_strips(member_count, group_count, chunks, per))
    blocks = [block for group in chunk_blocks for block in group]
    if per % 128:
        results = []
        for side in range(2):
            result = jnp.zeros((shard, width), F32)
            for away in range(member_count):
                other = member[0] ^ away
                for chunk, this, column, base in strips:
                    if this == side:
                        piece = chunk_blocks[chunk][away][:, column : column + per]
                        result = lax.dynamic_update_slice_in_dim(
                            result, piece.astype(F32) * gain, base + other * per, 1
                        )
            results.append(result)
        return results

    def kernel(member_ref, gain_ref, *refs):
        outs = refs[len(blocks) :]
        for away in range(member_count):
            other = member_ref[0] ^ away
            for chunk, side, column, base in strips:
                where = pl.ds(pl.multiple_of(base + other * per, per), per)
                piece = refs[chunk * member_count + away][:, column : column + per]
                outs[side][:, where] = piece.astype(F32) * gain_ref[...]

    shape = jax.ShapeDtypeStruct((shard, width), F32)
    return local_call(kernel, "units_together", [shape] * 2, member, gain, *blocks)


def heads_together(member, blocks, gain, heads):
    count = len(blocks)
    shard, columns = blocks[0].shape
    width = heads * HD
    out_width = columns - width - 2 * HD
    copies = count // KVH

    def kernel(member_ref, gain_ref, *refs):
        ins, (query_out, key_out, value_out, out_out) = refs[:count], refs[count:]
        row = lax.broadcasted_iota(jnp.int32, (width, width), 0)
        column = lax.broadcasted_iota(jnp.int32, (width, width), 1)
        source = column % HD // HALF * (HALF * heads) + column // HD * HALF + column % HALF
        order = (row == source).astype(BF16)
        pair_row = lax.broadcasted_iota(jnp.int32, (2 * HD, KVH * HD), 0)
        pair_column = lax.broadcasted_iota(jnp.int32, (2 * HD, KVH * HD), 1)
        gain_here = gain_ref[...]
        keys = jnp.zeros((shard, KVH * HD), F32)
        values = jnp.zeros((shard, KVH * HD), F32)
        for away in range(count):
            other = member_ref[0] ^ away
            block = ins[away]
            where = pl.ds(pl.multiple_of(other * width, width), width)
            query_out[:, where] = dot_nn(block[:, :width], order) * gain_here
            pair = block[:, width : width + 2 * HD]
            first = other // copies * HD
            keys = keys + dot_nn(pair, (pair_column == pair_row + first).astype(BF16) * (pair_row < HD).astype(BF16))
            values = values + dot_nn(
                pair, (pair_column == pair_row - HD + first).astype(BF16) * (pair_row >= HD).astype(BF16)
            )
            out_where = pl.ds(pl.multiple_of(other * out_width, out_width), out_width)
            out_out[:, out_where] = block[:, width + 2 * HD :].astype(F32)
        key_out[...] = keys * gain_here
        value_out[...] = values * gain_here

    shapes = [
        jax.ShapeDtypeStruct((shard, size), F32)
        for size in (count * width, KVH * HD, KVH * HD, count * out_width)
    ]
    return local_call(kernel, "heads_together", shapes, member, gain, *blocks)


def half_group(shape, heads):
    return (lax.broadcasted_iota(jnp.int32, shape, 1) // HALF) % heads


def full_group(shape):
    return lax.broadcasted_iota(jnp.int32, shape, 1) // HD


def spread_keys(width):
    heads = width // HD
    row = lax.broadcasted_iota(jnp.int32, (2 * HD, width), 0)
    column = lax.broadcasted_iota(jnp.int32, (2 * HD, width), 1)
    source = column // (HALF * heads) * HALF + column % HALF
    return (row == source).astype(F32)


def spread_values(width):
    row = lax.broadcasted_iota(jnp.int32, (2 * HD, width), 0)
    column = lax.broadcasted_iota(jnp.int32, (2 * HD, width), 1)
    return (row == HD + column % HD).astype(F32)


def exact(left, right, dims):
    return lax.dot_general(
        left,
        right,
        (dims, ((), ())),
        precision=lax.Precision.HIGHEST,
        preferred_element_type=F32,
    )


def tables(table, width):
    half = width // 2
    row = lax.broadcasted_iota(jnp.int32, (2 * HALF, half), 0)
    column = lax.broadcasted_iota(jnp.int32, (2 * HALF, half), 1) % HALF
    return (
        exact(table, (row == column).astype(F32), ((1,), (0,))),
        exact(table, (row == column + HALF).astype(F32), ((1,), (0,))),
    )


def turn(values, cosine, sine):
    half = cosine.shape[1]
    first = values[:, :half]
    second = values[:, half:]
    return jnp.concatenate([first * cosine - second * sine, second * cosine + first * sine], axis=1)


def forward_kernel(
    heads,
    first_ref,
    projected_ref,
    table_ref,
    start_ref,
    query_ref,
    key_ref,
    value_ref,
    mixed_ref,
    lse_ref,
    value_columns,
    top,
    total,
    acc,
):
    step = pl.program_id(0)
    width = heads * HD
    start = start_ref[...]
    cosine, sine = tables(table_ref[...], width)
    query = turn(projected_ref[:, :width], cosine, sine).astype(BF16)
    pair = projected_ref[:, width:]
    keys_here = turn(exact(pair, spread_keys(width), ((1,), (0,))), cosine, sine).astype(BF16)
    own_rows = pl.ds(pl.multiple_of(step * BLOCK, BLOCK), BLOCK)
    query_ref[...] = query
    key_ref[own_rows, :] = keys_here
    value_ref[...] = exact(pair, spread_values(width), ((1,), (0,))).astype(BF16)
    value_columns[:, own_rows] = jnp.transpose(pair)[HD:, :].astype(BF16)
    token = step * BLOCK + lax.broadcasted_iota(jnp.int32, (BLOCK, BLOCK), 1)
    within = lax.broadcasted_iota(jnp.int32, (BLOCK, BLOCK), 0)
    lane_head = half_group((BLOCK, width), heads)
    top[...] = jnp.full_like(top, MASKED)
    total[...] = jnp.zeros_like(total)
    acc[...] = jnp.zeros_like(acc)

    def one_block(block, carried):
        offset = pl.multiple_of(block * BLOCK, BLOCK)
        keys = key_ref[pl.ds(offset, BLOCK), :]
        values = value_columns[:, pl.ds(offset, BLOCK)]
        place = offset + within
        visible = (place >= start) & (place <= token)
        for head in range(heads):
            own_keys = jnp.where(lane_head == head, keys, jnp.zeros_like(keys))
            scores = jnp.where(visible, dot_nt(own_keys, query) * ATTENTION_SCALE, MASKED)
            old = top[head : head + 1, :]
            new = jnp.maximum(old, jnp.max(scores, axis=0, keepdims=True))
            weights = jnp.exp(scores - new)
            fade = jnp.exp(old - new)
            top[head : head + 1, :] = new
            total[head : head + 1, :] = total[head : head + 1, :] * fade + jnp.sum(
                weights, axis=0, keepdims=True
            )
            acc[head * HD : (head + 1) * HD, :] = acc[
                head * HD : (head + 1) * HD, :
            ] * fade + dot_nn(values, weights.astype(BF16))
        return carried

    lax.fori_loop(first_ref[step], step + 1, one_block, 0)
    for head in range(heads):
        acc[head * HD : (head + 1) * HD, :] = (
            acc[head * HD : (head + 1) * HD, :] / total[head : head + 1, :]
        )
    mixed_ref[...] = jnp.transpose(acc[...]).astype(BF16)
    lse_ref[...] = top[...] + jnp.log(total[...])


def attention_forward(first, projected, table, start):
    tokens, columns = projected.shape
    width = columns - 2 * HD
    heads = width // HD
    by_block = pl.BlockSpec((BLOCK, width), lambda i, first: (i, 0))
    whole = pl.BlockSpec((tokens, width), lambda i, first: (0, 0))
    return pl.pallas_call(
        functools.partial(forward_kernel, heads),
        grid_spec=pltpu.PrefetchScalarGridSpec(
            num_scalar_prefetch=1,
            grid=(tokens // BLOCK,),
            in_specs=[
                pl.BlockSpec((BLOCK, columns), lambda i, first: (i, 0)),
                pl.BlockSpec((BLOCK, 2 * HALF), lambda i, first: (i, 0)),
                pl.BlockSpec((1, BLOCK), lambda i, first: (0, i)),
            ],
            out_specs=[
                by_block,
                whole,
                by_block,
                by_block,
                pl.BlockSpec((heads, BLOCK), lambda i, first: (0, i)),
            ],
            scratch_shapes=[
                pltpu.VMEM((HD, tokens), BF16),
                pltpu.VMEM((heads, BLOCK), F32),
                pltpu.VMEM((heads, BLOCK), F32),
                pltpu.VMEM((width, BLOCK), F32),
            ],
        ),
        out_shape=[jax.ShapeDtypeStruct((tokens, width), BF16)] * 4
        + [jax.ShapeDtypeStruct((heads, tokens), F32)],
        compiler_params=pltpu.CompilerParams(vmem_limit_bytes=VMEM_BYTES),
        cost_estimate=pl.CostEstimate(
            flops=64 * tokens * BLOCK * width, bytes_accessed=8 * tokens * width, transcendentals=0
        ),
        name="attention_forward",
    )(first, projected, table, start)


def backward_kernel(
    heads,
    first_ref,
    query_ref,
    key_ref,
    value_ref,
    mixed_ref,
    grad_ref,
    lse_ref,
    start_ref,
    table_ref,
    out_ref,
    dquery,
    dkey,
    dvalue,
):
    step = pl.program_id(0)
    query = query_ref[...]
    grad = grad_ref[...]
    start = start_ref[...]
    width = query.shape[1]
    token = step * BLOCK + lax.broadcasted_iota(jnp.int32, (BLOCK, BLOCK), 1)
    within = lax.broadcasted_iota(jnp.int32, (BLOCK, BLOCK), 0)
    half_head = half_group((BLOCK, width), heads)
    full_head = full_group((BLOCK, width))
    zero = jnp.zeros((BLOCK, width), BF16)
    product = grad.astype(F32) * mixed_ref[...].astype(F32)
    chooser = (
        lax.broadcasted_iota(jnp.int32, (8, width), 0)
        == lax.broadcasted_iota(jnp.int32, (8, width), 1) // HD
    ).astype(F32)
    correction = exact(chooser, product, ((1,), (1,)))

    @pl.when(step == 0)
    def _():
        dkey[...] = jnp.zeros_like(dkey)
        dvalue[...] = jnp.zeros_like(dvalue)

    dquery[...] = jnp.zeros_like(dquery)

    def one_block(block, carried):
        offset = pl.multiple_of(block * BLOCK, BLOCK)
        rows = pl.ds(offset, BLOCK)
        keys = key_ref[rows, :]
        values = value_ref[rows, :]
        place = offset + within
        visible = (place >= start) & (place <= token)
        new_query = dquery[...]
        new_key = dkey[rows, :]
        new_value = dvalue[rows, :]
        for head in range(heads):
            own_keys = jnp.where(half_head == head, keys, zero)
            own_values = jnp.where(full_head == head, values, zero)
            scores = dot_nt(own_keys, query) * ATTENTION_SCALE
            probs = jnp.where(visible, jnp.exp(scores - lse_ref[head : head + 1, :]), 0.0)
            pressure = dot_nt(own_values, grad)
            dscores = (probs * (pressure - correction[head : head + 1, :])).astype(BF16)
            new_value = new_value + dot_nn(
                probs.astype(BF16), jnp.where(full_head == head, grad, zero)
            )
            new_key = new_key + dot_nn(dscores, jnp.where(half_head == head, query, zero))
            new_query = new_query + dot_tn(dscores, own_keys)
        dquery[...] = new_query
        dkey[rows, :] = new_key
        dvalue[rows, :] = new_value
        return carried

    lax.fori_loop(first_ref[step], step + 1, one_block, 0)
    own_rows = pl.ds(pl.multiple_of(step * BLOCK, BLOCK), BLOCK)
    cosine, sine = tables(table_ref[own_rows, :], width)
    out_ref[own_rows, :width] = (turn(dquery[...], cosine, -sine) * ATTENTION_SCALE).astype(BF16)

    @pl.when(step == pl.num_programs(0) - 1)
    def _():
        def fold(block, carried):
            rows = pl.ds(pl.multiple_of(block * BLOCK, BLOCK), BLOCK)
            cosine, sine = tables(table_ref[rows, :], width)
            turned = turn(dkey[rows, :], cosine, -sine) * ATTENTION_SCALE
            out_ref[rows, width:] = (
                exact(turned, spread_keys(width), ((1,), (1,)))
                + exact(dvalue[rows, :], spread_values(width), ((1,), (1,)))
            ).astype(BF16)
            return carried

        lax.fori_loop(0, pl.num_programs(0), fold, 0)


def attention_backward(first, query, keys, values, mixed, grad, lse, start, table):
    tokens, width = query.shape
    heads = width // HD
    columns = width + 2 * HD
    by_block = pl.BlockSpec((BLOCK, width), lambda i, first: (i, 0))
    whole = pl.BlockSpec((tokens, width), lambda i, first: (0, 0))
    return pl.pallas_call(
        functools.partial(backward_kernel, heads),
        grid_spec=pltpu.PrefetchScalarGridSpec(
            num_scalar_prefetch=1,
            grid=(tokens // BLOCK,),
            in_specs=[
                by_block,
                whole,
                whole,
                by_block,
                by_block,
                pl.BlockSpec((heads, BLOCK), lambda i, first: (0, i)),
                pl.BlockSpec((1, BLOCK), lambda i, first: (0, i)),
                pl.BlockSpec((tokens, 2 * HALF), lambda i, first: (0, 0)),
            ],
            out_specs=pl.BlockSpec((tokens, columns), lambda i, first: (0, 0)),
            scratch_shapes=[
                pltpu.VMEM((BLOCK, width), F32),
                pltpu.VMEM((tokens, width), F32),
                pltpu.VMEM((tokens, width), F32),
            ],
        ),
        out_shape=jax.ShapeDtypeStruct((tokens, columns), BF16),
        compiler_params=pltpu.CompilerParams(vmem_limit_bytes=VMEM_BYTES),
        cost_estimate=pl.CostEstimate(
            flops=160 * tokens * BLOCK * width,
            bytes_accessed=24 * tokens * width,
            transcendentals=0,
        ),
        name="attention_backward",
    )(first, query, keys, values, mixed, grad, lse, start, table)


def token_starts(lengths_row, group_tokens):
    count = lengths_row.shape[0]
    order = jnp.arange(count, dtype=jnp.int32)
    finish = jnp.sum(jnp.where(order[None, :] <= order[:, None], lengths_row[None, :], 0), axis=1)
    place = jnp.arange(group_tokens, dtype=jnp.int32)
    passed = place[:, None] >= finish[None, :]
    return jnp.max(jnp.where(passed, finish[None, :], 0), axis=1), place


def inverse_norm(values):
    return lax.rsqrt(jnp.mean(values * values, axis=1, keepdims=True) + EPSILON)


def after(value, *earlier):
    return lax.optimization_barrier((value, *earlier))[0]


def sum_over_groups(value):
    return lax.psum_scatter(value, "dp", scatter_dimension=0, tiled=True)


def gather_groups(value):
    return lax.all_gather(value, "dp", axis=0, tiled=True)


def body(
    tokens,
    cotangent,
    query_weight,
    key_weight,
    value_weight,
    output_weight,
    gate_weight,
    up_weight,
    down_weight,
    attention_gain,
    feedforward_gain,
    lengths,
):
    members = lax.axis_size("fsdp")
    groups = lax.axis_size("dp")
    rows, model = tokens.shape
    group_tokens = rows * members
    shard = query_weight.shape[0]
    heads = NH // members
    width = heads * HD
    columns = width + 2 * HD
    copies = members // KVH
    out_columns = model // members
    down_rows = down_weight.shape[0]
    units = groups * down_rows // CHUNKS
    gain_one = attention_gain.astype(F32)[:, None]
    gain_two = feedforward_gain.astype(F32)[:, None]
    member = lax.axis_index("fsdp").astype(jnp.int32)[None]

    scaled_query = (query_weight * gain_one).astype(BF16)
    scaled_key = (key_weight * gain_one).astype(BF16)
    scaled_value = (value_weight * gain_one).astype(BF16)
    packed_in = jnp.concatenate(
        [
            scaled_query.reshape(shard, members, heads, 2, HALF)
            .transpose(1, 0, 3, 2, 4)
            .reshape(members, shard, width),
            jnp.repeat(
                scaled_key.reshape(shard, KVH, HD).transpose(1, 0, 2), copies, axis=0
            ),
            jnp.repeat(
                scaled_value.reshape(shard, KVH, HD).transpose(1, 0, 2), copies, axis=0
            ),
        ],
        axis=2,
    )
    packed_in, packed_out = plane_swap(
        [packed_in, output_weight.reshape(shard, members, out_columns).transpose(1, 0, 2)],
        members,
        1,
    )
    packed_in = packed_in.reshape(members * shard, columns)
    packed_out = packed_out.reshape(members * shard, out_columns)
    inputs = tokens.astype(F32)
    inverse_one = inverse_norm(inputs)
    normed_one = plane_gather(after((inputs * inverse_one).astype(BF16), packed_in), members, 0, True)
    projection = gather_groups(packed_in)
    out_columns_piece = gather_groups(packed_out)
    upstream = cotangent.astype(F32)
    down_all = gather_groups(after(down_weight, normed_one))
    gate_up = exchanged(
        units_apart(
            member,
            after(gate_weight, normed_one),
            up_weight,
            gain_two,
            members,
            groups,
            CHUNKS,
        )
    )

    start, place = token_starts(lengths[0], group_tokens)
    first = start[::BLOCK] // BLOCK
    frequency = ROPE_BASE ** (-(2.0 * jnp.arange(HALF, dtype=F32)) / HD)
    angles = (place - start).astype(F32)[:, None] * frequency[None, :]
    table = jnp.concatenate([jnp.cos(angles), jnp.sin(angles)], axis=1)
    start = start[None, :]

    projected = dot_nn(normed_one, projection)
    out_blocks = exchanged(
        rows_apart(member, after(out_columns_piece, projected), members)
    )
    query, keys, values, mixed, lse = attention_forward(first, projected, table, start)
    mixed_then, out_blocks, gate_up = lax.optimization_barrier((mixed, out_blocks, gate_up))
    gate_up_chunks = [
        gather_groups(part) for part in rows_together(member, gate_up, CHUNKS)
    ]
    out_piece = columns_together(member, out_blocks)
    branch_one = product_scatter([mixed_then], [out_piece], False, members, 2, True)
    residual = inputs + RESIDUAL_SCALE * branch_one

    inverse_two = inverse_norm(residual)
    normed_two, down_all = lax.optimization_barrier(
        ((residual * inverse_two).astype(BF16), down_all)
    )
    normed_two = plane_gather(normed_two, members, 3, False)
    grad_two = plane_gather(
        after((RESIDUAL_SCALE * upstream).astype(BF16), normed_two), members, 9, False
    )
    hiddens = []
    grad_boths = []
    gate_up_grads = []
    for chunk in range(CHUNKS):
        both_weight = gate_up_chunks[chunk]
        down_piece = down_all[chunk * units : (chunk + 1) * units]
        both = dot_nn(normed_two, both_weight)
        gate = both[:, :units]
        up = both[:, units:]
        sigmoid = jax.nn.sigmoid(gate)
        hidden = (gate * sigmoid * up).astype(BF16)
        grad_hidden = dot_nt(grad_two, down_piece)
        grad_both = jnp.concatenate(
            [
                (grad_hidden * up * sigmoid * (1.0 + gate * (1.0 - sigmoid))).astype(BF16),
                (grad_hidden * gate * sigmoid).astype(BF16),
            ],
            axis=1,
        )
        gate_up_grad = dot_tn(normed_two, grad_both).astype(BF16)
        gate_up_grads.append(sum_over_groups(gate_up_grad))
        normed_two, grad_two, hidden, grad_both, _ = lax.optimization_barrier(
            (normed_two, grad_two, hidden, grad_both, gate_up_grad)
        )
        hiddens.append(hidden)
        grad_boths.append(grad_both)
    weighted_two = product_scatter(grad_boths, gate_up_chunks, True, members, 4, False)
    grad_residual = (
        upstream
        + inverse_two * weighted_two
        - residual * inverse_two**3 * jnp.mean(weighted_two * residual, axis=1, keepdims=True)
    )
    gain_term_two = jnp.sum(weighted_two * residual * inverse_two, axis=0)

    grad_one, gate_up_grads[0] = lax.optimization_barrier(
        ((RESIDUAL_SCALE * grad_residual).astype(BF16), gate_up_grads[0])
    )
    grad_one, down_grad, out_sibling, out_own = plane_gather(
        grad_one, members, 5, True, (hiddens, grad_two, down_all)
    )
    down_grad = sum_over_groups(down_grad)
    half_rows = group_tokens // 2
    out_sibling = send_to(out_sibling, members, lambda m: m ^ 1)
    grad_mixed = dot_nt(grad_one, out_piece).astype(BF16)
    out_grad = dot_tn(mixed, grad_one).astype(BF16)
    out_grad = lax.all_to_all(out_grad, "fsdp", split_axis=1, concat_axis=0, tiled=True)
    grad_mixed, gate_up_grads[-1], out_own, out_sibling = lax.optimization_barrier(
        (grad_mixed, gate_up_grads[-1], out_own, out_sibling)
    )
    steps = len(plane_masks(members))
    half_rows //= 2
    out_sent = send_to(
        added(out_own[half_rows:], out_sibling[half_rows:]).astype(BF16),
        members,
        hopped(steps - 1, members),
    )
    out_kept = added(out_own[:half_rows], out_sibling[:half_rows]).astype(BF16)
    gate_up_grads = [exchanged(rows_apart(member, part, members)) for part in gate_up_grads]
    grad_projected = attention_backward(
        first, query, keys, values, mixed, grad_mixed, lse, start, table
    )
    packed_grad = jnp.concatenate(
        [dot_tn(normed_one, grad_projected).astype(BF16), out_grad], axis=1
    )
    grad_projected, packed_grad, gate_up_grads, out_sent, out_kept, down_grad = (
        lax.optimization_barrier(
            (grad_projected, packed_grad, gate_up_grads, out_sent, out_kept, down_grad)
        )
    )
    for step in reversed(range(steps - 1)):
        half_rows //= 2
        out_next = added(out_kept[half_rows:], out_sent[half_rows:]).astype(BF16)
        out_kept = added(out_kept[:half_rows], out_sent[:half_rows])
        if step:
            out_kept = out_kept.astype(BF16)
        out_sent = send_to(out_next, members, hopped(step, members))
    packed_grad = sum_over_groups(packed_grad)
    weighted_one = product_scatter([grad_projected], [projection], True, members, 6, True)
    grad_inputs = (
        grad_residual
        + inverse_one * weighted_one
        - inputs * inverse_one**3 * jnp.mean(weighted_one * inputs, axis=1, keepdims=True)
    )
    gain_term_one = jnp.sum(weighted_one * inputs * inverse_one, axis=0)

    gains = jnp.stack(
        [
            gain_term_one.reshape(groups, members, shard),
            gain_term_two.reshape(groups, members, shard),
        ],
        axis=2,
    ).reshape(groups, members, 2 * shard)
    gains = jnp.pad(
        gains.transpose(1, 0, 2), ((0, 0), (0, (-groups) % 8), (0, (-2 * shard) % 128))
    )
    gains = total_over_all(gains, groups, 8)
    out_sent, out_kept, _ = lax.optimization_barrier((out_sent, out_kept, gains))
    output = residual + RESIDUAL_SCALE * added(out_kept, out_sent)

    gains = lax.dynamic_slice_in_dim(gains, lax.axis_index("dp"), 1, 0)[0, : 2 * shard]
    gains = gains.reshape(2, shard)
    gate_grad, up_grad = units_together(
        member, after(gate_up_grads, gains), gain_two, members, groups
    )
    query_grad, key_grad, value_grad, out_grad = heads_together(
        member, exchanged(rows_apart(member, packed_grad, members)), gain_one, heads
    )
    return (
        output.astype(BF16),
        grad_inputs.astype(BF16),
        query_grad,
        key_grad,
        value_grad,
        out_grad,
        gate_grad,
        up_grad,
        down_grad.astype(F32),
        gains[0] / gain_one[:, 0],
        gains[1] / gain_two[:, 0],
    )


def solution(mesh):
    by_rows = P(("dp", "fsdp"), None)
    by_entries = P(("dp", "fsdp"))
    return jax.shard_map(
        body,
        mesh=mesh,
        in_specs=(by_rows,) * 9 + (by_entries,) * 2 + (P("dp", None),),
        out_specs=(by_rows,) * 9 + (by_entries,) * 2,
        check_vma=False,
    )
```

```python
import functools

import jax
import jax.numpy as jnp
from jax import lax
from jax.experimental import pallas as pl
from jax.experimental.pallas import tpu as pltpu
from jax.sharding import PartitionSpec as P

NH = 32
KVH = 8
HD = 64
HALF = HD // 2

EPSILON = 1e-05
RESIDUAL_SCALE = 0.22
ATTENTION_SCALE = 0.015625
ROPE_BASE = 10000000.0
MASKED = -1e30
BLOCK = 256
CHUNKS = 2
PIECES = 4
SCATTER_PIECES = 8
VMEM_BYTES = 58 * 1024 * 1024
MESH = pl.DeviceIdType.MESH
BF16 = jnp.bfloat16
F32 = jnp.float32


def dot_nn(left, right):
    return jnp.dot(left, right, preferred_element_type=F32)


def dot_nt(left, right):
    return lax.dot_general(left, right, (((1,), (1,)), ((), ())), preferred_element_type=F32)


def dot_tn(left, right):
    return lax.dot_general(left, right, (((0,), (0,)), ((), ())), preferred_element_type=F32)


def flip(index, mask):
    return index + mask * (1 - 2 * ((index // mask) % 2))


def plane_masks(member_count):
    masks = []
    mask = 2
    while mask < member_count:
        masks.append(mask)
        mask *= 2
    return masks


def hop(index, step, masks):
    core = index % 2
    return (1 - core) * flip(index, masks[step]) + core * flip(index, masks[-1 - step])


def walk(index, subset, masks):
    for step in range(len(masks)):
        if (subset >> step) & 1:
            index = hop(index, step, masks)
    return index


def greet(group, member, masks):
    barrier = pltpu.get_barrier_semaphore()
    partners = [hop(member, step, masks) for step in range(len(masks))] + [flip(member, 1)]
    for partner in partners:
        pl.semaphore_signal(barrier, inc=1, device_id=(group, partner), device_id_type=MESH)
    pl.semaphore_wait(barrier, len(partners))


def gather_kernel(member_count, in_order, count, own_ref, *refs):
    operands = refs[: count + 2] if count else ()
    refs = refs[len(operands) :]
    all_ref, results, refs = refs[0], refs[1 : 4 if count else 1], refs[4 if count else 1 :]
    link_send, link_recv, core_send, core_recv, local_sem = refs[:5]
    group = lax.axis_index("dp")
    member = lax.axis_index("fsdp")
    masks = plane_masks(member_count)
    steps = len(masks)
    rows = own_ref.shape[0]
    piece = rows // PIECES
    greet(group, member, masks)

    blocks = 1 << steps

    def place(owner, subset, side, part):
        block = walk(owner, subset, masks) if in_order else subset + side * blocks
        return all_ref.at[pl.ds(pl.multiple_of(block * rows + part * piece, piece), piece)]

    def link_copy(step, subset, part):
        number = (1 << step) - 1 + subset
        here = place(member, subset, 0, part)
        there = here if in_order else place(member, subset | (1 << step), 0, part)
        return pltpu.make_async_remote_copy(
            own_ref.at[pl.ds(part * piece, piece)] if subset == 0 else here,
            there,
            link_send.at[number, part],
            link_recv.at[number, part],
            device_id=(group, hop(member, step, masks)),
            device_id_type=MESH,
        )

    def core_copy(subset, part):
        here = place(member, subset, 0, part)
        there = here if in_order else place(member, subset, 1, part)
        return pltpu.make_async_remote_copy(
            own_ref.at[pl.ds(part * piece, piece)] if subset == 0 else here,
            there,
            core_send.at[subset, part],
            core_recv.at[subset, part],
            device_id=(group, flip(member, 1)),
            device_id_type=MESH,
        )

    for part in range(PIECES):
        for step in range(steps):
            link_copy(step, 0, part).start()
    first = pl.multiple_of(member * rows, rows) if in_order else 0
    keep = pltpu.make_async_copy(own_ref, all_ref.at[pl.ds(first, rows)], local_sem)
    keep.start()
    for part in range(PIECES):
        core_copy(0, part).start()
    tiles = []
    if count:
        helds = refs[5 : 7 + count]
        down_grad, out_sibling, out_own, turned = refs[7 + count : 11 + count]
        load_sem, store_sem = refs[11 + count :]
        hiddens, gradient, down = helds[:count], helds[count], helds[count + 1]
        units = hiddens[0].shape[1]
        loads = [
            pltpu.make_async_copy(source, target, load_sem.at[number])
            for number, (source, target) in enumerate(zip(operands, helds))
        ]
        stores = [
            pltpu.make_async_copy(source, target, store_sem.at[number])
            for number, (source, target) in enumerate(
                zip((down_grad, out_sibling, out_own), results)
            )
        ]
        for load in loads:
            load.start()
        half = out_own.shape[0]
        width = 256

        def out_tile(target, base, column):
            total = None
            for number in range(count):
                term = dot_nn(
                    hiddens[number][base : base + half, :],
                    down[number * units : (number + 1) * units, column : column + width],
                )
                total = term if total is None else total + term
            target[:, column : column + width] = total.astype(BF16)

        def turn_tile(number):
            turned[...] = jnp.transpose(hiddens[number][...])

        def grad_tile(number, column):
            down_grad[number * units : (number + 1) * units, column : column + width] = dot_nn(
                turned[...], gradient[:, column : column + width]
            ).astype(BF16)

        for load in loads[:count] + loads[count + 1 :]:
            tiles.append(load.wait)
        for target, base, store in (
            (out_sibling, half, stores[1]),
            (out_own, 0, stores[2]),
        ):
            for column in range(0, down.shape[1], width):
                tiles.append(functools.partial(out_tile, target, base, column))
            tiles.append(store.start)
        tiles.append(loads[count].wait)
        for number in range(count):
            tiles.append(functools.partial(turn_tile, number))
            for column in range(0, down.shape[1], width):
                tiles.append(functools.partial(grad_tile, number, column))
        tiles.append(stores[0].start)
    shares = [1 << step for step in range(steps) for part in range(PIECES)]
    ends = [-(-len(tiles) * sum(shares[: n + 1]) // sum(shares)) for n in range(len(shares))]

    turn = 0
    for step in range(steps):
        for part in range(PIECES):
            for subset in range(1 << step):
                link_copy(step, subset, part).wait_recv()
                arrived = subset | (1 << step)
                for later in range(step + 1, steps):
                    link_copy(later, arrived, part).start()
                core_copy(arrived, part).start()
            for run in tiles[ends[turn - 1] if turn else 0 : ends[turn]]:
                run()
            turn += 1
    for part in range(PIECES):
        for subset in range(1 << steps):
            core_copy(subset, part).wait()
    for part in range(PIECES):
        for step in range(steps):
            for subset in range(1 << step):
                link_copy(step, subset, part).wait_send()
    keep.wait()
    if count:
        for store in stores:
            store.wait()


def plane_gather(own, member_count, collective_id, in_order, extras=None):
    rows, width = own.shape
    steps = len(plane_masks(member_count))
    blocks = 1 << steps
    total = member_count * rows
    any_space = pl.BlockSpec(memory_space=pl.ANY)
    scratch = [
        pltpu.SemaphoreType.DMA((blocks - 1, PIECES)),
        pltpu.SemaphoreType.DMA((blocks - 1, PIECES)),
        pltpu.SemaphoreType.DMA((blocks, PIECES)),
        pltpu.SemaphoreType.DMA((blocks, PIECES)),
        pltpu.SemaphoreType.DMA,
    ]
    operands = [own]
    out_shape = [jax.ShapeDtypeStruct((total, width), own.dtype)]
    count = 0
    if extras:
        hiddens, gradient, down = extras
        count = len(hiddens)
        operands += [*hiddens, gradient, down]
        scratch += [pltpu.VMEM(value.shape, BF16) for value in operands[1:]]
        out_shape += [
            jax.ShapeDtypeStruct((down.shape[0], gradient.shape[1]), BF16),
            jax.ShapeDtypeStruct((total // 2, down.shape[1]), BF16),
            jax.ShapeDtypeStruct((total // 2, down.shape[1]), BF16),
        ]
        scratch += [pltpu.VMEM(value.shape, BF16) for value in out_shape[1:]]
        scratch.append(pltpu.VMEM(hiddens[0].shape[::-1], BF16))
        scratch += [pltpu.SemaphoreType.DMA((count + 2,)), pltpu.SemaphoreType.DMA((3,))]
    result = pl.pallas_call(
        functools.partial(gather_kernel, member_count, in_order, count),
        out_shape=out_shape,
        in_specs=[any_space] * len(operands),
        out_specs=[any_space] * len(out_shape),
        scratch_shapes=scratch,
        compiler_params=pltpu.CompilerParams(
            collective_id=collective_id, has_side_effects=True, vmem_limit_bytes=VMEM_BYTES
        ),
        cost_estimate=pl.CostEstimate(
            flops=0, bytes_accessed=(1 if extras else 60) * total * width, transcendentals=0
        ),
        name="plane_gather",
    )(*operands)
    return result if extras else result[0]


def swap_kernel(member_count, count, *refs):
    sources, targets = refs[:count], refs[count : 2 * count]
    send_sem, recv_sem, local_sem = refs[2 * count :]
    group = lax.axis_index("dp")
    member = lax.axis_index("fsdp")
    barrier = pltpu.get_barrier_semaphore()
    for away in range(1, member_count):
        pl.semaphore_signal(
            barrier,
            inc=1,
            device_id=(group, (member + away) % member_count),
            device_id_type=MESH,
        )
    pl.semaphore_wait(barrier, member_count - 1)

    def copy(number, away):
        target = (member + away) % member_count
        return pltpu.make_async_remote_copy(
            sources[number].at[target],
            targets[number].at[member],
            send_sem.at[number, away],
            recv_sem.at[number, away],
            device_id=(group, target),
            device_id_type=MESH,
        )

    def keep(number):
        return pltpu.make_async_copy(
            sources[number].at[member], targets[number].at[member], local_sem.at[number]
        )

    for number in range(count):
        for away in range(1, member_count):
            copy(number, away).start()
        keep(number).start()
    for number in range(count):
        for away in range(1, member_count):
            copy(number, away).wait()
        keep(number).wait()


def plane_swap(values, member_count, collective_id):
    count = len(values)
    any_space = pl.BlockSpec(memory_space=pl.ANY)
    return pl.pallas_call(
        functools.partial(swap_kernel, member_count, count),
        out_shape=[jax.ShapeDtypeStruct(value.shape, value.dtype) for value in values],
        in_specs=[any_space] * count,
        out_specs=[any_space] * count,
        scratch_shapes=[
            pltpu.SemaphoreType.DMA((count, member_count)),
            pltpu.SemaphoreType.DMA((count, member_count)),
            pltpu.SemaphoreType.DMA((count,)),
        ],
        compiler_params=pltpu.CompilerParams(collective_id=collective_id, has_side_effects=True),
        cost_estimate=pl.CostEstimate(
            flops=0,
            bytes_accessed=60 * sum(value.size for value in values),
            transcendentals=0,
        ),
        name="plane_swap",
    )(*values)


def product_scatter_kernel(member_count, in_order, transposed, count, rows, with_grad, *refs):
    if with_grad:
        other_ref, grad_ref = refs[0], refs[2 * count + 2]
        held_other, held_grad, other_sem, grad_sem = refs[-4:]
        refs = refs[1 : 2 * count + 2] + refs[2 * count + 3 : -4]
    lefts, rights, sum_ref = refs[:count], refs[count : 2 * count], refs[2 * count]
    held_lefts, held_rights = refs[2 * count + 1 : 3 * count + 1], refs[3 * count + 1 : 4 * count + 1]
    (
        outgoing,
        core_buffer,
        held,
        link_buffer,
        left_sem,
        right_sem,
        link_send,
        link_recv,
        core_send,
        core_recv,
    ) = refs[4 * count + 1 :]
    group = lax.axis_index("dp")
    member = lax.axis_index("fsdp")
    sibling = flip(member, 1)
    masks = plane_masks(member_count)
    steps = len(masks)
    blocks = 1 << steps
    pieces = SCATTER_PIECES
    piece = sum_ref.shape[1] // pieces

    def left_copy(number, side, subset):
        owner = sibling if side else member
        block = walk(owner, subset, masks) if in_order else subset + side * blocks
        return pltpu.make_async_copy(
            lefts[number].at[pl.ds(pl.multiple_of(block * rows, rows), rows)],
            held_lefts[number].at[pl.ds((side * blocks + subset) * rows, rows)],
            left_sem.at[number, side, subset],
        )

    def right_copy(number):
        source = rights[number]
        if transposed and source.shape[1] != held_rights[number].shape[1]:
            source = source.at[:, pl.ds(0, held_rights[number].shape[1])]
        return pltpu.make_async_copy(source, held_rights[number], right_sem.at[number])

    for number in range(count):
        right_copy(number).start()
        for side in (1, 0):
            for subset in range(blocks):
                left_copy(number, side, subset).start()
    if with_grad:
        other_copy = pltpu.make_async_copy(other_ref, held_other, other_sem)
        other_copy.start()
    greet(group, member, masks)

    def part(side, subset, where):
        where_rows = pl.ds((side * blocks + subset) * rows, rows)
        total = None
        for number in range(count):
            left = held_lefts[number][where_rows, :]
            if transposed:
                term = dot_nt(left, held_rights[number][where, :])
            else:
                term = dot_nn(left, held_rights[number][:, where])
            total = term if total is None else total + term
        return total

    def columns(index):
        return pl.ds(pl.multiple_of(index * piece, piece), piece)

    def core_copy(index):
        return pltpu.make_async_remote_copy(
            outgoing.at[:, columns(index)],
            core_buffer.at[:, columns(index)],
            core_send.at[index],
            core_recv.at[index],
            device_id=(group, sibling),
            device_id_type=MESH,
        )

    def slot(step, kept):
        return sum(blocks >> (s + 1) for s in range(step)) + (kept >> (step + 1))

    def link_copy(step, subset, index):
        number = slot(step, subset & ~(1 << step))
        return pltpu.make_async_remote_copy(
            held.at[pl.ds(subset * rows, rows), columns(index)],
            link_buffer.at[pl.ds(number * rows, rows), columns(index)],
            link_send.at[number, index],
            link_recv.at[number, index],
            device_id=(group, hop(member, step, masks)),
            device_id_type=MESH,
        )

    order = sorted(range(blocks), key=lambda s: (-(s & 1), -s))

    for number in range(count):
        right_copy(number).wait()
        for side in (1, 0):
            for subset in range(blocks):
                left_copy(number, side, subset).wait()

    def for_sibling(index):
        where = columns(index)
        for subset in range(blocks):
            outgoing[pl.ds(subset * rows, rows), where] = part(1, subset, where).astype(BF16)
        core_copy(index).start()

    def for_links(index):
        where = columns(index)
        core_copy(index).wait_recv()
        for subset in order:
            where_rows = pl.ds(subset * rows, rows)
            total = part(0, subset, where) + core_buffer[where_rows, where].astype(F32)
            if subset == 0:
                sum_ref[:, where] = total
            else:
                held[where_rows, where] = total.astype(BF16)
            if subset & 1:
                link_copy(0, subset, index).start()

    def for_both(index, carried):
        for_sibling(index)
        for_links(index - 1)
        return carried

    for_sibling(0)
    lax.fori_loop(1, pieces, for_both, 0)
    for_links(pieces - 1)
    if with_grad:
        other_copy.wait()
        units = held_grad.shape[1] // pieces
        late = 3 if steps > 1 else 0

    def grad_tile(index):
        where = pl.ds(pl.multiple_of(index * units, units), units)
        turned = dot_tn(held_lefts[-1][:, where], held_other[...])
        held_grad[:, where] = jnp.transpose(turned.astype(BF16))

    for step in range(steps):

        def one_step(index, carried, step=step):
            where = columns(index)
            if with_grad and step == 0:
                pl.when(index >= late)(lambda: grad_tile(index - late))
            if with_grad and step == 1:
                pl.when(index < late)(lambda: grad_tile(pieces - late + index))
            for kept in sorted(range(0, blocks, 2 << step), reverse=True):
                link_copy(step, kept | (1 << step), index).wait_recv()
                arrived = link_buffer[pl.ds(slot(step, kept) * rows, rows), where].astype(F32)
                if kept == 0:
                    sum_ref[:, where] += arrived
                else:
                    where_rows = pl.ds(kept * rows, rows)
                    held[where_rows, where] = (
                        held[where_rows, where].astype(F32) + arrived
                    ).astype(BF16)
                if (kept >> (step + 1)) & 1:
                    link_copy(step + 1, kept, index).start()
            return carried

        lax.fori_loop(0, pieces, one_step, 0)
        if with_grad and step == min(1, steps - 1):
            grad_copy = pltpu.make_async_copy(held_grad, grad_ref, grad_sem)
            grad_copy.start()

    def finish(index, carried):
        core_copy(index).wait_send()
        for step in range(steps):
            for kept in range(0, blocks, 2 << step):
                link_copy(step, kept | (1 << step), index).wait_send()
        return carried

    lax.fori_loop(0, pieces, finish, 0)
    if with_grad:
        grad_copy.wait()


def product_scatter(
    lefts, rights, transposed, member_count, collective_id, in_order, other=None, weight=60
):
    count = len(lefts)
    total = lefts[0].shape[0]
    width = rights[0].shape[0 if transposed else 1]
    rows = total // member_count
    blocks = 1 << len(plane_masks(member_count))
    depth = sum(left.shape[1] for left in lefts)
    scratch = (
        [pltpu.VMEM(left.shape, BF16) for left in lefts]
        + [
            pltpu.VMEM((right.shape[0], left.shape[1]) if transposed else right.shape, BF16)
            for left, right in zip(lefts, rights)
        ]
        + [
            pltpu.VMEM((blocks * rows, width), BF16),
            pltpu.VMEM((blocks * rows, width), BF16),
            pltpu.VMEM((blocks * rows, width), BF16),
            pltpu.VMEM(((blocks - 1) * rows, width), BF16),
            pltpu.SemaphoreType.DMA((count, 2, blocks)),
            pltpu.SemaphoreType.DMA((count,)),
            pltpu.SemaphoreType.DMA((blocks - 1, SCATTER_PIECES)),
            pltpu.SemaphoreType.DMA((blocks - 1, SCATTER_PIECES)),
            pltpu.SemaphoreType.DMA((SCATTER_PIECES,)),
            pltpu.SemaphoreType.DMA((SCATTER_PIECES,)),
        ]
    )
    any_space = pl.BlockSpec(memory_space=pl.ANY)
    in_vmem = pl.BlockSpec(memory_space=pltpu.VMEM)
    operands = [*lefts, *rights]
    out_shape = [jax.ShapeDtypeStruct((rows, width), F32)]
    if other is not None:
        operands = [other] + operands
        grad_shape = (other.shape[1], lefts[-1].shape[1])
        out_shape.append(jax.ShapeDtypeStruct(grad_shape, BF16))
        scratch += [
            pltpu.VMEM(other.shape, BF16),
            pltpu.VMEM(grad_shape, BF16),
            pltpu.SemaphoreType.DMA,
            pltpu.SemaphoreType.DMA,
        ]
    result = pl.pallas_call(
        functools.partial(
            product_scatter_kernel,
            member_count,
            in_order,
            transposed,
            count,
            rows,
            other is not None,
        ),
        out_shape=out_shape,
        in_specs=[any_space] * len(operands),
        out_specs=[in_vmem] + [any_space] * (len(out_shape) - 1),
        scratch_shapes=scratch,
        compiler_params=pltpu.CompilerParams(
            collective_id=collective_id, has_side_effects=True, vmem_limit_bytes=VMEM_BYTES
        ),
        cost_estimate=pl.CostEstimate(
            flops=0, bytes_accessed=weight * total * width, transcendentals=0
        ),
        name="product_scatter",
    )(*operands)
    return result[0] if other is None else result


def finale_kernel(member_count, group_count, packed_ref, part_ref, arrived, sum_ref, *refs):
    near, held, far = refs[:3]
    packed_send, packed_recv, own_sem, near_send, near_recv, far_send, far_recv = refs[3:]
    group = lax.axis_index("dp")
    member = lax.axis_index("fsdp")
    shard = arrived.shape[1]
    barrier = pltpu.get_barrier_semaphore()
    for away in range(1, member_count):
        pl.semaphore_signal(
            barrier,
            inc=1,
            device_id=(group, (member + away) % member_count),
            device_id_type=MESH,
        )
    for away in range(1, group_count):
        pl.semaphore_signal(
            barrier, inc=1, device_id=((group + away) % group_count, member), device_id_type=MESH
        )
    pl.semaphore_wait(barrier, member_count + group_count - 2)

    def rows_of(target):
        return packed_ref.at[pl.ds(pl.multiple_of(target * shard, shard), shard)]

    def packed_copy(away):
        target = (member + away) % member_count
        return pltpu.make_async_remote_copy(
            rows_of(target),
            arrived.at[away],
            packed_send.at[away],
            packed_recv.at[away],
            device_id=(group, target),
            device_id_type=MESH,
        )

    def near_copy(away):
        target = (member + away) % member_count
        return pltpu.make_async_remote_copy(
            part_ref.at[target],
            near.at[away],
            near_send.at[away],
            near_recv.at[away],
            device_id=(group, target),
            device_id_type=MESH,
        )

    def far_copy(away):
        return pltpu.make_async_remote_copy(
            held,
            far.at[away],
            far_send.at[away],
            far_recv.at[away],
            device_id=((group + away) % group_count, member),
            device_id_type=MESH,
        )

    own_copy = pltpu.make_async_copy(rows_of(member), arrived.at[0], own_sem)
    for away in range(1, member_count):
        near_copy(away).start()
    for away in range(1, member_count):
        packed_copy(away).start()
    own_copy.start()
    total = part_ref[member]
    for away in range(1, member_count):
        near_copy(away).wait_recv()
        total = total + near[away]
    held[...] = total
    for away in range(1, group_count):
        far_copy(away).start()

    for away in range(1, member_count):
        packed_copy(away).wait_recv()
    own_copy.wait()
    for away in range(1, group_count):
        far_copy(away).wait_recv()
        total = total + far[away]
    sum_ref[...] = total
    for away in range(1, member_count):
        near_copy(away).wait_send()
        packed_copy(away).wait_send()
    for away in range(1, group_count):
        far_copy(away).wait_send()


def finale(packed, parts, group_count, collective_id):
    member_count, lines, lanes = parts.shape
    shard = packed.shape[0] // member_count
    in_vmem = pl.BlockSpec(memory_space=pltpu.VMEM)
    any_space = pl.BlockSpec(memory_space=pl.ANY)
    members_dma = pltpu.SemaphoreType.DMA((member_count,))
    groups_dma = pltpu.SemaphoreType.DMA((group_count,))
    return pl.pallas_call(
        functools.partial(finale_kernel, member_count, group_count),
        out_shape=[
            jax.ShapeDtypeStruct((member_count, shard, packed.shape[1]), BF16),
            jax.ShapeDtypeStruct((lines, lanes), F32),
        ],
        in_specs=[any_space, in_vmem],
        out_specs=[any_space, in_vmem],
        scratch_shapes=[
            pltpu.VMEM((member_count, lines, lanes), F32),
            pltpu.VMEM((lines, lanes), F32),
            pltpu.VMEM((group_count, lines, lanes), F32),
            members_dma,
            members_dma,
            pltpu.SemaphoreType.DMA,
            members_dma,
            members_dma,
            groups_dma,
            groups_dma,
        ],
        compiler_params=pltpu.CompilerParams(collective_id=collective_id, has_side_effects=True),
        cost_estimate=pl.CostEstimate(flops=0, bytes_accessed=40000000, transcendentals=0),
        name="finale",
    )(packed, parts)


def local_call(kernel, name, out_shape, *operands):
    in_vmem = pl.BlockSpec(memory_space=pltpu.VMEM)
    size = sum(value.size * value.dtype.itemsize for value in operands[1:])
    size += sum(value.size * value.dtype.itemsize for value in out_shape)
    return pl.pallas_call(
        kernel,
        grid_spec=pltpu.PrefetchScalarGridSpec(
            num_scalar_prefetch=1,
            in_specs=[in_vmem] * (len(operands) - 1),
            out_specs=[in_vmem] * len(out_shape),
            grid=(),
        ),
        out_shape=out_shape,
        compiler_params=pltpu.CompilerParams(vmem_limit_bytes=VMEM_BYTES),
        cost_estimate=pl.CostEstimate(flops=0, bytes_accessed=size, transcendentals=0),
        name=name,
    )(*operands)


def rows_apart(member, value, member_count, column=0):
    rows = value.shape[0] // member_count

    def kernel(member_ref, value_ref, *out_refs):
        for away, out_ref in enumerate(out_refs):
            other = member_ref[0] ^ away
            out_ref[...] = value_ref[pl.ds(pl.multiple_of(other * rows, rows), rows), column:]

    shape = jax.ShapeDtypeStruct((rows, value.shape[1] - column), value.dtype)
    return local_call(kernel, "rows_apart", [shape] * member_count, member, value)


def rows_together(member, blocks, chunks):
    rows, width = blocks[0].shape
    part = width // chunks
    count = len(blocks)

    def kernel(member_ref, *refs):
        for away in range(count):
            where = pl.ds(pl.multiple_of((member_ref[0] ^ away) * rows, rows), rows)
            for chunk in range(chunks):
                refs[count + chunk][where, :] = refs[away][:, chunk * part : (chunk + 1) * part]

    shape = jax.ShapeDtypeStruct((count * rows, part), blocks[0].dtype)
    return local_call(kernel, "rows_together", [shape] * chunks, member, *blocks)


def columns_together(member, blocks):
    rows, width = blocks[0].shape
    count = len(blocks)

    def kernel(member_ref, *refs):
        for away in range(count):
            where = pl.ds(pl.multiple_of((member_ref[0] ^ away) * width, width), width)
            refs[count][:, where] = refs[away][...]

    shape = jax.ShapeDtypeStruct((rows, count * width), blocks[0].dtype)
    return local_call(kernel, "columns_together", [shape], member, *blocks)[0]


def exchanged(blocks):
    return [blocks[0]] + [
        lax.ppermute(blocks[away], "fsdp", [(m, m ^ away) for m in range(len(blocks))])
        for away in range(1, len(blocks))
    ]


def added(left, right):
    return left.astype(F32) + right.astype(F32)


def send_to(value, member_count, partner):
    return lax.ppermute(value, "fsdp", [(m, partner(m)) for m in range(member_count)])


def hopped(step, member_count):
    masks = plane_masks(member_count)
    return lambda m: (m ^ masks[step]) if m % 2 == 0 else (m ^ masks[-1 - step])


def unit_strips(member_count, group_count, chunks, per):
    share = group_count // chunks
    for chunk in range(chunks):
        for side in range(2):
            for place in range(share):
                group = chunk * share + place
                yield chunk, side, (side * share + place) * per, group * member_count * per


def units_apart(member, gate, up, gain, member_count, group_count, chunks):
    shard, width = gate.shape
    per = width // (member_count * group_count)
    columns = 2 * group_count * per
    strips = list(unit_strips(member_count, group_count, chunks, per))
    shape = jax.ShapeDtypeStruct((shard, columns), BF16)
    if per % 128:
        scaled = [(value * gain).astype(BF16) for value in (gate, up)]

        def block(away):
            other = member[0] ^ away
            return jnp.concatenate(
                [
                    lax.dynamic_slice_in_dim(scaled[side], base + other * per, per, 1)
                    for chunk, side, column, base in strips
                ],
                axis=1,
            )

        return [block(away) for away in range(member_count)]

    def kernel(member_ref, gate_ref, up_ref, gain_ref, *out_refs):
        for away, out_ref in enumerate(out_refs):
            other = member_ref[0] ^ away
            for chunk, side, column, base in strips:
                where = pl.ds(pl.multiple_of(base + other * per, per), per)
                source = (gate_ref, up_ref)[side][:, where].astype(F32)
                column += chunk * (columns // chunks)
                out_ref[:, column : column + per] = (source * gain_ref[...]).astype(BF16)

    return local_call(kernel, "units_apart", [shape] * member_count, member, gate, up, gain)


def units_together(member, chunk_blocks, gain, member_count, group_count):
    chunks = len(chunk_blocks)
    shard, columns = chunk_blocks[0][0].shape
    per = columns * chunks // (2 * group_count)
    width = per * member_count * group_count
    strips = list(unit_strips(member_count, group_count, chunks, per))
    blocks = [block for group in chunk_blocks for block in group]
    if per % 128:
        results = []
        for side in range(2):
            result = jnp.zeros((shard, width), F32)
            for away in range(member_count):
                other = member[0] ^ away
                for chunk, this, column, base in strips:
                    if this == side:
                        piece = chunk_blocks[chunk][away][:, column : column + per]
                        result = lax.dynamic_update_slice_in_dim(
                            result, piece.astype(F32) * gain, base + other * per, 1
                        )
            results.append(result)
        return results

    def kernel(member_ref, gain_ref, *refs):
        outs = refs[len(blocks) :]
        for away in range(member_count):
            other = member_ref[0] ^ away
            for chunk, side, column, base in strips:
                where = pl.ds(pl.multiple_of(base + other * per, per), per)
                piece = refs[chunk * member_count + away][:, column : column + per]
                outs[side][:, where] = piece.astype(F32) * gain_ref[...]

    shape = jax.ShapeDtypeStruct((shard, width), F32)
    return local_call(kernel, "units_together", [shape] * 2, member, gain, *blocks)


def heads_together(member, arrived, gain, heads):
    count, shard, columns = arrived.shape
    width = heads * HD
    out_width = columns - width - 2 * HD
    copies = count // KVH

    def kernel(member_ref, arrived_ref, gain_ref, query_out, key_out, value_out, out_out):
        row = lax.broadcasted_iota(jnp.int32, (width, width), 0)
        column = lax.broadcasted_iota(jnp.int32, (width, width), 1)
        source = column % HD // HALF * (HALF * heads) + column // HD * HALF + column % HALF
        order = (row == source).astype(BF16)
        pair_row = lax.broadcasted_iota(jnp.int32, (2 * HD, KVH * HD), 0)
        pair_column = lax.broadcasted_iota(jnp.int32, (2 * HD, KVH * HD), 1)
        gain_here = gain_ref[...]
        keys = jnp.zeros((shard, KVH * HD), F32)
        values = jnp.zeros((shard, KVH * HD), F32)
        for away in range(count):
            other = (member_ref[0] + count - away) % count
            where = pl.ds(pl.multiple_of(other * width, width), width)
            query_out[:, where] = dot_nn(arrived_ref[away, :, :width], order) * gain_here
            pair = arrived_ref[away, :, width : width + 2 * HD]
            first = other // copies * HD
            to_keys = (pair_column == pair_row + first) & (pair_row < HD)
            to_values = (pair_column == pair_row - HD + first) & (pair_row >= HD)
            keys = keys + dot_nn(pair, to_keys.astype(BF16))
            values = values + dot_nn(pair, to_values.astype(BF16))
            out_where = pl.ds(pl.multiple_of(other * out_width, out_width), out_width)
            out_out[:, out_where] = arrived_ref[away, :, width + 2 * HD :].astype(F32)
        key_out[...] = keys * gain_here
        value_out[...] = values * gain_here

    shapes = [
        jax.ShapeDtypeStruct((shard, size), F32)
        for size in (count * width, KVH * HD, KVH * HD, count * out_width)
    ]
    return local_call(kernel, "heads_together", shapes, member, arrived, gain)


def units_kernel(normed_ref, gradient_ref, both_ref, down_ref, hidden_ref, grad_ref):
    units = down_ref.shape[0]
    normed = normed_ref[...]
    gradient = gradient_ref[...]
    part = min(256, units)
    for first in range(0, units, part):
        where = slice(first, first + part)
        past = slice(units + first, units + first + part)
        gate = dot_nn(normed, both_ref[:, where])
        up = dot_nn(normed, both_ref[:, past])
        upstream = dot_nt(gradient, down_ref[where, :])
        sigmoid = jax.nn.sigmoid(gate)
        active = gate * sigmoid
        hidden_ref[:, where] = (active * up).astype(BF16)
        grad_ref[:, where] = (
            upstream * up * sigmoid * (1.0 + gate * (1.0 - sigmoid))
        ).astype(BF16)
        grad_ref[:, past] = (upstream * active).astype(BF16)


def hidden_units(normed, gradient, both, down, chunk):
    tokens, model = normed.shape
    units = both.shape[1] // 2
    tile = 512
    by_tile = pl.BlockSpec((tile, model), lambda i: (i, 0))
    return pl.pallas_call(
        units_kernel,
        grid=(tokens // tile,),
        in_specs=[
            by_tile,
            by_tile,
            pl.BlockSpec(both.shape, lambda i: (0, 0)),
            pl.BlockSpec((units, model), lambda i: (chunk, 0)),
        ],
        out_specs=[
            pl.BlockSpec((tile, units), lambda i: (i, 0)),
            pl.BlockSpec((tile, 2 * units), lambda i: (i, 0)),
        ],
        out_shape=[
            jax.ShapeDtypeStruct((tokens, units), BF16),
            jax.ShapeDtypeStruct((tokens, 2 * units), BF16),
        ],
        compiler_params=pltpu.CompilerParams(vmem_limit_bytes=VMEM_BYTES),
        cost_estimate=pl.CostEstimate(
            flops=6 * tokens * model * units,
            bytes_accessed=4 * tokens * model + 6 * units * model,
            transcendentals=tokens * units,
        ),
        name="hidden_units",
    )(normed, gradient, both, down)


def half_group(shape, heads):
    return (lax.broadcasted_iota(jnp.int32, shape, 1) // HALF) % heads


def full_group(shape):
    return lax.broadcasted_iota(jnp.int32, shape, 1) // HD


def spread_keys(width):
    heads = width // HD
    row = lax.broadcasted_iota(jnp.int32, (2 * HD, width), 0)
    column = lax.broadcasted_iota(jnp.int32, (2 * HD, width), 1)
    source = column // (HALF * heads) * HALF + column % HALF
    return (row == source).astype(F32)


def spread_values(width):
    row = lax.broadcasted_iota(jnp.int32, (2 * HD, width), 0)
    column = lax.broadcasted_iota(jnp.int32, (2 * HD, width), 1)
    return (row == HD + column % HD).astype(F32)


def exact(left, right, dims):
    return lax.dot_general(
        left,
        right,
        (dims, ((), ())),
        precision=lax.Precision.HIGHEST,
        preferred_element_type=F32,
    )


def tables(table, width):
    half = width // 2
    row = lax.broadcasted_iota(jnp.int32, (2 * HALF, half), 0)
    column = lax.broadcasted_iota(jnp.int32, (2 * HALF, half), 1) % HALF
    return (
        exact(table, (row == column).astype(F32), ((1,), (0,))),
        exact(table, (row == column + HALF).astype(F32), ((1,), (0,))),
    )


def turn(values, cosine, sine):
    half = cosine.shape[1]
    first = values[:, :half]
    second = values[:, half:]
    return jnp.concatenate([first * cosine - second * sine, second * cosine + first * sine], axis=1)


def forward_kernel(
    heads,
    first_ref,
    normed_ref,
    weight_ref,
    table_ref,
    start_ref,
    query_ref,
    key_ref,
    key_columns_ref,
    value_ref,
    mixed_ref,
    lse_ref,
    value_columns,
    top,
    total,
    acc,
):
    step = pl.program_id(0)
    width = heads * HD
    start = start_ref[...]
    cosine, sine = tables(table_ref[...], width)
    projected = dot_nn(normed_ref[...], weight_ref[:, : width + 2 * HD])
    query = turn(projected[:, :width], cosine, sine).astype(BF16)
    pair = projected[:, width:]
    keys_here = turn(exact(pair, spread_keys(width), ((1,), (0,))), cosine, sine).astype(BF16)
    own_rows = pl.ds(pl.multiple_of(step * BLOCK, BLOCK), BLOCK)
    query_ref[...] = query
    key_ref[own_rows, :] = keys_here
    turned_keys = jnp.transpose(keys_here.astype(F32)).astype(BF16)
    key_columns_ref[:HALF, :] = turned_keys[:HALF, :]
    key_columns_ref[HALF:, :] = turned_keys[width // 2 : width // 2 + HALF, :]
    value_ref[...] = exact(pair, spread_values(width), ((1,), (0,))).astype(BF16)
    value_columns[:, own_rows] = jnp.transpose(pair)[HD:, :].astype(BF16)
    token = step * BLOCK + lax.broadcasted_iota(jnp.int32, (BLOCK, BLOCK), 1)
    within = lax.broadcasted_iota(jnp.int32, (BLOCK, BLOCK), 0)
    lane_head = half_group((BLOCK, width), heads)
    top[...] = jnp.full_like(top, MASKED)
    total[...] = jnp.zeros_like(total)
    acc[...] = jnp.zeros_like(acc)

    def one_block(block, carried):
        offset = pl.multiple_of(block * BLOCK, BLOCK)
        keys = key_ref[pl.ds(offset, BLOCK), :]
        values = value_columns[:, pl.ds(offset, BLOCK)]
        place = offset + within
        visible = (place >= start) & (place <= token)
        for head in range(heads):
            own_keys = jnp.where(lane_head == head, keys, jnp.zeros_like(keys))
            scores = jnp.where(visible, dot_nt(own_keys, query) * ATTENTION_SCALE, MASKED)
            old = top[head : head + 1, :]
            new = jnp.maximum(old, jnp.max(scores, axis=0, keepdims=True))
            weights = jnp.exp(scores - new)
            fade = jnp.exp(old - new)
            top[head : head + 1, :] = new
            total[head : head + 1, :] = total[head : head + 1, :] * fade + jnp.sum(
                weights, axis=0, keepdims=True
            )
            acc[head * HD : (head + 1) * HD, :] = acc[
                head * HD : (head + 1) * HD, :
            ] * fade + dot_nn(values, weights.astype(BF16))
        return carried

    lax.fori_loop(first_ref[step], step + 1, one_block, 0)
    for head in range(heads):
        acc[head * HD : (head + 1) * HD, :] = (
            acc[head * HD : (head + 1) * HD, :] / total[head : head + 1, :]
        )
    mixed_ref[...] = jnp.transpose(acc[...]).astype(BF16)
    lse_ref[...] = top[...] + jnp.log(total[...])


def attention_forward(first, normed, weight, table, start, heads):
    tokens, model = normed.shape
    width = heads * HD
    by_block = pl.BlockSpec((BLOCK, width), lambda i, first: (i, 0))
    whole = pl.BlockSpec((tokens, width), lambda i, first: (0, 0))
    return pl.pallas_call(
        functools.partial(forward_kernel, heads),
        grid_spec=pltpu.PrefetchScalarGridSpec(
            num_scalar_prefetch=1,
            grid=(tokens // BLOCK,),
            in_specs=[
                pl.BlockSpec((BLOCK, model), lambda i, first: (i, 0)),
                pl.BlockSpec(weight.shape, lambda i, first: (0, 0)),
                pl.BlockSpec((BLOCK, 2 * HALF), lambda i, first: (i, 0)),
                pl.BlockSpec((1, BLOCK), lambda i, first: (0, i)),
            ],
            out_specs=[
                by_block,
                whole,
                pl.BlockSpec((HD, BLOCK), lambda i, first: (0, i)),
                by_block,
                by_block,
                pl.BlockSpec((heads, BLOCK), lambda i, first: (0, i)),
            ],
            scratch_shapes=[
                pltpu.VMEM((HD, tokens), BF16),
                pltpu.VMEM((heads, BLOCK), F32),
                pltpu.VMEM((heads, BLOCK), F32),
                pltpu.VMEM((width, BLOCK), F32),
            ],
        ),
        out_shape=[jax.ShapeDtypeStruct((tokens, width), BF16)] * 2
        + [jax.ShapeDtypeStruct((HD, tokens), BF16)]
        + [jax.ShapeDtypeStruct((tokens, width), BF16)] * 2
        + [jax.ShapeDtypeStruct((heads, tokens), F32)],
        compiler_params=pltpu.CompilerParams(vmem_limit_bytes=VMEM_BYTES),
        cost_estimate=pl.CostEstimate(
            flops=64 * tokens * BLOCK * width, bytes_accessed=8 * tokens * width, transcendentals=0
        ),
        name="attention_forward",
    )(first, normed, weight, table, start)


def backward_kernel(
    heads,
    first_ref,
    query_ref,
    key_ref,
    key_columns_ref,
    value_ref,
    mixed_ref,
    grad_ref,
    weight_ref,
    lse_ref,
    start_ref,
    table_ref,
    out_ref,
    weight_grad_ref,
    dquery,
    dkey,
    dvalue,
    weight_grad,
):
    step = pl.program_id(0)
    query = query_ref[...]
    grad_one = grad_ref[...]
    grad = dot_nt(grad_one, weight_ref[...]).astype(BF16)
    start = start_ref[...]
    width = query.shape[1]
    token = step * BLOCK + lax.broadcasted_iota(jnp.int32, (BLOCK, BLOCK), 1)
    within = lax.broadcasted_iota(jnp.int32, (BLOCK, BLOCK), 0)
    half_head = half_group((BLOCK, width), heads)
    full_head = full_group((BLOCK, width))
    zero = jnp.zeros((BLOCK, width), BF16)
    product = grad.astype(F32) * mixed_ref[...].astype(F32)
    chooser = (
        lax.broadcasted_iota(jnp.int32, (8, width), 0)
        == lax.broadcasted_iota(jnp.int32, (8, width), 1) // HD
    ).astype(F32)
    correction = exact(chooser, product, ((1,), (1,)))

    @pl.when(step == 0)
    def _():
        dkey[...] = jnp.zeros_like(dkey)
        dvalue[...] = jnp.zeros_like(dvalue)
        weight_grad[...] = jnp.zeros_like(weight_grad)

    weight_grad[...] += dot_tn(mixed_ref[...], grad_one)
    dquery[...] = jnp.zeros_like(dquery)

    def one_block(block, carried):
        offset = pl.multiple_of(block * BLOCK, BLOCK)
        rows = pl.ds(offset, BLOCK)
        keys = key_ref[rows, :]
        values = value_ref[rows, :]
        key_columns = key_columns_ref[:, rows]
        place = offset + within
        visible = (place >= start) & (place <= token)
        new_key = dkey[rows, :]
        new_value = dvalue[rows, :]
        for head in range(heads):
            own_keys = jnp.where(half_head == head, keys, zero)
            own_values = jnp.where(full_head == head, values, zero)
            scores = dot_nt(own_keys, query) * ATTENTION_SCALE
            probs = jnp.where(visible, jnp.exp(scores - lse_ref[head : head + 1, :]), 0.0)
            pressure = dot_nt(own_values, grad)
            dscores = (probs * (pressure - correction[head : head + 1, :])).astype(BF16)
            new_value = new_value + dot_nn(
                probs.astype(BF16), jnp.where(full_head == head, grad, zero)
            )
            new_key = new_key + dot_nn(dscores, jnp.where(half_head == head, query, zero))
            term = dot_nn(key_columns, dscores)
            low = slice(head * HALF, (head + 1) * HALF)
            high = slice(width // 2 + head * HALF, width // 2 + (head + 1) * HALF)
            dquery[low, :] += term[:HALF]
            dquery[high, :] += term[HALF:]
        dkey[rows, :] = new_key
        dvalue[rows, :] = new_value
        return carried

    lax.fori_loop(first_ref[step], step + 1, one_block, 0)
    own_rows = pl.ds(pl.multiple_of(step * BLOCK, BLOCK), BLOCK)
    cosine, sine = tables(table_ref[own_rows, :], width)
    out_ref[own_rows, :width] = (
        turn(jnp.transpose(dquery[...]), cosine, -sine) * ATTENTION_SCALE
    ).astype(BF16)

    @pl.when(step == pl.num_programs(0) - 1)
    def _():
        def fold(block, carried):
            rows = pl.ds(pl.multiple_of(block * BLOCK, BLOCK), BLOCK)
            cosine, sine = tables(table_ref[rows, :], width)
            turned = turn(dkey[rows, :], cosine, -sine) * ATTENTION_SCALE
            out_ref[rows, width:] = (
                dot_nt(turned.astype(BF16), spread_keys(width).astype(BF16))
                + dot_nt(dvalue[rows, :].astype(BF16), spread_values(width).astype(BF16))
            ).astype(BF16)
            return carried

        lax.fori_loop(0, pl.num_programs(0), fold, 0)
        weight_grad_ref[...] = weight_grad[...].astype(BF16)


def attention_backward(
    first, query, keys, key_columns, values, mixed, grad, weight, lse, start, table
):
    tokens, width = query.shape
    model = grad.shape[1]
    heads = width // HD
    columns = width + 2 * HD
    by_block = pl.BlockSpec((BLOCK, width), lambda i, first: (i, 0))
    whole = pl.BlockSpec((tokens, width), lambda i, first: (0, 0))
    return pl.pallas_call(
        functools.partial(backward_kernel, heads),
        grid_spec=pltpu.PrefetchScalarGridSpec(
            num_scalar_prefetch=1,
            grid=(tokens // BLOCK,),
            in_specs=[
                by_block,
                whole,
                pl.BlockSpec((HD, tokens), lambda i, first: (0, 0)),
                whole,
                by_block,
                pl.BlockSpec((BLOCK, model), lambda i, first: (i, 0)),
                pl.BlockSpec((width, model), lambda i, first: (0, 0)),
                pl.BlockSpec((heads, BLOCK), lambda i, first: (0, i)),
                pl.BlockSpec((1, BLOCK), lambda i, first: (0, i)),
                pl.BlockSpec((tokens, 2 * HALF), lambda i, first: (0, 0)),
            ],
            out_specs=[
                pl.BlockSpec((tokens, columns), lambda i, first: (0, 0)),
                pl.BlockSpec((width, model), lambda i, first: (0, 0)),
            ],
            scratch_shapes=[
                pltpu.VMEM((width, BLOCK), F32),
                pltpu.VMEM((tokens, width), F32),
                pltpu.VMEM((tokens, width), F32),
                pltpu.VMEM((width, model), F32),
            ],
        ),
        out_shape=[
            jax.ShapeDtypeStruct((tokens, columns), BF16),
            jax.ShapeDtypeStruct((width, model), BF16),
        ],
        compiler_params=pltpu.CompilerParams(vmem_limit_bytes=VMEM_BYTES),
        cost_estimate=pl.CostEstimate(
            flops=0, bytes_accessed=tokens * width, transcendentals=0
        ),
        name="attention_backward",
    )(first, query, keys, key_columns, values, mixed, grad, weight, lse, start, table)


def token_starts(lengths_row, group_tokens):
    count = lengths_row.shape[0]
    order = jnp.arange(count, dtype=jnp.int32)
    finish = jnp.sum(jnp.where(order[None, :] <= order[:, None], lengths_row[None, :], 0), axis=1)
    place = jnp.arange(group_tokens, dtype=jnp.int32)
    passed = place[:, None] >= finish[None, :]
    return jnp.max(jnp.where(passed, finish[None, :], 0), axis=1), place


def inverse_norm(values):
    return lax.rsqrt(jnp.mean(values * values, axis=1, keepdims=True) + EPSILON)


def after(value, *earlier):
    return lax.optimization_barrier((value, *earlier))[0]


def sum_over_groups(value):
    return lax.psum_scatter(value, "dp", scatter_dimension=0, tiled=True)


def gather_groups(value):
    return lax.all_gather(value, "dp", axis=0, tiled=True)


def body(
    tokens,
    cotangent,
    query_weight,
    key_weight,
    value_weight,
    output_weight,
    gate_weight,
    up_weight,
    down_weight,
    attention_gain,
    feedforward_gain,
    lengths,
):
    members = lax.axis_size("fsdp")
    groups = lax.axis_size("dp")
    rows, model = tokens.shape
    group_tokens = rows * members
    shard = query_weight.shape[0]
    heads = NH // members
    width = heads * HD
    columns = width + 2 * HD
    copies = members // KVH
    out_columns = model // members
    down_rows = down_weight.shape[0]
    units = groups * down_rows // CHUNKS
    gain_one = attention_gain.astype(F32)[:, None]
    gain_two = feedforward_gain.astype(F32)[:, None]
    member = lax.axis_index("fsdp").astype(jnp.int32)[None]

    scaled_query = (query_weight * gain_one).astype(BF16)
    scaled_key = (key_weight * gain_one).astype(BF16)
    scaled_value = (value_weight * gain_one).astype(BF16)
    packed_in = jnp.concatenate(
        [
            scaled_query.reshape(shard, members, heads, 2, HALF)
            .transpose(1, 0, 3, 2, 4)
            .reshape(members, shard, width),
            jnp.repeat(
                scaled_key.reshape(shard, KVH, HD).transpose(1, 0, 2), copies, axis=0
            ),
            jnp.repeat(
                scaled_value.reshape(shard, KVH, HD).transpose(1, 0, 2), copies, axis=0
            ),
            output_weight.reshape(shard, members, out_columns).transpose(1, 0, 2),
        ],
        axis=2,
    )
    [packed_in] = plane_swap([packed_in], members, 1)
    packed_in = packed_in.reshape(members * shard, columns + out_columns)
    inputs = tokens.astype(F32)
    inverse_one = inverse_norm(inputs)
    early = model // 4
    down_early = gather_groups(down_weight[:, :early])
    normed_one = plane_gather(
        after((inputs * inverse_one).astype(BF16), packed_in, down_early), members, 0, True
    )
    packed = gather_groups(packed_in)
    upstream = cotangent.astype(F32)
    down_rest = gather_groups(after(down_weight[:, early:], normed_one))
    gate_up = exchanged(
        units_apart(
            member,
            after(gate_weight, normed_one),
            up_weight,
            gain_two,
            members,
            groups,
            CHUNKS,
        )
    )

    start, place = token_starts(lengths[0], group_tokens)
    first = start[::BLOCK] // BLOCK
    frequency = ROPE_BASE ** (-(2.0 * jnp.arange(HALF, dtype=F32)) / HD)
    angles = (place - start).astype(F32)[:, None] * frequency[None, :]
    table = jnp.concatenate([jnp.cos(angles), jnp.sin(angles)], axis=1)
    start = start[None, :]

    out_blocks = exchanged(rows_apart(member, packed, members, columns))
    query, keys, key_columns, values, mixed, lse = attention_forward(
        first, normed_one, packed, table, start, heads
    )
    mixed_then, out_blocks, gate_up = lax.optimization_barrier((mixed, out_blocks, gate_up))
    gate_up_chunks = [
        gather_groups(part) for part in rows_together(member, gate_up, CHUNKS)
    ]
    out_piece = columns_together(member, out_blocks)
    branch_one = product_scatter([mixed_then], [out_piece], False, members, 2, True)
    residual = inputs + RESIDUAL_SCALE * branch_one

    inverse_two = inverse_norm(residual)
    normed_two, down_rest = lax.optimization_barrier(
        ((residual * inverse_two).astype(BF16), down_rest)
    )
    normed_two = plane_gather(normed_two, members, 3, False)
    grad_two = plane_gather(
        after((RESIDUAL_SCALE * upstream).astype(BF16), normed_two), members, 9, False
    )
    down_all = jnp.concatenate([down_early, after(down_rest, grad_two)], axis=1)
    fused = group_tokens <= 2048
    hiddens = []
    grad_boths = []
    gate_up_grads = []
    for chunk in range(CHUNKS):
        both_weight = gate_up_chunks[chunk]
        hidden, grad_both = hidden_units(normed_two, grad_two, both_weight, down_all, chunk)
        hiddens.append(hidden)
        grad_boths.append(grad_both)
        if chunk < CHUNKS - 1 or not fused:
            gate_up_grad = dot_tn(normed_two, grad_both).astype(BF16)
            gate_up_grads.append(sum_over_groups(gate_up_grad))
            normed_two, grad_two, hiddens, grad_boths, _ = lax.optimization_barrier(
                (normed_two, grad_two, hiddens, grad_boths, gate_up_grad)
            )
    if fused:
        weighted_two, gate_up_grad = product_scatter(
            grad_boths, gate_up_chunks, True, members, 4, False, normed_two
        )
        gate_up_grads.append(sum_over_groups(gate_up_grad))
    else:
        weighted_two = product_scatter(grad_boths, gate_up_chunks, True, members, 4, False)
    grad_residual = (
        upstream
        + inverse_two * weighted_two
        - residual * inverse_two**3 * jnp.mean(weighted_two * residual, axis=1, keepdims=True)
    )
    gain_term_two = jnp.sum(weighted_two * residual * inverse_two, axis=0)

    grad_one, gate_up_grads[0] = lax.optimization_barrier(
        ((RESIDUAL_SCALE * grad_residual).astype(BF16), gate_up_grads[0])
    )
    grad_one, down_grad, out_sibling, out_own = plane_gather(
        grad_one, members, 5, True, (hiddens, grad_two, down_all)
    )
    down_grad = sum_over_groups(down_grad)
    half_rows = group_tokens // 2
    out_sibling = send_to(out_sibling, members, lambda m: m ^ 1)
    gate_up_grads[0] = exchanged(rows_apart(member, gate_up_grads[0], members))
    grad_one, out_own, out_sibling = lax.optimization_barrier(
        (grad_one, out_own, out_sibling)
    )
    steps = len(plane_masks(members))
    half_rows //= 2
    out_sent = send_to(
        added(out_own[half_rows:], out_sibling[half_rows:]).astype(BF16),
        members,
        hopped(steps - 1, members),
    )
    out_kept = added(out_own[:half_rows], out_sibling[:half_rows]).astype(BF16)
    grad_projected, out_grad = attention_backward(
        first, query, keys, key_columns, values, mixed, grad_one, out_piece, lse, start, table
    )
    out_grad = lax.all_to_all(out_grad, "fsdp", split_axis=1, concat_axis=0, tiled=True)
    packed_grad = jnp.concatenate(
        [dot_tn(normed_one, grad_projected).astype(BF16), out_grad], axis=1
    )
    gate_up_grads[1:] = [
        exchanged(rows_apart(member, part, members))
        for part in after(gate_up_grads[1:], grad_projected)
    ]
    grad_projected, packed_grad, gate_up_grads[0], out_sent, out_kept = lax.optimization_barrier(
        (grad_projected, packed_grad, gate_up_grads[0], out_sent, out_kept)
    )
    for step in reversed(range(steps - 1)):
        half_rows //= 2
        out_next = added(out_kept[half_rows:], out_sent[half_rows:]).astype(BF16)
        out_kept = added(out_kept[:half_rows], out_sent[:half_rows])
        if step:
            out_kept = out_kept.astype(BF16)
        out_sent = send_to(out_next, members, hopped(step, members))
    packed_grad = sum_over_groups(packed_grad)
    weighted_one = product_scatter([grad_projected], [packed], True, members, 6, True, weight=1)
    weighted_one, down_grad = lax.optimization_barrier((weighted_one, down_grad))
    grad_inputs = (
        grad_residual
        + inverse_one * weighted_one
        - inputs * inverse_one**3 * jnp.mean(weighted_one * inputs, axis=1, keepdims=True)
    )
    gain_term_one = jnp.sum(weighted_one * inputs * inverse_one, axis=0)

    gains = jnp.stack(
        [
            gain_term_one.reshape(groups, members, shard),
            gain_term_two.reshape(groups, members, shard),
        ],
        axis=2,
    ).reshape(groups, members, 2 * shard)
    gains = jnp.pad(
        gains.transpose(1, 0, 2), ((0, 0), (0, (-groups) % 8), (0, (-2 * shard) % 128))
    )
    output = (residual + RESIDUAL_SCALE * added(out_kept, out_sent)).astype(BF16)

    gate_grad, up_grad = units_together(
        member, after(gate_up_grads, weighted_one), gain_two, members, groups
    )
    arrived, gains = finale(packed_grad, gains, groups, 8)
    query_grad, key_grad, value_grad, out_grad = heads_together(member, arrived, gain_one, heads)
    gains = lax.dynamic_slice_in_dim(gains, lax.axis_index("dp"), 1, 0)[0, : 2 * shard]
    gains = gains.reshape(2, shard)
    return (
        output,
        grad_inputs.astype(BF16),
        query_grad,
        key_grad,
        value_grad,
        out_grad,
        gate_grad,
        up_grad,
        down_grad.astype(F32),
        gains[0] / gain_one[:, 0],
        gains[1] / gain_two[:, 0],
    )


def solution(mesh):
    by_rows = P(("dp", "fsdp"), None)
    by_entries = P(("dp", "fsdp"))
    return jax.shard_map(
        body,
        mesh=mesh,
        in_specs=(by_rows,) * 9 + (by_entries,) * 2 + (P("dp", None),),
        out_specs=(by_rows,) * 9 + (by_entries,) * 2,
        check_vma=False,
    )
```

```python
import functools

import jax
import jax.numpy as jnp
from jax import lax
from jax.experimental import pallas as pl
from jax.experimental.pallas import tpu as pltpu
from jax.sharding import PartitionSpec as P

NH = 32
KVH = 8
HD = 64
HALF = HD // 2

EPSILON = 1e-05
RESIDUAL_SCALE = 0.22
ATTENTION_SCALE = 0.015625
ROPE_BASE = 10000000.0
MASKED = -1e30
BLOCK = 256
CHUNKS = 2
PIECES = 4
SCATTER_PIECES = 8
VMEM_BYTES = 58 * 1024 * 1024
MESH = pl.DeviceIdType.MESH
BF16 = jnp.bfloat16
F32 = jnp.float32


def dot_nn(left, right):
    return jnp.dot(left, right, preferred_element_type=F32)


def dot_nt(left, right):
    return lax.dot_general(left, right, (((1,), (1,)), ((), ())), preferred_element_type=F32)


def dot_tn(left, right):
    return lax.dot_general(left, right, (((0,), (0,)), ((), ())), preferred_element_type=F32)


def flip(index, mask):
    return index + mask * (1 - 2 * ((index // mask) % 2))


def plane_masks(member_count):
    masks = []
    mask = 2
    while mask < member_count:
        masks.append(mask)
        mask *= 2
    return masks


def hop(index, step, masks):
    core = index % 2
    return (1 - core) * flip(index, masks[step]) + core * flip(index, masks[-1 - step])


def walk(index, subset, masks):
    for step in range(len(masks)):
        if (subset >> step) & 1:
            index = hop(index, step, masks)
    return index


def greet(group, member, masks):
    barrier = pltpu.get_barrier_semaphore()
    partners = [hop(member, step, masks) for step in range(len(masks))] + [flip(member, 1)]
    for partner in partners:
        pl.semaphore_signal(barrier, inc=1, device_id=(group, partner), device_id_type=MESH)
    pl.semaphore_wait(barrier, len(partners))


def gather_kernel(member_count, in_order, count, own_ref, *refs):
    operands = refs[: count + 2] if count else ()
    refs = refs[len(operands) :]
    extra = 4 if count else 1
    all_ref, results, refs = refs[0], refs[1:extra], refs[extra:]
    link_send, link_recv, core_send, core_recv, local_sem = refs[:5]
    group = lax.axis_index("dp")
    member = lax.axis_index("fsdp")
    masks = plane_masks(member_count)
    steps = len(masks)
    rows = own_ref.shape[0]
    piece = rows // PIECES
    greet(group, member, masks)

    blocks = 1 << steps

    def place(owner, subset, side, part):
        block = walk(owner, subset, masks) if in_order else subset + side * blocks
        return all_ref.at[pl.ds(pl.multiple_of(block * rows + part * piece, piece), piece)]

    def link_copy(step, subset, part):
        number = (1 << step) - 1 + subset
        here = place(member, subset, 0, part)
        there = here if in_order else place(member, subset | (1 << step), 0, part)
        return pltpu.make_async_remote_copy(
            own_ref.at[pl.ds(part * piece, piece)] if subset == 0 else here,
            there,
            link_send.at[number, part],
            link_recv.at[number, part],
            device_id=(group, hop(member, step, masks)),
            device_id_type=MESH,
        )

    def core_copy(subset, part):
        here = place(member, subset, 0, part)
        there = here if in_order else place(member, subset, 1, part)
        return pltpu.make_async_remote_copy(
            own_ref.at[pl.ds(part * piece, piece)] if subset == 0 else here,
            there,
            core_send.at[subset, part],
            core_recv.at[subset, part],
            device_id=(group, flip(member, 1)),
            device_id_type=MESH,
        )

    for part in range(PIECES):
        for step in range(steps):
            link_copy(step, 0, part).start()
    first = pl.multiple_of(member * rows, rows) if in_order else 0
    keep = pltpu.make_async_copy(own_ref, all_ref.at[pl.ds(first, rows)], local_sem)
    keep.start()
    for part in range(PIECES):
        core_copy(0, part).start()
    tiles = []
    if count:
        hidden, gradient, down, down_grad, out_sibling, out_own, turned, out_arrived = refs[5:13]
        load_sem, store_sem, out_send, out_recv = refs[13:]
        units = operands[0].shape[1]
        targets = [hidden.at[:, pl.ds(number * units, units)] for number in range(count)]
        loads = [
            pltpu.make_async_copy(source, target, load_sem.at[number])
            for number, (source, target) in enumerate(zip(operands, (*targets, gradient, down)))
        ]
        half = out_own.shape[0]
        finished = (
            down_grad,
            out_own.at[pl.ds(half // 2, half // 2)],
            out_own.at[pl.ds(0, half // 2)],
        )
        stores = [
            pltpu.make_async_copy(source, target, store_sem.at[number])
            for number, (source, target) in enumerate(zip(finished, results))
        ]
        for load in loads:
            load.start()
        width = 256

        def out_copy(column):
            where = pl.ds(column, width)
            return pltpu.make_async_remote_copy(
                out_sibling.at[:, where],
                out_arrived.at[:, where],
                out_send.at[column // width],
                out_recv.at[column // width],
                device_id=(group, flip(member, 1)),
                device_id_type=MESH,
            )

        def sibling_tile(column):
            out_sibling[:, column : column + width] = dot_nn(
                hidden[half:, :], down[:, column : column + width]
            ).astype(BF16)
            out_copy(column).start()

        def own_tile(column):
            product = dot_nn(hidden[:half, :], down[:, column : column + width])
            out_copy(column).wait()
            out_own[:, column : column + width] = (
                product + out_arrived[:, column : column + width].astype(F32)
            ).astype(BF16)

        def turn_tile(number):
            part = slice(number * units, (number + 1) * units)
            turned[part, :] = jnp.transpose(hidden[:, part])

        def grad_tile(column):
            down_grad[:, column : column + width] = dot_nn(
                turned[...], gradient[:, column : column + width]
            ).astype(BF16)

        for load in loads[:count] + loads[count + 1 :]:
            tiles.append(load.wait)
        starts = range(0, down.shape[1], width)
        for column in starts:
            tiles.append(functools.partial(sibling_tile, column))
        for column in starts:
            tiles.append(functools.partial(own_tile, column))
        tiles += [stores[1].start, stores[2].start]
        tiles.append(loads[count].wait)
        for number in range(count):
            tiles.append(functools.partial(turn_tile, number))
        for column in starts:
            tiles.append(functools.partial(grad_tile, column))
        tiles.append(stores[0].start)
    shares = [4] * PIECES + [2, 1, 0, 0] * max(1, steps - 1)
    shares = shares[: steps * PIECES]
    ends = [-(-len(tiles) * sum(shares[: n + 1]) // sum(shares)) for n in range(len(shares))]

    turn = 0
    for step in range(steps):
        for part in range(PIECES):
            for subset in range(1 << step):
                link_copy(step, subset, part).wait_recv()
                arrived = subset | (1 << step)
                for later in range(step + 1, steps):
                    link_copy(later, arrived, part).start()
                core_copy(arrived, part).start()
            for run in tiles[ends[turn - 1] if turn else 0 : ends[turn]]:
                run()
            turn += 1
    for part in range(PIECES):
        for subset in range(1 << steps):
            core_copy(subset, part).wait()
    for part in range(PIECES):
        for step in range(steps):
            for subset in range(1 << step):
                link_copy(step, subset, part).wait_send()
    keep.wait()
    if count:
        for store in stores:
            store.wait()


def plane_gather(own, member_count, collective_id, in_order, extras=None):
    rows, width = own.shape
    steps = len(plane_masks(member_count))
    blocks = 1 << steps
    total = member_count * rows
    any_space = pl.BlockSpec(memory_space=pl.ANY)
    scratch = [
        pltpu.SemaphoreType.DMA((blocks - 1, PIECES)),
        pltpu.SemaphoreType.DMA((blocks - 1, PIECES)),
        pltpu.SemaphoreType.DMA((blocks, PIECES)),
        pltpu.SemaphoreType.DMA((blocks, PIECES)),
        pltpu.SemaphoreType.DMA,
    ]
    operands = [own]
    out_shape = [jax.ShapeDtypeStruct((total, width), own.dtype)]
    count = 0
    if extras:
        hiddens, gradient, down = extras
        count = len(hiddens)
        operands += [*hiddens, gradient, down]
        units = down.shape[0]
        scratch += [
            pltpu.VMEM((total, units), BF16),
            pltpu.VMEM(gradient.shape, BF16),
            pltpu.VMEM(down.shape, BF16),
        ]
        out_shape += [
            jax.ShapeDtypeStruct((down.shape[0], gradient.shape[1]), BF16),
            jax.ShapeDtypeStruct((total // 4, down.shape[1]), BF16),
            jax.ShapeDtypeStruct((total // 4, down.shape[1]), BF16),
        ]
        out_half = pltpu.VMEM((total // 2, down.shape[1]), BF16)
        scratch += [
            pltpu.VMEM(out_shape[1].shape, BF16),
            out_half,
            out_half,
            pltpu.VMEM((units, total), BF16),
            out_half,
            pltpu.SemaphoreType.DMA((count + 2,)),
            pltpu.SemaphoreType.DMA((3,)),
            pltpu.SemaphoreType.DMA((down.shape[1] // 256,)),
            pltpu.SemaphoreType.DMA((down.shape[1] // 256,)),
        ]
    result = pl.pallas_call(
        functools.partial(gather_kernel, member_count, in_order, count),
        out_shape=out_shape,
        in_specs=[any_space] * len(operands),
        out_specs=[any_space] * len(out_shape),
        scratch_shapes=scratch,
        compiler_params=pltpu.CompilerParams(
            collective_id=collective_id, has_side_effects=True, vmem_limit_bytes=VMEM_BYTES
        ),
        cost_estimate=pl.CostEstimate(
            flops=0, bytes_accessed=(1 if extras else 60) * total * width, transcendentals=0
        ),
        name="plane_gather",
    )(*operands)
    return result if extras else result[0]


def swap_kernel(member_count, count, *refs):
    sources, targets = refs[:count], refs[count : 2 * count]
    send_sem, recv_sem, local_sem = refs[2 * count :]
    group = lax.axis_index("dp")
    member = lax.axis_index("fsdp")
    barrier = pltpu.get_barrier_semaphore()
    for away in range(1, member_count):
        pl.semaphore_signal(
            barrier,
            inc=1,
            device_id=(group, (member + away) % member_count),
            device_id_type=MESH,
        )
    pl.semaphore_wait(barrier, member_count - 1)

    def copy(number, away):
        target = (member + away) % member_count
        return pltpu.make_async_remote_copy(
            sources[number].at[target],
            targets[number].at[member],
            send_sem.at[number, away],
            recv_sem.at[number, away],
            device_id=(group, target),
            device_id_type=MESH,
        )

    def keep(number):
        return pltpu.make_async_copy(
            sources[number].at[member], targets[number].at[member], local_sem.at[number]
        )

    for number in range(count):
        for away in range(1, member_count):
            copy(number, away).start()
        keep(number).start()
    for number in range(count):
        for away in range(1, member_count):
            copy(number, away).wait()
        keep(number).wait()


def plane_swap(values, member_count, collective_id):
    count = len(values)
    any_space = pl.BlockSpec(memory_space=pl.ANY)
    return pl.pallas_call(
        functools.partial(swap_kernel, member_count, count),
        out_shape=[jax.ShapeDtypeStruct(value.shape, value.dtype) for value in values],
        in_specs=[any_space] * count,
        out_specs=[any_space] * count,
        scratch_shapes=[
            pltpu.SemaphoreType.DMA((count, member_count)),
            pltpu.SemaphoreType.DMA((count, member_count)),
            pltpu.SemaphoreType.DMA((count,)),
        ],
        compiler_params=pltpu.CompilerParams(collective_id=collective_id, has_side_effects=True),
        cost_estimate=pl.CostEstimate(
            flops=0,
            bytes_accessed=60 * sum(value.size for value in values),
            transcendentals=0,
        ),
        name="plane_swap",
    )(*values)


def product_scatter_kernel(member_count, in_order, transposed, count, rows, with_grad, *refs):
    if with_grad:
        other_ref, grad_ref = refs[0], refs[2 * count + 2]
        held_other, held_grad, other_sem, grad_sem = refs[-4:]
        refs = refs[1 : 2 * count + 2] + refs[2 * count + 3 : -4]
    lefts, rights, sum_ref = refs[:count], refs[count : 2 * count], refs[2 * count]
    held_left, held_right = refs[2 * count + 1 : 2 * count + 3]
    depths = [left.shape[1] for left in lefts]
    offsets = [sum(depths[:number]) for number in range(count)]
    (
        outgoing,
        core_buffer,
        held,
        link_buffer,
        left_sem,
        right_sem,
        link_send,
        link_recv,
        core_send,
        core_recv,
    ) = refs[2 * count + 3 :]
    group = lax.axis_index("dp")
    member = lax.axis_index("fsdp")
    sibling = flip(member, 1)
    masks = plane_masks(member_count)
    steps = len(masks)
    blocks = 1 << steps
    pieces = SCATTER_PIECES
    piece = sum_ref.shape[1] // pieces

    def left_copy(number, side, subset):
        owner = sibling if side else member
        block = walk(owner, subset, masks) if in_order else subset + side * blocks
        return pltpu.make_async_copy(
            lefts[number].at[pl.ds(pl.multiple_of(block * rows, rows), rows)],
            held_left.at[
                pl.ds((side * blocks + subset) * rows, rows), pl.ds(offsets[number], depths[number])
            ],
            left_sem.at[number, side, subset],
        )

    def right_copy(number, index):
        where = pl.ds(pl.multiple_of(index * piece, piece), piece)
        source, there = rights[number], pl.ds(offsets[number], depths[number])
        if transposed:
            return pltpu.make_async_copy(
                source.at[where, pl.ds(0, depths[number])],
                held_right.at[where, there],
                right_sem.at[number, index],
            )
        return pltpu.make_async_copy(
            source.at[:, where], held_right.at[there, where], right_sem.at[number, index]
        )

    def load_side(side):
        for number in range(count):
            for subset in range(blocks):
                left_copy(number, side, subset).start()

    def wait_side(side):
        for number in range(count):
            for subset in range(blocks):
                left_copy(number, side, subset).wait()

    def load_right(index):
        for number in range(count):
            right_copy(number, index).start()

    load_side(1)
    load_right(0)
    greet(group, member, masks)

    def part(side, subset, where):
        left = held_left[pl.ds((side * blocks + subset) * rows, rows), :]
        if transposed:
            return dot_nt(left, held_right[where, :])
        return dot_nn(left, held_right[:, where])

    def columns(index):
        return pl.ds(pl.multiple_of(index * piece, piece), piece)

    def core_copy(index):
        return pltpu.make_async_remote_copy(
            outgoing.at[:, columns(index)],
            core_buffer.at[:, columns(index)],
            core_send.at[index],
            core_recv.at[index],
            device_id=(group, sibling),
            device_id_type=MESH,
        )

    def slot(step, kept):
        return sum(blocks >> (s + 1) for s in range(step)) + (kept >> (step + 1))

    def link_copy(step, subset, index):
        number = slot(step, subset & ~(1 << step))
        return pltpu.make_async_remote_copy(
            held.at[pl.ds(subset * rows, rows), columns(index)],
            link_buffer.at[pl.ds(number * rows, rows), columns(index)],
            link_send.at[number, index],
            link_recv.at[number, index],
            device_id=(group, hop(member, step, masks)),
            device_id_type=MESH,
        )

    order = sorted(range(blocks), key=lambda s: (-(s & 1), -s))

    def for_sibling(index):
        where = columns(index)
        for number in range(count):
            right_copy(number, index).wait()
        pl.when(index + 1 < pieces)(lambda: load_right(index + 1))
        for subset in range(blocks):
            outgoing[pl.ds(subset * rows, rows), where] = part(1, subset, where).astype(BF16)
        core_copy(index).start()

    def for_links(index):
        where = columns(index)
        core_copy(index).wait_recv()
        for subset in order:
            where_rows = pl.ds(subset * rows, rows)
            total = part(0, subset, where) + core_buffer[where_rows, where].astype(F32)
            if subset == 0:
                sum_ref[:, where] = total
            else:
                held[where_rows, where] = total.astype(BF16)
            if subset & 1:
                link_copy(0, subset, index).start()

    def for_both(index, carried):
        for_sibling(index)
        for_links(index - 1)
        return carried

    wait_side(1)
    load_side(0)
    for_sibling(0)
    wait_side(0)
    if with_grad:
        other_copy = pltpu.make_async_copy(other_ref, held_other, other_sem)
        other_copy.start()
    lax.fori_loop(1, pieces, for_both, 0)
    for_links(pieces - 1)
    if with_grad:
        other_copy.wait()
        units = held_grad.shape[1] // pieces
        late = 3 if steps > 1 else 0

    def grad_tile(index):
        where = pl.ds(pl.multiple_of(index * units, units), units)
        turned = dot_tn(
            held_left[:, pl.ds(pl.multiple_of(offsets[-1] + index * units, units), units)],
            held_other[...],
        )
        held_grad[:, where] = jnp.transpose(turned.astype(BF16))

    for step in range(steps):

        def one_step(index, carried, step=step):
            where = columns(index)
            if with_grad and step == 0:
                pl.when(index >= late)(lambda: grad_tile(index - late))
            if with_grad and step == 1:
                pl.when(index < late)(lambda: grad_tile(pieces - late + index))
            for kept in sorted(range(0, blocks, 2 << step), reverse=True):
                link_copy(step, kept | (1 << step), index).wait_recv()
                arrived = link_buffer[pl.ds(slot(step, kept) * rows, rows), where].astype(F32)
                if kept == 0:
                    sum_ref[:, where] += arrived
                else:
                    where_rows = pl.ds(kept * rows, rows)
                    held[where_rows, where] = (
                        held[where_rows, where].astype(F32) + arrived
                    ).astype(BF16)
                if (kept >> (step + 1)) & 1:
                    link_copy(step + 1, kept, index).start()
            return carried

        lax.fori_loop(0, pieces, one_step, 0)
        if with_grad and step == min(1, steps - 1):
            grad_copy = pltpu.make_async_copy(held_grad, grad_ref, grad_sem)
            grad_copy.start()

    def finish(index, carried):
        core_copy(index).wait_send()
        for step in range(steps):
            for kept in range(0, blocks, 2 << step):
                link_copy(step, kept | (1 << step), index).wait_send()
        return carried

    lax.fori_loop(0, pieces, finish, 0)
    if with_grad:
        grad_copy.wait()


def product_scatter(
    lefts, rights, transposed, member_count, collective_id, in_order, other=None, weight=60
):
    count = len(lefts)
    total = lefts[0].shape[0]
    width = rights[0].shape[0 if transposed else 1]
    rows = total // member_count
    blocks = 1 << len(plane_masks(member_count))
    depth = sum(left.shape[1] for left in lefts)
    scratch = (
        [
            pltpu.VMEM((total, depth), BF16),
            pltpu.VMEM((width, depth) if transposed else (depth, width), BF16),
        ]
        + [
            pltpu.VMEM((blocks * rows, width), BF16),
            pltpu.VMEM((blocks * rows, width), BF16),
            pltpu.VMEM((blocks * rows, width), BF16),
            pltpu.VMEM(((blocks - 1) * rows, width), BF16),
            pltpu.SemaphoreType.DMA((count, 2, blocks)),
            pltpu.SemaphoreType.DMA((count, SCATTER_PIECES)),
            pltpu.SemaphoreType.DMA((blocks - 1, SCATTER_PIECES)),
            pltpu.SemaphoreType.DMA((blocks - 1, SCATTER_PIECES)),
            pltpu.SemaphoreType.DMA((SCATTER_PIECES,)),
            pltpu.SemaphoreType.DMA((SCATTER_PIECES,)),
        ]
    )
    any_space = pl.BlockSpec(memory_space=pl.ANY)
    in_vmem = pl.BlockSpec(memory_space=pltpu.VMEM)
    operands = [*lefts, *rights]
    out_shape = [jax.ShapeDtypeStruct((rows, width), F32)]
    if other is not None:
        operands = [other] + operands
        grad_shape = (other.shape[1], lefts[-1].shape[1])
        out_shape.append(jax.ShapeDtypeStruct(grad_shape, BF16))
        scratch += [
            pltpu.VMEM(other.shape, BF16),
            pltpu.VMEM(grad_shape, BF16),
            pltpu.SemaphoreType.DMA,
            pltpu.SemaphoreType.DMA,
        ]
    result = pl.pallas_call(
        functools.partial(
            product_scatter_kernel,
            member_count,
            in_order,
            transposed,
            count,
            rows,
            other is not None,
        ),
        out_shape=out_shape,
        in_specs=[any_space] * len(operands),
        out_specs=[in_vmem] + [any_space] * (len(out_shape) - 1),
        scratch_shapes=scratch,
        compiler_params=pltpu.CompilerParams(
            collective_id=collective_id, has_side_effects=True, vmem_limit_bytes=VMEM_BYTES
        ),
        cost_estimate=pl.CostEstimate(
            flops=0, bytes_accessed=weight * total * width, transcendentals=0
        ),
        name="product_scatter",
    )(*operands)
    return result[0] if other is None else result


def finale_kernel(member_count, group_count, packed_ref, part_ref, arrived, sum_ref, *refs):
    near, held, far = refs[:3]
    packed_send, packed_recv, own_sem, near_send, near_recv, far_send, far_recv = refs[3:]
    group = lax.axis_index("dp")
    member = lax.axis_index("fsdp")
    shard = arrived.shape[1]
    barrier = pltpu.get_barrier_semaphore()
    for away in range(1, member_count):
        pl.semaphore_signal(
            barrier,
            inc=1,
            device_id=(group, (member + away) % member_count),
            device_id_type=MESH,
        )
    for away in range(1, group_count):
        pl.semaphore_signal(
            barrier, inc=1, device_id=((group + away) % group_count, member), device_id_type=MESH
        )
    pl.semaphore_wait(barrier, member_count + group_count - 2)

    def rows_of(target):
        return packed_ref.at[pl.ds(pl.multiple_of(target * shard, shard), shard)]

    def packed_copy(away):
        target = (member + away) % member_count
        return pltpu.make_async_remote_copy(
            rows_of(target),
            arrived.at[away],
            packed_send.at[away],
            packed_recv.at[away],
            device_id=(group, target),
            device_id_type=MESH,
        )

    def near_copy(away):
        target = (member + away) % member_count
        return pltpu.make_async_remote_copy(
            part_ref.at[target],
            near.at[away],
            near_send.at[away],
            near_recv.at[away],
            device_id=(group, target),
            device_id_type=MESH,
        )

    def far_copy(away):
        return pltpu.make_async_remote_copy(
            held,
            far.at[away],
            far_send.at[away],
            far_recv.at[away],
            device_id=((group + away) % group_count, member),
            device_id_type=MESH,
        )

    own_copy = pltpu.make_async_copy(rows_of(member), arrived.at[0], own_sem)
    for away in range(1, member_count):
        near_copy(away).start()
    for away in range(1, member_count):
        packed_copy(away).start()
    own_copy.start()
    total = part_ref[member]
    for away in range(1, member_count):
        near_copy(away).wait_recv()
        total = total + near[away]
    held[...] = total
    for away in range(1, group_count):
        far_copy(away).start()

    for away in range(1, member_count):
        packed_copy(away).wait_recv()
    own_copy.wait()
    for away in range(1, group_count):
        far_copy(away).wait_recv()
        total = total + far[away]
    sum_ref[...] = total
    for away in range(1, member_count):
        near_copy(away).wait_send()
        packed_copy(away).wait_send()
    for away in range(1, group_count):
        far_copy(away).wait_send()


def finale(packed, parts, group_count, collective_id):
    member_count, lines, lanes = parts.shape
    shard = packed.shape[0] // member_count
    in_vmem = pl.BlockSpec(memory_space=pltpu.VMEM)
    any_space = pl.BlockSpec(memory_space=pl.ANY)
    members_dma = pltpu.SemaphoreType.DMA((member_count,))
    groups_dma = pltpu.SemaphoreType.DMA((group_count,))
    return pl.pallas_call(
        functools.partial(finale_kernel, member_count, group_count),
        out_shape=[
            jax.ShapeDtypeStruct((member_count, shard, packed.shape[1]), BF16),
            jax.ShapeDtypeStruct((lines, lanes), F32),
        ],
        in_specs=[any_space, in_vmem],
        out_specs=[any_space, in_vmem],
        scratch_shapes=[
            pltpu.VMEM((member_count, lines, lanes), F32),
            pltpu.VMEM((lines, lanes), F32),
            pltpu.VMEM((group_count, lines, lanes), F32),
            members_dma,
            members_dma,
            pltpu.SemaphoreType.DMA,
            members_dma,
            members_dma,
            groups_dma,
            groups_dma,
        ],
        compiler_params=pltpu.CompilerParams(collective_id=collective_id, has_side_effects=True),
        cost_estimate=pl.CostEstimate(flops=0, bytes_accessed=40000000, transcendentals=0),
        name="finale",
    )(packed, parts)


def local_call(kernel, name, out_shape, *operands):
    in_vmem = pl.BlockSpec(memory_space=pltpu.VMEM)
    size = sum(value.size * value.dtype.itemsize for value in operands[1:])
    size += sum(value.size * value.dtype.itemsize for value in out_shape)
    return pl.pallas_call(
        kernel,
        grid_spec=pltpu.PrefetchScalarGridSpec(
            num_scalar_prefetch=1,
            in_specs=[in_vmem] * (len(operands) - 1),
            out_specs=[in_vmem] * len(out_shape),
            grid=(),
        ),
        out_shape=out_shape,
        compiler_params=pltpu.CompilerParams(vmem_limit_bytes=VMEM_BYTES),
        cost_estimate=pl.CostEstimate(flops=0, bytes_accessed=size, transcendentals=0),
        name=name,
    )(*operands)


def rows_apart(member, value, member_count, column=0):
    rows = value.shape[0] // member_count

    def kernel(member_ref, value_ref, *out_refs):
        for away, out_ref in enumerate(out_refs):
            other = member_ref[0] ^ away
            out_ref[...] = value_ref[pl.ds(pl.multiple_of(other * rows, rows), rows), column:]

    shape = jax.ShapeDtypeStruct((rows, value.shape[1] - column), value.dtype)
    return local_call(kernel, "rows_apart", [shape] * member_count, member, value)


def rows_together(member, blocks, chunks):
    rows, width = blocks[0].shape
    part = width // chunks
    count = len(blocks)

    def kernel(member_ref, *refs):
        for away in range(count):
            where = pl.ds(pl.multiple_of((member_ref[0] ^ away) * rows, rows), rows)
            for chunk in range(chunks):
                refs[count + chunk][where, :] = refs[away][:, chunk * part : (chunk + 1) * part]

    shape = jax.ShapeDtypeStruct((count * rows, part), blocks[0].dtype)
    return local_call(kernel, "rows_together", [shape] * chunks, member, *blocks)


def columns_together(member, blocks):
    rows, width = blocks[0].shape
    count = len(blocks)

    def kernel(member_ref, *refs):
        for away in range(count):
            where = pl.ds(pl.multiple_of((member_ref[0] ^ away) * width, width), width)
            refs[count][:, where] = refs[away][...]

    shape = jax.ShapeDtypeStruct((rows, count * width), blocks[0].dtype)
    return local_call(kernel, "columns_together", [shape], member, *blocks)[0]


def exchanged(blocks):
    return [blocks[0]] + [
        lax.ppermute(blocks[away], "fsdp", [(m, m ^ away) for m in range(len(blocks))])
        for away in range(1, len(blocks))
    ]


def added(left, right):
    return left.astype(F32) + right.astype(F32)


def send_to(value, member_count, partner):
    return lax.ppermute(value, "fsdp", [(m, partner(m)) for m in range(member_count)])


def hopped(step, member_count):
    masks = plane_masks(member_count)
    return lambda m: (m ^ masks[step]) if m % 2 == 0 else (m ^ masks[-1 - step])


def unit_strips(member_count, group_count, chunks, per):
    share = group_count // chunks
    for chunk in range(chunks):
        for side in range(2):
            for place in range(share):
                group = chunk * share + place
                yield chunk, side, (side * share + place) * per, group * member_count * per


def units_apart(member, gate, up, gain, member_count, group_count, chunks):
    shard, width = gate.shape
    per = width // (member_count * group_count)
    columns = 2 * group_count * per
    strips = list(unit_strips(member_count, group_count, chunks, per))
    shape = jax.ShapeDtypeStruct((shard, columns), BF16)
    if per % 128:
        scaled = [(value * gain).astype(BF16) for value in (gate, up)]

        def block(away):
            other = member[0] ^ away
            return jnp.concatenate(
                [
                    lax.dynamic_slice_in_dim(scaled[side], base + other * per, per, 1)
                    for chunk, side, column, base in strips
                ],
                axis=1,
            )

        return [block(away) for away in range(member_count)]

    def kernel(member_ref, gate_ref, up_ref, gain_ref, *out_refs):
        for away, out_ref in enumerate(out_refs):
            other = member_ref[0] ^ away
            for chunk, side, column, base in strips:
                where = pl.ds(pl.multiple_of(base + other * per, per), per)
                source = (gate_ref, up_ref)[side][:, where].astype(F32)
                column += chunk * (columns // chunks)
                out_ref[:, column : column + per] = (source * gain_ref[...]).astype(BF16)

    return local_call(kernel, "units_apart", [shape] * member_count, member, gate, up, gain)


def units_together(member, chunk_blocks, gain, down, member_count, group_count):
    chunks = len(chunk_blocks)
    shard, columns = chunk_blocks[0][0].shape
    per = columns * chunks // (2 * group_count)
    width = per * member_count * group_count
    strips = list(unit_strips(member_count, group_count, chunks, per))
    blocks = [block for group in chunk_blocks for block in group]
    if per % 128:
        results = []
        for side in range(2):
            result = jnp.zeros((shard, width), F32)
            for away in range(member_count):
                other = member[0] ^ away
                for chunk, this, column, base in strips:
                    if this == side:
                        piece = chunk_blocks[chunk][away][:, column : column + per]
                        result = lax.dynamic_update_slice_in_dim(
                            result, piece.astype(F32) * gain, base + other * per, 1
                        )
            results.append(result)
        return *results, down.astype(F32)

    def kernel(member_ref, gain_ref, down_ref, *refs):
        outs = refs[len(blocks) :]
        outs[2][...] = down_ref[...].astype(F32)
        for away in range(member_count):
            other = member_ref[0] ^ away
            for chunk, side, column, base in strips:
                where = pl.ds(pl.multiple_of(base + other * per, per), per)
                piece = refs[chunk * member_count + away][:, column : column + per]
                outs[side][:, where] = piece.astype(F32) * gain_ref[...]

    shape = jax.ShapeDtypeStruct((shard, width), F32)
    shapes = [shape, shape, jax.ShapeDtypeStruct(down.shape, F32)]
    return local_call(kernel, "units_together", shapes, member, gain, down, *blocks)


def heads_together(member, arrived, gain, heads):
    count, shard, columns = arrived.shape
    width = heads * HD
    out_width = columns - width - 2 * HD
    copies = count // KVH

    def kernel(member_ref, arrived_ref, gain_ref, query_out, key_out, value_out, out_out):
        row = lax.broadcasted_iota(jnp.int32, (width, width), 0)
        column = lax.broadcasted_iota(jnp.int32, (width, width), 1)
        source = column % HD // HALF * (HALF * heads) + column // HD * HALF + column % HALF
        order = (row == source).astype(BF16)
        pair_row = lax.broadcasted_iota(jnp.int32, (2 * HD, KVH * HD), 0)
        pair_column = lax.broadcasted_iota(jnp.int32, (2 * HD, KVH * HD), 1)
        gain_here = gain_ref[...]
        keys = jnp.zeros((shard, KVH * HD), F32)
        values = jnp.zeros((shard, KVH * HD), F32)
        for away in range(count):
            other = (member_ref[0] + count - away) % count
            where = pl.ds(pl.multiple_of(other * width, width), width)
            query_out[:, where] = dot_nn(arrived_ref[away, :, :width], order) * gain_here
            pair = arrived_ref[away, :, width : width + 2 * HD]
            first = other // copies * HD
            to_keys = (pair_column == pair_row + first) & (pair_row < HD)
            to_values = (pair_column == pair_row - HD + first) & (pair_row >= HD)
            keys = keys + dot_nn(pair, to_keys.astype(BF16))
            values = values + dot_nn(pair, to_values.astype(BF16))
            out_where = pl.ds(pl.multiple_of(other * out_width, out_width), out_width)
            out_out[:, out_where] = arrived_ref[away, :, width + 2 * HD :].astype(F32)
        key_out[...] = keys * gain_here
        value_out[...] = values * gain_here

    shapes = [
        jax.ShapeDtypeStruct((shard, size), F32)
        for size in (count * width, KVH * HD, KVH * HD, count * out_width)
    ]
    return local_call(kernel, "heads_together", shapes, member, arrived, gain)


def units_kernel(normed_ref, gradient_ref, both_ref, down_ref, hidden_ref, grad_ref):
    units = down_ref.shape[0]
    normed = normed_ref[...]
    gradient = gradient_ref[...]
    part = min(256, units)
    for first in range(0, units, part):
        where = slice(first, first + part)
        past = slice(units + first, units + first + part)
        gate = dot_nn(normed, both_ref[:, where])
        up = dot_nn(normed, both_ref[:, past])
        upstream = dot_nt(gradient, down_ref[where, :])
        sigmoid = jax.nn.sigmoid(gate)
        active = gate * sigmoid
        hidden_ref[:, where] = (active * up).astype(BF16)
        grad_ref[:, where] = (
            upstream * up * sigmoid * (1.0 + gate * (1.0 - sigmoid))
        ).astype(BF16)
        grad_ref[:, past] = (upstream * active).astype(BF16)


def hidden_units(normed, gradient, both, down, chunk):
    tokens, model = normed.shape
    units = both.shape[1] // 2
    tile = 512
    by_tile = pl.BlockSpec((tile, model), lambda i: (i, 0))
    return pl.pallas_call(
        units_kernel,
        grid=(tokens // tile,),
        in_specs=[
            by_tile,
            by_tile,
            pl.BlockSpec(both.shape, lambda i: (0, 0)),
            pl.BlockSpec((units, model), lambda i: (chunk, 0)),
        ],
        out_specs=[
            pl.BlockSpec((tile, units), lambda i: (i, 0)),
            pl.BlockSpec((tile, 2 * units), lambda i: (i, 0)),
        ],
        out_shape=[
            jax.ShapeDtypeStruct((tokens, units), BF16),
            jax.ShapeDtypeStruct((tokens, 2 * units), BF16),
        ],
        compiler_params=pltpu.CompilerParams(vmem_limit_bytes=VMEM_BYTES),
        cost_estimate=pl.CostEstimate(
            flops=6 * tokens * model * units,
            bytes_accessed=4 * tokens * model + 6 * units * model,
            transcendentals=tokens * units,
        ),
        name="hidden_units",
    )(normed, gradient, both, down)


def half_group(shape, heads):
    return (lax.broadcasted_iota(jnp.int32, shape, 1) // HALF) % heads


def full_group(shape):
    return lax.broadcasted_iota(jnp.int32, shape, 1) // HD


def spread_keys(width):
    heads = width // HD
    row = lax.broadcasted_iota(jnp.int32, (2 * HD, width), 0)
    column = lax.broadcasted_iota(jnp.int32, (2 * HD, width), 1)
    source = column // (HALF * heads) * HALF + column % HALF
    return (row == source).astype(F32)


def spread_values(width):
    row = lax.broadcasted_iota(jnp.int32, (2 * HD, width), 0)
    column = lax.broadcasted_iota(jnp.int32, (2 * HD, width), 1)
    return (row == HD + column % HD).astype(F32)


def exact(left, right, dims):
    return lax.dot_general(
        left,
        right,
        (dims, ((), ())),
        precision=lax.Precision.HIGHEST,
        preferred_element_type=F32,
    )


def tables(table, width):
    half = width // 2
    row = lax.broadcasted_iota(jnp.int32, (2 * HALF, half), 0)
    column = lax.broadcasted_iota(jnp.int32, (2 * HALF, half), 1) % HALF
    return (
        exact(table, (row == column).astype(F32), ((1,), (0,))),
        exact(table, (row == column + HALF).astype(F32), ((1,), (0,))),
    )


def turn(values, cosine, sine):
    half = cosine.shape[1]
    first = values[:, :half]
    second = values[:, half:]
    return jnp.concatenate([first * cosine - second * sine, second * cosine + first * sine], axis=1)


def forward_kernel(
    heads,
    first_ref,
    normed_ref,
    weight_ref,
    table_ref,
    start_ref,
    query_ref,
    key_ref,
    key_columns_ref,
    value_ref,
    mixed_ref,
    lse_ref,
    value_columns,
    top,
    total,
    acc,
):
    step = pl.program_id(0)
    width = heads * HD
    start = start_ref[...]
    cosine, sine = tables(table_ref[...], width)
    projected = dot_nn(normed_ref[...], weight_ref[:, : width + 2 * HD])
    query = turn(projected[:, :width], cosine, sine).astype(BF16)
    pair = projected[:, width:]
    keys_here = turn(exact(pair, spread_keys(width), ((1,), (0,))), cosine, sine).astype(BF16)
    own_rows = pl.ds(pl.multiple_of(step * BLOCK, BLOCK), BLOCK)
    query_ref[...] = query
    key_ref[own_rows, :] = keys_here
    turned_keys = jnp.transpose(keys_here.astype(F32)).astype(BF16)
    key_columns_ref[:HALF, :] = turned_keys[:HALF, :]
    key_columns_ref[HALF:, :] = turned_keys[width // 2 : width // 2 + HALF, :]
    value_ref[...] = exact(pair, spread_values(width), ((1,), (0,))).astype(BF16)
    value_columns[:, own_rows] = jnp.transpose(pair)[HD:, :].astype(BF16)
    token = step * BLOCK + lax.broadcasted_iota(jnp.int32, (BLOCK, BLOCK), 1)
    within = lax.broadcasted_iota(jnp.int32, (BLOCK, BLOCK), 0)
    lane_head = half_group((BLOCK, width), heads)
    top[...] = jnp.full_like(top, MASKED)
    total[...] = jnp.zeros_like(total)
    acc[...] = jnp.zeros_like(acc)

    def one_block(block, carried):
        offset = pl.multiple_of(block * BLOCK, BLOCK)
        keys = key_ref[pl.ds(offset, BLOCK), :]
        values = value_columns[:, pl.ds(offset, BLOCK)]
        place = offset + within
        visible = (place >= start) & (place <= token)
        for head in range(heads):
            own_keys = jnp.where(lane_head == head, keys, jnp.zeros_like(keys))
            scores = jnp.where(visible, dot_nt(own_keys, query) * ATTENTION_SCALE, MASKED)
            old = top[head : head + 1, :]
            new = jnp.maximum(old, jnp.max(scores, axis=0, keepdims=True))
            weights = jnp.exp(scores - new)
            fade = jnp.exp(old - new)
            top[head : head + 1, :] = new
            total[head : head + 1, :] = total[head : head + 1, :] * fade + jnp.sum(
                weights, axis=0, keepdims=True
            )
            acc[head * HD : (head + 1) * HD, :] = acc[
                head * HD : (head + 1) * HD, :
            ] * fade + dot_nn(values, weights.astype(BF16))
        return carried

    lax.fori_loop(first_ref[step], step + 1, one_block, 0)
    for head in range(heads):
        acc[head * HD : (head + 1) * HD, :] = (
            acc[head * HD : (head + 1) * HD, :] / total[head : head + 1, :]
        )
    mixed_ref[...] = jnp.transpose(acc[...]).astype(BF16)
    lse_ref[...] = top[...] + jnp.log(total[...])


def attention_forward(first, normed, weight, table, start, heads):
    tokens, model = normed.shape
    width = heads * HD
    by_block = pl.BlockSpec((BLOCK, width), lambda i, first: (i, 0))
    whole = pl.BlockSpec((tokens, width), lambda i, first: (0, 0))
    return pl.pallas_call(
        functools.partial(forward_kernel, heads),
        grid_spec=pltpu.PrefetchScalarGridSpec(
            num_scalar_prefetch=1,
            grid=(tokens // BLOCK,),
            in_specs=[
                pl.BlockSpec((BLOCK, model), lambda i, first: (i, 0)),
                pl.BlockSpec(weight.shape, lambda i, first: (0, 0)),
                pl.BlockSpec((BLOCK, 2 * HALF), lambda i, first: (i, 0)),
                pl.BlockSpec((1, BLOCK), lambda i, first: (0, i)),
            ],
            out_specs=[
                by_block,
                whole,
                pl.BlockSpec((HD, BLOCK), lambda i, first: (0, i)),
                by_block,
                by_block,
                pl.BlockSpec((heads, BLOCK), lambda i, first: (0, i)),
            ],
            scratch_shapes=[
                pltpu.VMEM((HD, tokens), BF16),
                pltpu.VMEM((heads, BLOCK), F32),
                pltpu.VMEM((heads, BLOCK), F32),
                pltpu.VMEM((width, BLOCK), F32),
            ],
        ),
        out_shape=[jax.ShapeDtypeStruct((tokens, width), BF16)] * 2
        + [jax.ShapeDtypeStruct((HD, tokens), BF16)]
        + [jax.ShapeDtypeStruct((tokens, width), BF16)] * 2
        + [jax.ShapeDtypeStruct((heads, tokens), F32)],
        compiler_params=pltpu.CompilerParams(vmem_limit_bytes=VMEM_BYTES),
        cost_estimate=pl.CostEstimate(
            flops=64 * tokens * BLOCK * width, bytes_accessed=8 * tokens * width, transcendentals=0
        ),
        name="attention_forward",
    )(first, normed, weight, table, start)


def backward_kernel(
    heads,
    first_ref,
    query_ref,
    key_ref,
    key_columns_ref,
    value_ref,
    mixed_ref,
    grad_ref,
    weight_ref,
    lse_ref,
    start_ref,
    table_ref,
    out_ref,
    weight_grad_ref,
    dquery,
    dkey,
    dvalue,
    weight_grad,
):
    step = pl.program_id(0)
    query = query_ref[...]
    grad_one = grad_ref[...]
    grad = dot_nt(grad_one, weight_ref[...]).astype(BF16)
    start = start_ref[...]
    width = query.shape[1]
    token = step * BLOCK + lax.broadcasted_iota(jnp.int32, (BLOCK, BLOCK), 1)
    within = lax.broadcasted_iota(jnp.int32, (BLOCK, BLOCK), 0)
    half_head = half_group((BLOCK, width), heads)
    full_head = full_group((BLOCK, width))
    zero = jnp.zeros((BLOCK, width), BF16)
    product = grad.astype(F32) * mixed_ref[...].astype(F32)
    chooser = (
        lax.broadcasted_iota(jnp.int32, (8, width), 0)
        == lax.broadcasted_iota(jnp.int32, (8, width), 1) // HD
    ).astype(F32)
    correction = exact(chooser, product, ((1,), (1,)))

    @pl.when(step == 0)
    def _():
        dkey[...] = jnp.zeros_like(dkey)
        dvalue[...] = jnp.zeros_like(dvalue)
        weight_grad[...] = jnp.zeros_like(weight_grad)

    weight_grad[...] += dot_tn(mixed_ref[...], grad_one)
    dquery[...] = jnp.zeros_like(dquery)

    def one_block(block, carried):
        offset = pl.multiple_of(block * BLOCK, BLOCK)
        rows = pl.ds(offset, BLOCK)
        keys = key_ref[rows, :]
        values = value_ref[rows, :]
        key_columns = key_columns_ref[:, rows]
        place = offset + within
        visible = (place >= start) & (place <= token)
        new_key = dkey[rows, :]
        new_value = dvalue[rows, :]
        for head in range(heads):
            own_keys = jnp.where(half_head == head, keys, zero)
            own_values = jnp.where(full_head == head, values, zero)
            scores = dot_nt(own_keys, query) * ATTENTION_SCALE
            probs = jnp.where(visible, jnp.exp(scores - lse_ref[head : head + 1, :]), 0.0)
            pressure = dot_nt(own_values, grad)
            dscores = (probs * (pressure - correction[head : head + 1, :])).astype(BF16)
            new_value = new_value + dot_nn(
                probs.astype(BF16), jnp.where(full_head == head, grad, zero)
            )
            new_key = new_key + dot_nn(dscores, jnp.where(half_head == head, query, zero))
            term = dot_nn(key_columns, dscores)
            low = slice(head * HALF, (head + 1) * HALF)
            high = slice(width // 2 + head * HALF, width // 2 + (head + 1) * HALF)
            dquery[low, :] += term[:HALF]
            dquery[high, :] += term[HALF:]
        dkey[rows, :] = new_key
        dvalue[rows, :] = new_value
        return carried

    lax.fori_loop(first_ref[step], step + 1, one_block, 0)
    own_rows = pl.ds(pl.multiple_of(step * BLOCK, BLOCK), BLOCK)
    cosine, sine = tables(table_ref[own_rows, :], width)
    out_ref[own_rows, :width] = (
        turn(jnp.transpose(dquery[...]), cosine, -sine) * ATTENTION_SCALE
    ).astype(BF16)

    @pl.when(step == pl.num_programs(0) - 1)
    def _():
        def fold(block, carried):
            rows = pl.ds(pl.multiple_of(block * BLOCK, BLOCK), BLOCK)
            cosine, sine = tables(table_ref[rows, :], width)
            turned = turn(dkey[rows, :], cosine, -sine) * ATTENTION_SCALE
            out_ref[rows, width:] = (
                dot_nt(turned.astype(BF16), spread_keys(width).astype(BF16))
                + dot_nt(dvalue[rows, :].astype(BF16), spread_values(width).astype(BF16))
            ).astype(BF16)
            return carried

        lax.fori_loop(0, pl.num_programs(0), fold, 0)
        weight_grad_ref[...] = weight_grad[...].astype(BF16)


def attention_backward(
    first, query, keys, key_columns, values, mixed, grad, weight, lse, start, table
):
    tokens, width = query.shape
    model = grad.shape[1]
    heads = width // HD
    columns = width + 2 * HD
    by_block = pl.BlockSpec((BLOCK, width), lambda i, first: (i, 0))
    whole = pl.BlockSpec((tokens, width), lambda i, first: (0, 0))
    return pl.pallas_call(
        functools.partial(backward_kernel, heads),
        grid_spec=pltpu.PrefetchScalarGridSpec(
            num_scalar_prefetch=1,
            grid=(tokens // BLOCK,),
            in_specs=[
                by_block,
                whole,
                pl.BlockSpec((HD, tokens), lambda i, first: (0, 0)),
                whole,
                by_block,
                pl.BlockSpec((BLOCK, model), lambda i, first: (i, 0)),
                pl.BlockSpec((width, model), lambda i, first: (0, 0)),
                pl.BlockSpec((heads, BLOCK), lambda i, first: (0, i)),
                pl.BlockSpec((1, BLOCK), lambda i, first: (0, i)),
                pl.BlockSpec((tokens, 2 * HALF), lambda i, first: (0, 0)),
            ],
            out_specs=[
                pl.BlockSpec((tokens, columns), lambda i, first: (0, 0)),
                pl.BlockSpec((width, model), lambda i, first: (0, 0)),
            ],
            scratch_shapes=[
                pltpu.VMEM((width, BLOCK), F32),
                pltpu.VMEM((tokens, width), F32),
                pltpu.VMEM((tokens, width), F32),
                pltpu.VMEM((width, model), F32),
            ],
        ),
        out_shape=[
            jax.ShapeDtypeStruct((tokens, columns), BF16),
            jax.ShapeDtypeStruct((width, model), BF16),
        ],
        compiler_params=pltpu.CompilerParams(vmem_limit_bytes=VMEM_BYTES),
        cost_estimate=pl.CostEstimate(
            flops=0, bytes_accessed=tokens * width, transcendentals=0
        ),
        name="attention_backward",
    )(first, query, keys, key_columns, values, mixed, grad, weight, lse, start, table)


def projection_grad(normed, grad, out_grad):
    tokens, model = normed.shape
    columns, more = grad.shape[1], out_grad.shape[1]
    tile = 512

    def kernel(normed_ref, grad_ref, out_grad_ref, result_ref):
        result_ref[:, :columns] = dot_tn(normed_ref[...], grad_ref[...]).astype(BF16)
        result_ref[:, columns:] = out_grad_ref[...]

    return pl.pallas_call(
        kernel,
        grid=(model // tile,),
        in_specs=[
            pl.BlockSpec((tokens, tile), lambda i: (0, i)),
            pl.BlockSpec((tokens, columns), lambda i: (0, 0)),
            pl.BlockSpec((tile, more), lambda i: (i, 0)),
        ],
        out_specs=pl.BlockSpec((tile, columns + more), lambda i: (i, 0)),
        out_shape=jax.ShapeDtypeStruct((model, columns + more), BF16),
        compiler_params=pltpu.CompilerParams(vmem_limit_bytes=VMEM_BYTES),
        cost_estimate=pl.CostEstimate(
            flops=2 * tokens * model * columns, bytes_accessed=2 * tokens * model, transcendentals=0
        ),
        name="projection_grad",
    )(normed, grad, out_grad)


def token_starts(lengths_row, group_tokens):
    count = lengths_row.shape[0]
    order = jnp.arange(count, dtype=jnp.int32)
    finish = jnp.sum(jnp.where(order[None, :] <= order[:, None], lengths_row[None, :], 0), axis=1)
    place = jnp.arange(group_tokens, dtype=jnp.int32)
    passed = place[:, None] >= finish[None, :]
    return jnp.max(jnp.where(passed, finish[None, :], 0), axis=1), place


def inverse_norm(values):
    return lax.rsqrt(jnp.mean(values * values, axis=1, keepdims=True) + EPSILON)


def after(value, *earlier):
    return lax.optimization_barrier((value, *earlier))[0]


def sum_over_groups(value):
    return lax.psum_scatter(value, "dp", scatter_dimension=0, tiled=True)


def gather_groups(value):
    return lax.all_gather(value, "dp", axis=0, tiled=True)


def body(
    tokens,
    cotangent,
    query_weight,
    key_weight,
    value_weight,
    output_weight,
    gate_weight,
    up_weight,
    down_weight,
    attention_gain,
    feedforward_gain,
    lengths,
):
    members = lax.axis_size("fsdp")
    groups = lax.axis_size("dp")
    rows, model = tokens.shape
    group_tokens = rows * members
    shard = query_weight.shape[0]
    heads = NH // members
    width = heads * HD
    columns = width + 2 * HD
    copies = members // KVH
    out_columns = model // members
    down_rows = down_weight.shape[0]
    units = groups * down_rows // CHUNKS
    gain_one = attention_gain.astype(F32)[:, None]
    gain_two = feedforward_gain.astype(F32)[:, None]
    member = lax.axis_index("fsdp").astype(jnp.int32)[None]

    scaled_query = (query_weight * gain_one).astype(BF16)
    scaled_key = (key_weight * gain_one).astype(BF16)
    scaled_value = (value_weight * gain_one).astype(BF16)
    packed_in = jnp.concatenate(
        [
            scaled_query.reshape(shard, members, heads, 2, HALF)
            .transpose(1, 0, 3, 2, 4)
            .reshape(members, shard, width),
            jnp.repeat(
                scaled_key.reshape(shard, KVH, HD).transpose(1, 0, 2), copies, axis=0
            ),
            jnp.repeat(
                scaled_value.reshape(shard, KVH, HD).transpose(1, 0, 2), copies, axis=0
            ),
            output_weight.reshape(shard, members, out_columns).transpose(1, 0, 2),
        ],
        axis=2,
    )
    [packed_in] = plane_swap([packed_in], members, 1)
    packed_in = packed_in.reshape(members * shard, columns + out_columns)
    inputs = tokens.astype(F32)
    inverse_one = inverse_norm(inputs)
    start, place = token_starts(lengths[0], group_tokens)
    first = start[::BLOCK] // BLOCK
    frequency = ROPE_BASE ** (-(2.0 * jnp.arange(HALF, dtype=F32)) / HD)
    angles = (place - start).astype(F32)[:, None] * frequency[None, :]
    table = jnp.concatenate([jnp.cos(angles), jnp.sin(angles)], axis=1)
    start = start[None, :]

    gate_up = exchanged(
        units_apart(
            member, after(gate_weight, packed_in), up_weight, gain_two, members, groups, CHUNKS
        )
    )
    packed = gather_groups(packed_in)
    down_all = gather_groups(down_weight)
    normed_one = plane_gather(
        after((inputs * inverse_one).astype(BF16), packed_in), members, 0, True
    )
    upstream = cotangent.astype(F32)
    grad_two = (RESIDUAL_SCALE * upstream).astype(BF16)
    grad_two, down_all, table, first, start, _ = lax.optimization_barrier(
        (grad_two, down_all, table, first, start, normed_one)
    )
    grad_two = plane_gather(grad_two, members, 9, False)
    gate_up, grad_two = lax.optimization_barrier((gate_up, grad_two))
    gate_up_parts = rows_together(member, gate_up, CHUNKS)
    gate_up_chunks = [gather_groups(part) for part in gate_up_parts]
    packed, gate_up_parts = lax.optimization_barrier((packed, gate_up_parts))

    out_blocks = exchanged(rows_apart(member, packed, members, columns))
    query, keys, key_columns, values, mixed, lse = attention_forward(
        first, normed_one, packed, table, start, heads
    )
    mixed_then, out_blocks = lax.optimization_barrier((mixed, out_blocks))
    out_piece = columns_together(member, out_blocks)
    branch_one = product_scatter([mixed_then], [out_piece], False, members, 2, True)
    residual = inputs + RESIDUAL_SCALE * branch_one

    inverse_two = inverse_norm(residual)
    normed_two = plane_gather((residual * inverse_two).astype(BF16), members, 3, False)
    fused = group_tokens <= 2048
    hiddens = []
    grad_boths = []
    gate_up_grads = []
    for chunk in range(CHUNKS):
        both_weight = gate_up_chunks[chunk]
        hidden, grad_both = hidden_units(normed_two, grad_two, both_weight, down_all, chunk)
        hiddens.append(hidden)
        grad_boths.append(grad_both)
        if chunk < CHUNKS - 1 or not fused:
            gate_up_grad = dot_tn(normed_two, grad_both).astype(BF16)
            gate_up_grads.append(sum_over_groups(gate_up_grad))
            normed_two, grad_two, hiddens, grad_boths, _ = lax.optimization_barrier(
                (normed_two, grad_two, hiddens, grad_boths, gate_up_grad)
            )
    if fused:
        weighted_two, gate_up_grad = product_scatter(
            grad_boths, gate_up_chunks, True, members, 4, False, normed_two
        )
        gate_up_grads.append(sum_over_groups(gate_up_grad))
    else:
        weighted_two = product_scatter(grad_boths, gate_up_chunks, True, members, 4, False)
    grad_residual = (
        upstream
        + inverse_two * weighted_two
        - residual * inverse_two**3 * jnp.mean(weighted_two * residual, axis=1, keepdims=True)
    )
    gain_term_two = jnp.sum(weighted_two * residual * inverse_two, axis=0)

    grad_one, down_grad, out_high, out_kept = plane_gather(
        (RESIDUAL_SCALE * grad_residual).astype(BF16),
        members,
        5,
        True,
        (hiddens, grad_two, down_all),
    )
    down_grad = sum_over_groups(down_grad)
    gate_up_grads[0] = exchanged(
        rows_apart(member, after(gate_up_grads[0], grad_one), members)
    )
    steps = len(plane_masks(members))
    half_rows = group_tokens // 4
    out_sent = send_to(out_high, members, hopped(steps - 1, members))
    grad_projected, out_grad = attention_backward(
        first, query, keys, key_columns, values, mixed, grad_one, out_piece, lse, start, table
    )
    out_grad = lax.all_to_all(out_grad, "fsdp", split_axis=1, concat_axis=0, tiled=True)
    packed_grad = projection_grad(normed_one, grad_projected, out_grad)
    gate_up_grads[1:] = [
        exchanged(rows_apart(member, part, members))
        for part in after(gate_up_grads[1:], grad_projected)
    ]
    grad_projected, packed_grad, gate_up_grads[0], out_sent, out_kept = lax.optimization_barrier(
        (grad_projected, packed_grad, gate_up_grads[0], out_sent, out_kept)
    )
    for step in reversed(range(steps - 1)):
        half_rows //= 2
        out_next = added(out_kept[half_rows:], out_sent[half_rows:]).astype(BF16)
        out_kept = added(out_kept[:half_rows], out_sent[:half_rows])
        if step:
            out_kept = out_kept.astype(BF16)
        out_sent = send_to(out_next, members, hopped(step, members))
    packed_grad = sum_over_groups(packed_grad)
    weighted_one = product_scatter([grad_projected], [packed], True, members, 6, True, weight=1)
    weighted_one, down_grad = lax.optimization_barrier((weighted_one, down_grad))
    grad_inputs = (
        grad_residual
        + inverse_one * weighted_one
        - inputs * inverse_one**3 * jnp.mean(weighted_one * inputs, axis=1, keepdims=True)
    )
    gain_term_one = jnp.sum(weighted_one * inputs * inverse_one, axis=0)

    gains = jnp.stack(
        [
            gain_term_one.reshape(groups, members, shard),
            gain_term_two.reshape(groups, members, shard),
        ],
        axis=2,
    ).reshape(groups, members, 2 * shard)
    gains = jnp.pad(
        gains.transpose(1, 0, 2), ((0, 0), (0, (-groups) % 8), (0, (-2 * shard) % 128))
    )
    output = (residual + RESIDUAL_SCALE * added(out_kept, out_sent)).astype(BF16)

    gate_grad, up_grad, down_grad = units_together(
        member, after(gate_up_grads, weighted_one), gain_two, down_grad, members, groups
    )
    arrived, gains = finale(packed_grad, gains, groups, 8)
    query_grad, key_grad, value_grad, out_grad = heads_together(member, arrived, gain_one, heads)
    gains = lax.dynamic_slice_in_dim(gains, lax.axis_index("dp"), 1, 0)[0, : 2 * shard]
    gains = gains.reshape(2, shard)
    return (
        output,
        grad_inputs.astype(BF16),
        query_grad,
        key_grad,
        value_grad,
        out_grad,
        gate_grad,
        up_grad,
        down_grad,
        gains[0] / gain_one[:, 0],
        gains[1] / gain_two[:, 0],
    )


def solution(mesh):
    by_rows = P(("dp", "fsdp"), None)
    by_entries = P(("dp", "fsdp"))
    return jax.shard_map(
        body,
        mesh=mesh,
        in_specs=(by_rows,) * 9 + (by_entries,) * 2 + (P("dp", None),),
        out_specs=(by_rows,) * 9 + (by_entries,) * 2,
        check_vma=False,
    )
```

```python
import functools

import jax
import jax.numpy as jnp
from jax import lax
from jax.experimental import pallas as pl
from jax.experimental.pallas import tpu as pltpu
from jax.sharding import PartitionSpec as P

NH = 32
KVH = 8
HD = 64
HALF = HD // 2

EPSILON = 1e-05
RESIDUAL_SCALE = 0.22
ATTENTION_SCALE = 0.015625
ROPE_BASE = 10000000.0
MASKED = -1e30
BLOCK = 256
CHUNKS = 2
PIECES = 4
SCATTER_PIECES = 8
VMEM_BYTES = 58 * 1024 * 1024
MESH = pl.DeviceIdType.MESH
BF16 = jnp.bfloat16
F32 = jnp.float32


def dot_nn(left, right):
    return jnp.dot(left, right, preferred_element_type=F32)


def dot_nt(left, right):
    return lax.dot_general(left, right, (((1,), (1,)), ((), ())), preferred_element_type=F32)


def dot_tn(left, right):
    return lax.dot_general(left, right, (((0,), (0,)), ((), ())), preferred_element_type=F32)


def flip(index, mask):
    return index + mask * (1 - 2 * ((index // mask) % 2))


def plane_masks(member_count):
    masks = []
    mask = 2
    while mask < member_count:
        masks.append(mask)
        mask *= 2
    return masks


def hop(index, step, masks):
    core = index % 2
    return (1 - core) * flip(index, masks[step]) + core * flip(index, masks[-1 - step])


def walk(index, subset, masks):
    for step in range(len(masks)):
        if (subset >> step) & 1:
            index = hop(index, step, masks)
    return index


def greet(group, member, masks):
    barrier = pltpu.get_barrier_semaphore()
    partners = [hop(member, step, masks) for step in range(len(masks))] + [flip(member, 1)]
    for partner in partners:
        pl.semaphore_signal(barrier, inc=1, device_id=(group, partner), device_id_type=MESH)
    pl.semaphore_wait(barrier, len(partners))


def gather_kernel(member_count, in_order, count, own_ref, *refs):
    operands = refs[: count + 2] if count else ()
    refs = refs[len(operands) :]
    extra = 4 if count else 1
    all_ref, results, refs = refs[0], refs[1:extra], refs[extra:]
    link_send, link_recv, core_send, core_recv, local_sem = refs[:5]
    group = lax.axis_index("dp")
    member = lax.axis_index("fsdp")
    masks = plane_masks(member_count)
    steps = len(masks)
    rows = own_ref.shape[0]
    piece = rows // PIECES
    greet(group, member, masks)

    blocks = 1 << steps

    def place(owner, subset, side, part):
        block = walk(owner, subset, masks) if in_order else subset + side * blocks
        return all_ref.at[pl.ds(pl.multiple_of(block * rows + part * piece, piece), piece)]

    def link_copy(step, subset, part):
        number = (1 << step) - 1 + subset
        here = place(member, subset, 0, part)
        there = here if in_order else place(member, subset | (1 << step), 0, part)
        return pltpu.make_async_remote_copy(
            own_ref.at[pl.ds(part * piece, piece)] if subset == 0 else here,
            there,
            link_send.at[number, part],
            link_recv.at[number, part],
            device_id=(group, hop(member, step, masks)),
            device_id_type=MESH,
        )

    def core_copy(subset, part):
        here = place(member, subset, 0, part)
        there = here if in_order else place(member, subset, 1, part)
        return pltpu.make_async_remote_copy(
            own_ref.at[pl.ds(part * piece, piece)] if subset == 0 else here,
            there,
            core_send.at[subset, part],
            core_recv.at[subset, part],
            device_id=(group, flip(member, 1)),
            device_id_type=MESH,
        )

    for part in range(PIECES):
        for step in range(steps):
            link_copy(step, 0, part).start()
    first = pl.multiple_of(member * rows, rows) if in_order else 0
    keep = pltpu.make_async_copy(own_ref, all_ref.at[pl.ds(first, rows)], local_sem)
    keep.start()
    for part in range(PIECES):
        core_copy(0, part).start()
    tiles = []
    if count:
        hidden, gradient, down, down_grad, out_sibling, out_own, turned, out_arrived = refs[5:13]
        load_sem, store_sem, out_send, out_recv = refs[13:]
        units = operands[0].shape[1]
        targets = [hidden.at[:, pl.ds(number * units, units)] for number in range(count)]
        loads = [
            pltpu.make_async_copy(source, target, load_sem.at[number])
            for number, (source, target) in enumerate(zip(operands, (*targets, gradient, down)))
        ]
        half = out_own.shape[0]
        finished = (
            down_grad,
            out_own.at[pl.ds(half // 2, half // 2)],
            out_own.at[pl.ds(0, half // 2)],
        )
        stores = [
            pltpu.make_async_copy(source, target, store_sem.at[number])
            for number, (source, target) in enumerate(zip(finished, results))
        ]
        for load in loads:
            load.start()
        width = 256

        def out_copy(column):
            where = pl.ds(column, width)
            return pltpu.make_async_remote_copy(
                out_sibling.at[:, where],
                out_arrived.at[:, where],
                out_send.at[column // width],
                out_recv.at[column // width],
                device_id=(group, flip(member, 1)),
                device_id_type=MESH,
            )

        def sibling_tile(column):
            out_sibling[:, column : column + width] = dot_nn(
                hidden[half:, :], down[:, column : column + width]
            ).astype(BF16)
            out_copy(column).start()

        def own_tile(column):
            product = dot_nn(hidden[:half, :], down[:, column : column + width])
            out_copy(column).wait()
            out_own[:, column : column + width] = (
                product + out_arrived[:, column : column + width].astype(F32)
            ).astype(BF16)

        def turn_tile(number):
            part = slice(number * units, (number + 1) * units)
            turned[part, :] = jnp.transpose(hidden[:, part])

        def grad_tile(column):
            down_grad[:, column : column + width] = dot_nn(
                turned[...], gradient[:, column : column + width]
            ).astype(BF16)

        for load in loads[:count] + loads[count + 1 :]:
            tiles.append(load.wait)
        starts = range(0, down.shape[1], width)
        for column in starts:
            tiles.append(functools.partial(sibling_tile, column))
        for column in starts:
            tiles.append(functools.partial(own_tile, column))
        tiles += [stores[1].start, stores[2].start]
        tiles.append(loads[count].wait)
        for number in range(count):
            tiles.append(functools.partial(turn_tile, number))
        for column in starts:
            tiles.append(functools.partial(grad_tile, column))
        tiles.append(stores[0].start)
    shares = [4] * PIECES + [2, 1, 0, 0] * max(1, steps - 1)
    shares = shares[: steps * PIECES]
    ends = [-(-len(tiles) * sum(shares[: n + 1]) // sum(shares)) for n in range(len(shares))]

    turn = 0
    for step in range(steps):
        for part in range(PIECES):
            for subset in range(1 << step):
                link_copy(step, subset, part).wait_recv()
                arrived = subset | (1 << step)
                for later in range(step + 1, steps):
                    link_copy(later, arrived, part).start()
                core_copy(arrived, part).start()
            for run in tiles[ends[turn - 1] if turn else 0 : ends[turn]]:
                run()
            turn += 1
    for part in range(PIECES):
        for subset in range(1 << steps):
            core_copy(subset, part).wait()
    for part in range(PIECES):
        for step in range(steps):
            for subset in range(1 << step):
                link_copy(step, subset, part).wait_send()
    keep.wait()
    if count:
        for store in stores:
            store.wait()


def plane_gather(own, member_count, collective_id, in_order, extras=None):
    rows, width = own.shape
    steps = len(plane_masks(member_count))
    blocks = 1 << steps
    total = member_count * rows
    any_space = pl.BlockSpec(memory_space=pl.ANY)
    scratch = [
        pltpu.SemaphoreType.DMA((blocks - 1, PIECES)),
        pltpu.SemaphoreType.DMA((blocks - 1, PIECES)),
        pltpu.SemaphoreType.DMA((blocks, PIECES)),
        pltpu.SemaphoreType.DMA((blocks, PIECES)),
        pltpu.SemaphoreType.DMA,
    ]
    operands = [own]
    out_shape = [jax.ShapeDtypeStruct((total, width), own.dtype)]
    count = 0
    if extras:
        hiddens, gradient, down = extras
        count = len(hiddens)
        operands += [*hiddens, gradient, down]
        units = down.shape[0]
        scratch += [
            pltpu.VMEM((total, units), BF16),
            pltpu.VMEM(gradient.shape, BF16),
            pltpu.VMEM(down.shape, BF16),
        ]
        out_shape += [
            jax.ShapeDtypeStruct((down.shape[0], gradient.shape[1]), BF16),
            jax.ShapeDtypeStruct((total // 4, down.shape[1]), BF16),
            jax.ShapeDtypeStruct((total // 4, down.shape[1]), BF16),
        ]
        out_half = pltpu.VMEM((total // 2, down.shape[1]), BF16)
        scratch += [
            pltpu.VMEM(out_shape[1].shape, BF16),
            out_half,
            out_half,
            pltpu.VMEM((units, total), BF16),
            out_half,
            pltpu.SemaphoreType.DMA((count + 2,)),
            pltpu.SemaphoreType.DMA((3,)),
            pltpu.SemaphoreType.DMA((down.shape[1] // 256,)),
            pltpu.SemaphoreType.DMA((down.shape[1] // 256,)),
        ]
    result = pl.pallas_call(
        functools.partial(gather_kernel, member_count, in_order, count),
        out_shape=out_shape,
        in_specs=[any_space] * len(operands),
        out_specs=[any_space] * len(out_shape),
        scratch_shapes=scratch,
        compiler_params=pltpu.CompilerParams(
            collective_id=collective_id, has_side_effects=True, vmem_limit_bytes=VMEM_BYTES
        ),
        cost_estimate=pl.CostEstimate(
            flops=0, bytes_accessed=(1 if extras else 60) * total * width, transcendentals=0
        ),
        name="plane_gather",
    )(*operands)
    return result if extras else result[0]


def swap_kernel(member_count, count, *refs):
    sources, targets = refs[:count], refs[count : 2 * count]
    send_sem, recv_sem, local_sem = refs[2 * count :]
    group = lax.axis_index("dp")
    member = lax.axis_index("fsdp")
    barrier = pltpu.get_barrier_semaphore()
    for away in range(1, member_count):
        pl.semaphore_signal(
            barrier,
            inc=1,
            device_id=(group, (member + away) % member_count),
            device_id_type=MESH,
        )
    pl.semaphore_wait(barrier, member_count - 1)

    def copy(number, away):
        target = (member + away) % member_count
        return pltpu.make_async_remote_copy(
            sources[number].at[target],
            targets[number].at[member],
            send_sem.at[number, away],
            recv_sem.at[number, away],
            device_id=(group, target),
            device_id_type=MESH,
        )

    def keep(number):
        return pltpu.make_async_copy(
            sources[number].at[member], targets[number].at[member], local_sem.at[number]
        )

    for number in range(count):
        for away in range(1, member_count):
            copy(number, away).start()
        keep(number).start()
    for number in range(count):
        for away in range(1, member_count):
            copy(number, away).wait()
        keep(number).wait()


def plane_swap(values, member_count, collective_id):
    count = len(values)
    any_space = pl.BlockSpec(memory_space=pl.ANY)
    return pl.pallas_call(
        functools.partial(swap_kernel, member_count, count),
        out_shape=[jax.ShapeDtypeStruct(value.shape, value.dtype) for value in values],
        in_specs=[any_space] * count,
        out_specs=[any_space] * count,
        scratch_shapes=[
            pltpu.SemaphoreType.DMA((count, member_count)),
            pltpu.SemaphoreType.DMA((count, member_count)),
            pltpu.SemaphoreType.DMA((count,)),
        ],
        compiler_params=pltpu.CompilerParams(collective_id=collective_id, has_side_effects=True),
        cost_estimate=pl.CostEstimate(
            flops=0,
            bytes_accessed=60 * sum(value.size for value in values),
            transcendentals=0,
        ),
        name="plane_swap",
    )(*values)


def product_scatter_kernel(member_count, in_order, transposed, count, rows, with_grad, *refs):
    if with_grad:
        other_ref, grad_ref = refs[0], refs[2 * count + 2]
        held_other, held_grad, other_sem, grad_sem = refs[-4:]
        refs = refs[1 : 2 * count + 2] + refs[2 * count + 3 : -4]
    lefts, rights, sum_ref = refs[:count], refs[count : 2 * count], refs[2 * count]
    held_left, held_right = refs[2 * count + 1 : 2 * count + 3]
    depths = [left.shape[1] for left in lefts]
    offsets = [sum(depths[:number]) for number in range(count)]
    (
        outgoing,
        core_buffer,
        held,
        link_buffer,
        left_sem,
        right_sem,
        link_send,
        link_recv,
        core_send,
        core_recv,
    ) = refs[2 * count + 3 :]
    group = lax.axis_index("dp")
    member = lax.axis_index("fsdp")
    sibling = flip(member, 1)
    masks = plane_masks(member_count)
    steps = len(masks)
    blocks = 1 << steps
    pieces = SCATTER_PIECES
    piece = sum_ref.shape[1] // pieces

    def left_copy(number, side, subset):
        owner = sibling if side else member
        block = walk(owner, subset, masks) if in_order else subset + side * blocks
        return pltpu.make_async_copy(
            lefts[number].at[pl.ds(pl.multiple_of(block * rows, rows), rows)],
            held_left.at[
                pl.ds((side * blocks + subset) * rows, rows), pl.ds(offsets[number], depths[number])
            ],
            left_sem.at[number, side, subset],
        )

    def right_copy(number, index):
        where = pl.ds(pl.multiple_of(index * piece, piece), piece)
        source, there = rights[number], pl.ds(offsets[number], depths[number])
        if transposed:
            return pltpu.make_async_copy(
                source.at[where, pl.ds(0, depths[number])],
                held_right.at[where, there],
                right_sem.at[number, index],
            )
        return pltpu.make_async_copy(
            source.at[:, where], held_right.at[there, where], right_sem.at[number, index]
        )

    def load_side(side):
        for number in range(count):
            for subset in range(blocks):
                left_copy(number, side, subset).start()

    def wait_side(side):
        for number in range(count):
            for subset in range(blocks):
                left_copy(number, side, subset).wait()

    def load_right(index):
        for number in range(count):
            right_copy(number, index).start()

    load_side(1)
    load_right(0)
    greet(group, member, masks)

    def part(side, subset, where):
        left = held_left[pl.ds((side * blocks + subset) * rows, rows), :]
        if transposed:
            return dot_nt(left, held_right[where, :])
        return dot_nn(left, held_right[:, where])

    def columns(index):
        return pl.ds(pl.multiple_of(index * piece, piece), piece)

    def core_copy(index):
        return pltpu.make_async_remote_copy(
            outgoing.at[:, columns(index)],
            core_buffer.at[:, columns(index)],
            core_send.at[index],
            core_recv.at[index],
            device_id=(group, sibling),
            device_id_type=MESH,
        )

    def slot(step, kept):
        return sum(blocks >> (s + 1) for s in range(step)) + (kept >> (step + 1))

    def link_copy(step, subset, index):
        number = slot(step, subset & ~(1 << step))
        return pltpu.make_async_remote_copy(
            held.at[pl.ds(subset * rows, rows), columns(index)],
            link_buffer.at[pl.ds(number * rows, rows), columns(index)],
            link_send.at[number, index],
            link_recv.at[number, index],
            device_id=(group, hop(member, step, masks)),
            device_id_type=MESH,
        )

    order = sorted(range(blocks), key=lambda s: (-(s & 1), -s))

    def for_sibling(index):
        where = columns(index)
        for number in range(count):
            right_copy(number, index).wait()
        pl.when(index + 1 < pieces)(lambda: load_right(index + 1))
        for subset in range(blocks):
            outgoing[pl.ds(subset * rows, rows), where] = part(1, subset, where).astype(BF16)
        core_copy(index).start()

    def for_links(index):
        where = columns(index)
        core_copy(index).wait_recv()
        for subset in order:
            where_rows = pl.ds(subset * rows, rows)
            total = part(0, subset, where) + core_buffer[where_rows, where].astype(F32)
            if subset == 0:
                sum_ref[:, where] = total
            else:
                held[where_rows, where] = total.astype(BF16)
            if subset & 1:
                link_copy(0, subset, index).start()

    def for_both(index, carried):
        for_sibling(index)
        for_links(index - 1)
        return carried

    wait_side(1)
    load_side(0)
    for_sibling(0)
    wait_side(0)
    if with_grad:
        other_copy = pltpu.make_async_copy(other_ref, held_other, other_sem)
        other_copy.start()
    lax.fori_loop(1, pieces, for_both, 0)
    for_links(pieces - 1)
    if with_grad:
        other_copy.wait()
        units = held_grad.shape[1] // pieces
        late = 3 if steps > 1 else 0

    def grad_tile(index):
        where = pl.ds(pl.multiple_of(index * units, units), units)
        turned = dot_tn(
            held_left[:, pl.ds(pl.multiple_of(offsets[-1] + index * units, units), units)],
            held_other[...],
        )
        held_grad[:, where] = jnp.transpose(turned.astype(BF16))

    for step in range(steps):

        def one_step(index, carried, step=step):
            where = columns(index)
            if with_grad and step == 0:
                pl.when(index >= late)(lambda: grad_tile(index - late))
            if with_grad and step == 1:
                pl.when(index < late)(lambda: grad_tile(pieces - late + index))
            for kept in sorted(range(0, blocks, 2 << step), reverse=True):
                link_copy(step, kept | (1 << step), index).wait_recv()
                arrived = link_buffer[pl.ds(slot(step, kept) * rows, rows), where].astype(F32)
                if kept == 0:
                    sum_ref[:, where] += arrived
                else:
                    where_rows = pl.ds(kept * rows, rows)
                    held[where_rows, where] = (
                        held[where_rows, where].astype(F32) + arrived
                    ).astype(BF16)
                if (kept >> (step + 1)) & 1:
                    link_copy(step + 1, kept, index).start()
            return carried

        lax.fori_loop(0, pieces, one_step, 0)
        if with_grad and step == min(1, steps - 1):
            grad_copy = pltpu.make_async_copy(held_grad, grad_ref, grad_sem)
            grad_copy.start()

    def finish(index, carried):
        core_copy(index).wait_send()
        for step in range(steps):
            for kept in range(0, blocks, 2 << step):
                link_copy(step, kept | (1 << step), index).wait_send()
        return carried

    lax.fori_loop(0, pieces, finish, 0)
    if with_grad:
        grad_copy.wait()


def product_scatter(
    lefts, rights, transposed, member_count, collective_id, in_order, other=None, weight=60
):
    count = len(lefts)
    total = lefts[0].shape[0]
    width = rights[0].shape[0 if transposed else 1]
    rows = total // member_count
    blocks = 1 << len(plane_masks(member_count))
    depth = sum(left.shape[1] for left in lefts)
    scratch = (
        [
            pltpu.VMEM((total, depth), BF16),
            pltpu.VMEM((width, depth) if transposed else (depth, width), BF16),
        ]
        + [
            pltpu.VMEM((blocks * rows, width), BF16),
            pltpu.VMEM((blocks * rows, width), BF16),
            pltpu.VMEM((blocks * rows, width), BF16),
            pltpu.VMEM(((blocks - 1) * rows, width), BF16),
            pltpu.SemaphoreType.DMA((count, 2, blocks)),
            pltpu.SemaphoreType.DMA((count, SCATTER_PIECES)),
            pltpu.SemaphoreType.DMA((blocks - 1, SCATTER_PIECES)),
            pltpu.SemaphoreType.DMA((blocks - 1, SCATTER_PIECES)),
            pltpu.SemaphoreType.DMA((SCATTER_PIECES,)),
            pltpu.SemaphoreType.DMA((SCATTER_PIECES,)),
        ]
    )
    any_space = pl.BlockSpec(memory_space=pl.ANY)
    in_vmem = pl.BlockSpec(memory_space=pltpu.VMEM)
    operands = [*lefts, *rights]
    out_shape = [jax.ShapeDtypeStruct((rows, width), F32)]
    if other is not None:
        operands = [other] + operands
        grad_shape = (other.shape[1], lefts[-1].shape[1])
        out_shape.append(jax.ShapeDtypeStruct(grad_shape, BF16))
        scratch += [
            pltpu.VMEM(other.shape, BF16),
            pltpu.VMEM(grad_shape, BF16),
            pltpu.SemaphoreType.DMA,
            pltpu.SemaphoreType.DMA,
        ]
    result = pl.pallas_call(
        functools.partial(
            product_scatter_kernel,
            member_count,
            in_order,
            transposed,
            count,
            rows,
            other is not None,
        ),
        out_shape=out_shape,
        in_specs=[any_space] * len(operands),
        out_specs=[in_vmem] + [any_space] * (len(out_shape) - 1),
        scratch_shapes=scratch,
        compiler_params=pltpu.CompilerParams(
            collective_id=collective_id, has_side_effects=True, vmem_limit_bytes=VMEM_BYTES
        ),
        cost_estimate=pl.CostEstimate(
            flops=0, bytes_accessed=weight * total * width, transcendentals=0
        ),
        name="product_scatter",
    )(*operands)
    return result[0] if other is None else result


def finale_kernel(member_count, group_count, packed_ref, part_ref, arrived, sum_ref, *refs):
    near, held, far = refs[:3]
    packed_send, packed_recv, own_sem, near_send, near_recv, far_send, far_recv = refs[3:]
    group = lax.axis_index("dp")
    member = lax.axis_index("fsdp")
    shard = arrived.shape[1]
    barrier = pltpu.get_barrier_semaphore()
    for away in range(1, member_count):
        pl.semaphore_signal(
            barrier,
            inc=1,
            device_id=(group, (member + away) % member_count),
            device_id_type=MESH,
        )
    for away in range(1, group_count):
        pl.semaphore_signal(
            barrier, inc=1, device_id=((group + away) % group_count, member), device_id_type=MESH
        )
    pl.semaphore_wait(barrier, member_count + group_count - 2)

    def rows_of(target):
        return packed_ref.at[pl.ds(pl.multiple_of(target * shard, shard), shard)]

    def packed_copy(away):
        target = (member + away) % member_count
        return pltpu.make_async_remote_copy(
            rows_of(target),
            arrived.at[away],
            packed_send.at[away],
            packed_recv.at[away],
            device_id=(group, target),
            device_id_type=MESH,
        )

    def near_copy(away):
        target = (member + away) % member_count
        return pltpu.make_async_remote_copy(
            part_ref.at[target],
            near.at[away],
            near_send.at[away],
            near_recv.at[away],
            device_id=(group, target),
            device_id_type=MESH,
        )

    def far_copy(away):
        return pltpu.make_async_remote_copy(
            held,
            far.at[away],
            far_send.at[away],
            far_recv.at[away],
            device_id=((group + away) % group_count, member),
            device_id_type=MESH,
        )

    own_copy = pltpu.make_async_copy(rows_of(member), arrived.at[0], own_sem)
    for away in range(1, member_count):
        near_copy(away).start()
    for away in range(1, member_count):
        packed_copy(away).start()
    own_copy.start()
    total = part_ref[member]
    for away in range(1, member_count):
        near_copy(away).wait_recv()
        total = total + near[away]
    held[...] = total
    for away in range(1, group_count):
        far_copy(away).start()

    for away in range(1, member_count):
        packed_copy(away).wait_recv()
    own_copy.wait()
    for away in range(1, group_count):
        far_copy(away).wait_recv()
        total = total + far[away]
    sum_ref[...] = total
    for away in range(1, member_count):
        near_copy(away).wait_send()
        packed_copy(away).wait_send()
    for away in range(1, group_count):
        far_copy(away).wait_send()


def finale(packed, parts, group_count, collective_id):
    member_count, lines, lanes = parts.shape
    shard = packed.shape[0] // member_count
    in_vmem = pl.BlockSpec(memory_space=pltpu.VMEM)
    any_space = pl.BlockSpec(memory_space=pl.ANY)
    members_dma = pltpu.SemaphoreType.DMA((member_count,))
    groups_dma = pltpu.SemaphoreType.DMA((group_count,))
    return pl.pallas_call(
        functools.partial(finale_kernel, member_count, group_count),
        out_shape=[
            jax.ShapeDtypeStruct((member_count, shard, packed.shape[1]), BF16),
            jax.ShapeDtypeStruct((lines, lanes), F32),
        ],
        in_specs=[any_space, in_vmem],
        out_specs=[any_space, in_vmem],
        scratch_shapes=[
            pltpu.VMEM((member_count, lines, lanes), F32),
            pltpu.VMEM((lines, lanes), F32),
            pltpu.VMEM((group_count, lines, lanes), F32),
            members_dma,
            members_dma,
            pltpu.SemaphoreType.DMA,
            members_dma,
            members_dma,
            groups_dma,
            groups_dma,
        ],
        compiler_params=pltpu.CompilerParams(collective_id=collective_id, has_side_effects=True),
        cost_estimate=pl.CostEstimate(flops=0, bytes_accessed=40000000, transcendentals=0),
        name="finale",
    )(packed, parts)


def local_call(kernel, name, out_shape, *operands):
    in_vmem = pl.BlockSpec(memory_space=pltpu.VMEM)
    size = sum(value.size * value.dtype.itemsize for value in operands[1:])
    size += sum(value.size * value.dtype.itemsize for value in out_shape)
    return pl.pallas_call(
        kernel,
        grid_spec=pltpu.PrefetchScalarGridSpec(
            num_scalar_prefetch=1,
            in_specs=[in_vmem] * (len(operands) - 1),
            out_specs=[in_vmem] * len(out_shape),
            grid=(),
        ),
        out_shape=out_shape,
        compiler_params=pltpu.CompilerParams(vmem_limit_bytes=VMEM_BYTES),
        cost_estimate=pl.CostEstimate(flops=0, bytes_accessed=size, transcendentals=0),
        name=name,
    )(*operands)


def rows_apart(member, value, member_count, column=0):
    rows = value.shape[0] // member_count

    def kernel(member_ref, value_ref, *out_refs):
        for away, out_ref in enumerate(out_refs):
            other = member_ref[0] ^ away
            out_ref[...] = value_ref[pl.ds(pl.multiple_of(other * rows, rows), rows), column:]

    shape = jax.ShapeDtypeStruct((rows, value.shape[1] - column), value.dtype)
    return local_call(kernel, "rows_apart", [shape] * member_count, member, value)


def rows_together(member, blocks, chunks):
    rows, width = blocks[0].shape
    part = width // chunks
    count = len(blocks)

    def kernel(member_ref, *refs):
        for away in range(count):
            where = pl.ds(pl.multiple_of((member_ref[0] ^ away) * rows, rows), rows)
            for chunk in range(chunks):
                refs[count + chunk][where, :] = refs[away][:, chunk * part : (chunk + 1) * part]

    shape = jax.ShapeDtypeStruct((count * rows, part), blocks[0].dtype)
    return local_call(kernel, "rows_together", [shape] * chunks, member, *blocks)


def columns_together(member, blocks):
    rows, width = blocks[0].shape
    count = len(blocks)

    def kernel(member_ref, *refs):
        for away in range(count):
            where = pl.ds(pl.multiple_of((member_ref[0] ^ away) * width, width), width)
            refs[count][:, where] = refs[away][...]

    shape = jax.ShapeDtypeStruct((rows, count * width), blocks[0].dtype)
    return local_call(kernel, "columns_together", [shape], member, *blocks)[0]


def exchanged(blocks):
    return [blocks[0]] + [
        lax.ppermute(blocks[away], "fsdp", [(m, m ^ away) for m in range(len(blocks))])
        for away in range(1, len(blocks))
    ]


def added(left, right):
    return left.astype(F32) + right.astype(F32)


def send_to(value, member_count, partner):
    return lax.ppermute(value, "fsdp", [(m, partner(m)) for m in range(member_count)])


def hopped(step, member_count):
    masks = plane_masks(member_count)
    return lambda m: (m ^ masks[step]) if m % 2 == 0 else (m ^ masks[-1 - step])


def unit_strips(member_count, group_count, chunks, per):
    share = group_count // chunks
    for chunk in range(chunks):
        for side in range(2):
            for place in range(share):
                group = chunk * share + place
                yield chunk, side, (side * share + place) * per, group * member_count * per


def units_apart(member, gate, up, gain, member_count, group_count, chunks):
    shard, width = gate.shape
    per = width // (member_count * group_count)
    columns = 2 * group_count * per
    strips = list(unit_strips(member_count, group_count, chunks, per))
    shape = jax.ShapeDtypeStruct((shard, columns), BF16)
    if per % 128:
        scaled = [(value * gain).astype(BF16) for value in (gate, up)]

        def block(away):
            other = member[0] ^ away
            return jnp.concatenate(
                [
                    lax.dynamic_slice_in_dim(scaled[side], base + other * per, per, 1)
                    for chunk, side, column, base in strips
                ],
                axis=1,
            )

        return [block(away) for away in range(member_count)]

    def kernel(member_ref, gate_ref, up_ref, gain_ref, *out_refs):
        for away, out_ref in enumerate(out_refs):
            other = member_ref[0] ^ away
            for chunk, side, column, base in strips:
                where = pl.ds(pl.multiple_of(base + other * per, per), per)
                source = (gate_ref, up_ref)[side][:, where].astype(F32)
                column += chunk * (columns // chunks)
                out_ref[:, column : column + per] = (source * gain_ref[...]).astype(BF16)

    return local_call(kernel, "units_apart", [shape] * member_count, member, gate, up, gain)


def units_together(member, chunk_blocks, gain, down, member_count, group_count):
    chunks = len(chunk_blocks)
    shard, columns = chunk_blocks[0][0].shape
    per = columns * chunks // (2 * group_count)
    width = per * member_count * group_count
    strips = list(unit_strips(member_count, group_count, chunks, per))
    blocks = [block for group in chunk_blocks for block in group]
    if per % 128:
        results = []
        for side in range(2):
            result = jnp.zeros((shard, width), F32)
            for away in range(member_count):
                other = member[0] ^ away
                for chunk, this, column, base in strips:
                    if this == side:
                        piece = chunk_blocks[chunk][away][:, column : column + per]
                        result = lax.dynamic_update_slice_in_dim(
                            result, piece.astype(F32) * gain, base + other * per, 1
                        )
            results.append(result)
        return *results, down.astype(F32)

    def kernel(member_ref, gain_ref, down_ref, *refs):
        outs = refs[len(blocks) :]
        outs[2][...] = down_ref[...].astype(F32)
        for away in range(member_count):
            other = member_ref[0] ^ away
            for chunk, side, column, base in strips:
                where = pl.ds(pl.multiple_of(base + other * per, per), per)
                piece = refs[chunk * member_count + away][:, column : column + per]
                outs[side][:, where] = piece.astype(F32) * gain_ref[...]

    shape = jax.ShapeDtypeStruct((shard, width), F32)
    shapes = [shape, shape, jax.ShapeDtypeStruct(down.shape, F32)]
    return local_call(kernel, "units_together", shapes, member, gain, down, *blocks)


def heads_together(member, arrived, gain, heads):
    count, shard, columns = arrived.shape
    width = heads * HD
    out_width = columns - width - 2 * HD
    copies = count // KVH

    def kernel(member_ref, arrived_ref, gain_ref, query_out, key_out, value_out, out_out):
        row = lax.broadcasted_iota(jnp.int32, (width, width), 0)
        column = lax.broadcasted_iota(jnp.int32, (width, width), 1)
        source = column % HD // HALF * (HALF * heads) + column // HD * HALF + column % HALF
        order = (row == source).astype(BF16)
        pair_row = lax.broadcasted_iota(jnp.int32, (2 * HD, KVH * HD), 0)
        pair_column = lax.broadcasted_iota(jnp.int32, (2 * HD, KVH * HD), 1)
        gain_here = gain_ref[...]
        keys = jnp.zeros((shard, KVH * HD), F32)
        values = jnp.zeros((shard, KVH * HD), F32)
        for away in range(count):
            other = (member_ref[0] + count - away) % count
            where = pl.ds(pl.multiple_of(other * width, width), width)
            query_out[:, where] = dot_nn(arrived_ref[away, :, :width], order) * gain_here
            pair = arrived_ref[away, :, width : width + 2 * HD]
            first = other // copies * HD
            to_keys = (pair_column == pair_row + first) & (pair_row < HD)
            to_values = (pair_column == pair_row - HD + first) & (pair_row >= HD)
            keys = keys + dot_nn(pair, to_keys.astype(BF16))
            values = values + dot_nn(pair, to_values.astype(BF16))
            out_where = pl.ds(pl.multiple_of(other * out_width, out_width), out_width)
            out_out[:, out_where] = arrived_ref[away, :, width + 2 * HD :].astype(F32)
        key_out[...] = keys * gain_here
        value_out[...] = values * gain_here

    shapes = [
        jax.ShapeDtypeStruct((shard, size), F32)
        for size in (count * width, KVH * HD, KVH * HD, count * out_width)
    ]
    return local_call(kernel, "heads_together", shapes, member, arrived, gain)


def units_kernel(normed_ref, gradient_ref, both_ref, down_ref, hidden_ref, grad_ref):
    units = down_ref.shape[0]
    normed = normed_ref[...]
    gradient = gradient_ref[...]
    part = min(256, units)
    for first in range(0, units, part):
        where = slice(first, first + part)
        past = slice(units + first, units + first + part)
        gate = dot_nn(normed, both_ref[:, where])
        up = dot_nn(normed, both_ref[:, past])
        upstream = dot_nt(gradient, down_ref[where, :])
        sigmoid = jax.nn.sigmoid(gate)
        active = gate * sigmoid
        hidden_ref[:, where] = (active * up).astype(BF16)
        grad_ref[:, where] = (
            upstream * up * sigmoid * (1.0 + gate * (1.0 - sigmoid))
        ).astype(BF16)
        grad_ref[:, past] = (upstream * active).astype(BF16)


def hidden_units(normed, gradient, both, down, chunk):
    tokens, model = normed.shape
    units = both.shape[1] // 2
    tile = 512
    by_tile = pl.BlockSpec((tile, model), lambda i: (i, 0))
    return pl.pallas_call(
        units_kernel,
        grid=(tokens // tile,),
        in_specs=[
            by_tile,
            by_tile,
            pl.BlockSpec(both.shape, lambda i: (0, 0)),
            pl.BlockSpec((units, model), lambda i: (chunk, 0)),
        ],
        out_specs=[
            pl.BlockSpec((tile, units), lambda i: (i, 0)),
            pl.BlockSpec((tile, 2 * units), lambda i: (i, 0)),
        ],
        out_shape=[
            jax.ShapeDtypeStruct((tokens, units), BF16),
            jax.ShapeDtypeStruct((tokens, 2 * units), BF16),
        ],
        compiler_params=pltpu.CompilerParams(vmem_limit_bytes=VMEM_BYTES),
        cost_estimate=pl.CostEstimate(
            flops=6 * tokens * model * units,
            bytes_accessed=4 * tokens * model + 6 * units * model,
            transcendentals=tokens * units,
        ),
        name="hidden_units",
    )(normed, gradient, both, down)


def half_group(shape, heads):
    return (lax.broadcasted_iota(jnp.int32, shape, 1) // HALF) % heads


def full_group(shape):
    return lax.broadcasted_iota(jnp.int32, shape, 1) // HD


def spread_keys(width):
    heads = width // HD
    row = lax.broadcasted_iota(jnp.int32, (2 * HD, width), 0)
    column = lax.broadcasted_iota(jnp.int32, (2 * HD, width), 1)
    source = column // (HALF * heads) * HALF + column % HALF
    return (row == source).astype(F32)


def spread_values(width):
    row = lax.broadcasted_iota(jnp.int32, (2 * HD, width), 0)
    column = lax.broadcasted_iota(jnp.int32, (2 * HD, width), 1)
    return (row == HD + column % HD).astype(F32)


def split(value):
    high = value.astype(BF16)
    return high, (value - high.astype(F32)).astype(BF16)


def exact(value, choice):
    high, low = split(value)
    choice = choice.astype(BF16)
    return dot_nn(high, choice) + dot_nn(low, choice)


def tables(table, width):
    half = width // 2
    row = lax.broadcasted_iota(jnp.int32, (2 * HALF, half), 0)
    column = lax.broadcasted_iota(jnp.int32, (2 * HALF, half), 1) % HALF
    return (
        exact(table, row == column),
        exact(table, row == column + HALF),
    )


def turn(values, cosine, sine):
    half = cosine.shape[1]
    first = values[:, :half]
    second = values[:, half:]
    return jnp.concatenate([first * cosine - second * sine, second * cosine + first * sine], axis=1)


def forward_kernel(
    heads,
    first_ref,
    normed_ref,
    weight_ref,
    table_ref,
    start_ref,
    query_ref,
    key_ref,
    key_columns_ref,
    value_ref,
    mixed_ref,
    lse_ref,
    value_columns,
    top,
    total,
    acc,
):
    step = pl.program_id(0)
    width = heads * HD
    start = start_ref[...]
    cosine, sine = tables(table_ref[...], width)
    projected = dot_nn(normed_ref[...], weight_ref[:, : width + 2 * HD])
    query = turn(projected[:, :width], cosine, sine).astype(BF16) * ATTENTION_SCALE
    pair = projected[:, width:]
    keys_here = turn(exact(pair, spread_keys(width)), cosine, sine).astype(BF16)
    own_rows = pl.ds(pl.multiple_of(step * BLOCK, BLOCK), BLOCK)
    query_ref[...] = query
    key_ref[own_rows, :] = keys_here
    turned_keys = jnp.transpose(keys_here.astype(F32)).astype(BF16)
    key_columns_ref[:HALF, :] = turned_keys[:HALF, :]
    key_columns_ref[HALF:, :] = turned_keys[width // 2 : width // 2 + HALF, :]
    value_ref[...] = dot_nn(pair.astype(BF16), spread_values(width).astype(BF16)).astype(BF16)
    value_columns[:, own_rows] = jnp.transpose(pair)[HD:, :].astype(BF16)
    token = step * BLOCK + lax.broadcasted_iota(jnp.int32, (BLOCK, BLOCK), 1)
    within = lax.broadcasted_iota(jnp.int32, (BLOCK, BLOCK), 0)
    lane_head = half_group((BLOCK, width), heads)
    top[...] = jnp.full_like(top, MASKED)
    total[...] = jnp.zeros_like(total)
    acc[...] = jnp.zeros_like(acc)

    def one_block(block, carried):
        offset = pl.multiple_of(block * BLOCK, BLOCK)
        keys = key_ref[pl.ds(offset, BLOCK), :]
        values = value_columns[:, pl.ds(offset, BLOCK)]
        place = offset + within
        visible = (place >= start) & (place <= token)
        for head in range(heads):
            own_keys = jnp.where(lane_head == head, keys, jnp.zeros_like(keys))
            scores = jnp.where(visible, dot_nt(own_keys, query), MASKED)
            old = top[head : head + 1, :]
            new = jnp.maximum(old, jnp.max(scores, axis=0, keepdims=True))
            weights = jnp.exp(scores - new)
            fade = jnp.exp(old - new)
            top[head : head + 1, :] = new
            total[head : head + 1, :] = total[head : head + 1, :] * fade + jnp.sum(
                weights, axis=0, keepdims=True
            )
            acc[head * HD : (head + 1) * HD, :] = acc[
                head * HD : (head + 1) * HD, :
            ] * fade + dot_nn(values, weights.astype(BF16))
        return carried

    lax.fori_loop(first_ref[step], step + 1, one_block, 0)
    for head in range(heads):
        acc[head * HD : (head + 1) * HD, :] = (
            acc[head * HD : (head + 1) * HD, :] / total[head : head + 1, :]
        )
    mixed_ref[...] = jnp.transpose(acc[...]).astype(BF16)
    lse_ref[...] = top[...] + jnp.log(total[...])


def attention_forward(first, normed, weight, table, start, heads):
    tokens, model = normed.shape
    width = heads * HD
    by_block = pl.BlockSpec((BLOCK, width), lambda i, first: (i, 0))
    whole = pl.BlockSpec((tokens, width), lambda i, first: (0, 0))
    return pl.pallas_call(
        functools.partial(forward_kernel, heads),
        grid_spec=pltpu.PrefetchScalarGridSpec(
            num_scalar_prefetch=1,
            grid=(tokens // BLOCK,),
            in_specs=[
                pl.BlockSpec((BLOCK, model), lambda i, first: (i, 0)),
                pl.BlockSpec(weight.shape, lambda i, first: (0, 0)),
                pl.BlockSpec((BLOCK, 2 * HALF), lambda i, first: (i, 0)),
                pl.BlockSpec((1, BLOCK), lambda i, first: (0, i)),
            ],
            out_specs=[
                by_block,
                whole,
                pl.BlockSpec((HD, BLOCK), lambda i, first: (0, i)),
                by_block,
                by_block,
                pl.BlockSpec((heads, BLOCK), lambda i, first: (0, i)),
            ],
            scratch_shapes=[
                pltpu.VMEM((HD, tokens), BF16),
                pltpu.VMEM((heads, BLOCK), F32),
                pltpu.VMEM((heads, BLOCK), F32),
                pltpu.VMEM((width, BLOCK), F32),
            ],
        ),
        out_shape=[jax.ShapeDtypeStruct((tokens, width), BF16)] * 2
        + [jax.ShapeDtypeStruct((HD, tokens), BF16)]
        + [jax.ShapeDtypeStruct((tokens, width), BF16)] * 2
        + [jax.ShapeDtypeStruct((heads, tokens), F32)],
        compiler_params=pltpu.CompilerParams(vmem_limit_bytes=VMEM_BYTES),
        cost_estimate=pl.CostEstimate(
            flops=64 * tokens * BLOCK * width, bytes_accessed=8 * tokens * width, transcendentals=0
        ),
        name="attention_forward",
    )(first, normed, weight, table, start)


def backward_kernel(
    heads,
    first_ref,
    query_ref,
    key_ref,
    key_columns_ref,
    value_ref,
    mixed_ref,
    grad_ref,
    weight_ref,
    lse_ref,
    start_ref,
    table_ref,
    out_ref,
    weight_grad_ref,
    dquery,
    dkey,
    dvalue,
    weight_grad,
):
    step = pl.program_id(0)
    query = query_ref[...]
    grad_one = grad_ref[...]
    grad = dot_nt(grad_one, weight_ref[...]).astype(BF16)
    start = start_ref[...]
    width = query.shape[1]
    token = step * BLOCK + lax.broadcasted_iota(jnp.int32, (BLOCK, BLOCK), 1)
    within = lax.broadcasted_iota(jnp.int32, (BLOCK, BLOCK), 0)
    half_head = half_group((BLOCK, width), heads)
    full_head = full_group((BLOCK, width))
    zero = jnp.zeros((BLOCK, width), BF16)
    product = grad.astype(F32) * mixed_ref[...].astype(F32)
    chooser = (
        lax.broadcasted_iota(jnp.int32, (8, width), 0)
        == lax.broadcasted_iota(jnp.int32, (8, width), 1) // HD
    ).astype(BF16)
    high, low = split(product)
    correction = dot_nt(chooser, high) + dot_nt(chooser, low)

    @pl.when(step == 0)
    def _():
        dkey[...] = jnp.zeros_like(dkey)
        dvalue[...] = jnp.zeros_like(dvalue)
        weight_grad[...] = jnp.zeros_like(weight_grad)

    weight_grad[...] += dot_tn(mixed_ref[...], grad_one)
    dquery[...] = jnp.zeros_like(dquery)

    def one_block(block, carried):
        offset = pl.multiple_of(block * BLOCK, BLOCK)
        rows = pl.ds(offset, BLOCK)
        keys = key_ref[rows, :]
        values = value_ref[rows, :]
        key_columns = key_columns_ref[:, rows]
        place = offset + within
        visible = (place >= start) & (place <= token)
        new_key = dkey[rows, :]
        new_value = dvalue[rows, :]
        for head in range(heads):
            own_keys = jnp.where(half_head == head, keys, zero)
            own_values = jnp.where(full_head == head, values, zero)
            scores = dot_nt(own_keys, query)
            probs = jnp.where(visible, jnp.exp(scores - lse_ref[head : head + 1, :]), 0.0)
            pressure = dot_nt(own_values, grad)
            dscores = (probs * (pressure - correction[head : head + 1, :])).astype(BF16)
            new_value = new_value + dot_nn(
                probs.astype(BF16), jnp.where(full_head == head, grad, zero)
            )
            new_key = new_key + dot_nn(dscores, jnp.where(half_head == head, query, zero))
            term = dot_nn(key_columns, dscores)
            low = slice(head * HALF, (head + 1) * HALF)
            high = slice(width // 2 + head * HALF, width // 2 + (head + 1) * HALF)
            dquery[low, :] += term[:HALF]
            dquery[high, :] += term[HALF:]
        dkey[rows, :] = new_key
        dvalue[rows, :] = new_value
        return carried

    lax.fori_loop(first_ref[step], step + 1, one_block, 0)
    own_rows = pl.ds(pl.multiple_of(step * BLOCK, BLOCK), BLOCK)
    cosine, sine = tables(table_ref[own_rows, :], width)
    out_ref[own_rows, :width] = (
        turn(jnp.transpose(dquery[...]), cosine, -sine) * ATTENTION_SCALE
    ).astype(BF16)

    @pl.when(step == pl.num_programs(0) - 1)
    def _():
        def fold(block, carried):
            rows = pl.ds(pl.multiple_of(block * BLOCK, BLOCK), BLOCK)
            cosine, sine = tables(table_ref[rows, :], width)
            turned = turn(dkey[rows, :], cosine, -sine)
            out_ref[rows, width:] = (
                dot_nt(turned.astype(BF16), spread_keys(width).astype(BF16))
                + dot_nt(dvalue[rows, :].astype(BF16), spread_values(width).astype(BF16))
            ).astype(BF16)
            return carried

        lax.fori_loop(0, pl.num_programs(0), fold, 0)
        weight_grad_ref[...] = weight_grad[...].astype(BF16)


def attention_backward(
    first, query, keys, key_columns, values, mixed, grad, weight, lse, start, table
):
    tokens, width = query.shape
    model = grad.shape[1]
    heads = width // HD
    columns = width + 2 * HD
    by_block = pl.BlockSpec((BLOCK, width), lambda i, first: (i, 0))
    whole = pl.BlockSpec((tokens, width), lambda i, first: (0, 0))
    return pl.pallas_call(
        functools.partial(backward_kernel, heads),
        grid_spec=pltpu.PrefetchScalarGridSpec(
            num_scalar_prefetch=1,
            grid=(tokens // BLOCK,),
            in_specs=[
                by_block,
                whole,
                pl.BlockSpec((HD, tokens), lambda i, first: (0, 0)),
                whole,
                by_block,
                pl.BlockSpec((BLOCK, model), lambda i, first: (i, 0)),
                pl.BlockSpec((width, model), lambda i, first: (0, 0)),
                pl.BlockSpec((heads, BLOCK), lambda i, first: (0, i)),
                pl.BlockSpec((1, BLOCK), lambda i, first: (0, i)),
                pl.BlockSpec((tokens, 2 * HALF), lambda i, first: (0, 0)),
            ],
            out_specs=[
                pl.BlockSpec((tokens, columns), lambda i, first: (0, 0)),
                pl.BlockSpec((width, model), lambda i, first: (0, 0)),
            ],
            scratch_shapes=[
                pltpu.VMEM((width, BLOCK), F32),
                pltpu.VMEM((tokens, width), F32),
                pltpu.VMEM((tokens, width), F32),
                pltpu.VMEM((width, model), F32),
            ],
        ),
        out_shape=[
            jax.ShapeDtypeStruct((tokens, columns), BF16),
            jax.ShapeDtypeStruct((width, model), BF16),
        ],
        compiler_params=pltpu.CompilerParams(vmem_limit_bytes=VMEM_BYTES),
        cost_estimate=pl.CostEstimate(
            flops=0, bytes_accessed=tokens * width, transcendentals=0
        ),
        name="attention_backward",
    )(first, query, keys, key_columns, values, mixed, grad, weight, lse, start, table)


def projection_grad(normed, grad, out_grad):
    tokens, model = normed.shape
    columns, more = grad.shape[1], out_grad.shape[1]
    tile = 512

    def kernel(normed_ref, grad_ref, out_grad_ref, result_ref):
        result_ref[:, :columns] = dot_tn(normed_ref[...], grad_ref[...]).astype(BF16)
        result_ref[:, columns:] = out_grad_ref[...]

    return pl.pallas_call(
        kernel,
        grid=(model // tile,),
        in_specs=[
            pl.BlockSpec((tokens, tile), lambda i: (0, i)),
            pl.BlockSpec((tokens, columns), lambda i: (0, 0)),
            pl.BlockSpec((tile, more), lambda i: (i, 0)),
        ],
        out_specs=pl.BlockSpec((tile, columns + more), lambda i: (i, 0)),
        out_shape=jax.ShapeDtypeStruct((model, columns + more), BF16),
        compiler_params=pltpu.CompilerParams(vmem_limit_bytes=VMEM_BYTES),
        cost_estimate=pl.CostEstimate(
            flops=2 * tokens * model * columns, bytes_accessed=2 * tokens * model, transcendentals=0
        ),
        name="projection_grad",
    )(normed, grad, out_grad)


def token_starts(lengths_row, group_tokens):
    count = lengths_row.shape[0]
    order = jnp.arange(count, dtype=jnp.int32)
    finish = jnp.sum(jnp.where(order[None, :] <= order[:, None], lengths_row[None, :], 0), axis=1)
    place = jnp.arange(group_tokens, dtype=jnp.int32)
    passed = place[:, None] >= finish[None, :]
    return jnp.max(jnp.where(passed, finish[None, :], 0), axis=1), place


def inverse_norm(values):
    return lax.rsqrt(jnp.mean(values * values, axis=1, keepdims=True) + EPSILON)


def after(value, *earlier):
    return lax.optimization_barrier((value, *earlier))[0]


def sum_over_groups(value):
    return lax.psum_scatter(value, "dp", scatter_dimension=0, tiled=True)


def gather_groups(value):
    return lax.all_gather(value, "dp", axis=0, tiled=True)


def body(
    tokens,
    cotangent,
    query_weight,
    key_weight,
    value_weight,
    output_weight,
    gate_weight,
    up_weight,
    down_weight,
    attention_gain,
    feedforward_gain,
    lengths,
):
    members = lax.axis_size("fsdp")
    groups = lax.axis_size("dp")
    rows, model = tokens.shape
    group_tokens = rows * members
    shard = query_weight.shape[0]
    heads = NH // members
    width = heads * HD
    columns = width + 2 * HD
    copies = members // KVH
    out_columns = model // members
    down_rows = down_weight.shape[0]
    units = groups * down_rows // CHUNKS
    gain_one = attention_gain.astype(F32)[:, None]
    gain_two = feedforward_gain.astype(F32)[:, None]
    member = lax.axis_index("fsdp").astype(jnp.int32)[None]

    scaled_query = (query_weight * gain_one).astype(BF16)
    scaled_key = (key_weight * gain_one).astype(BF16)
    scaled_value = (value_weight * gain_one).astype(BF16)
    packed_in = jnp.concatenate(
        [
            scaled_query.reshape(shard, members, heads, 2, HALF)
            .transpose(1, 0, 3, 2, 4)
            .reshape(members, shard, width),
            jnp.repeat(
                scaled_key.reshape(shard, KVH, HD).transpose(1, 0, 2), copies, axis=0
            ),
            jnp.repeat(
                scaled_value.reshape(shard, KVH, HD).transpose(1, 0, 2), copies, axis=0
            ),
            output_weight.reshape(shard, members, out_columns).transpose(1, 0, 2),
        ],
        axis=2,
    )
    [packed_in] = plane_swap([packed_in], members, 1)
    packed_in = packed_in.reshape(members * shard, columns + out_columns)
    inputs = tokens.astype(F32)
    inverse_one = inverse_norm(inputs)
    start, place = token_starts(lengths[0], group_tokens)
    first = start[::BLOCK] // BLOCK
    frequency = ROPE_BASE ** (-(2.0 * jnp.arange(HALF, dtype=F32)) / HD)
    angles = (place - start).astype(F32)[:, None] * frequency[None, :]
    table = jnp.concatenate([jnp.cos(angles), jnp.sin(angles)], axis=1)
    start = start[None, :]

    gate_up = exchanged(
        units_apart(
            member, after(gate_weight, packed_in), up_weight, gain_two, members, groups, CHUNKS
        )
    )
    packed = gather_groups(packed_in)
    down_all = gather_groups(down_weight)
    normed_one = plane_gather(
        after((inputs * inverse_one).astype(BF16), packed_in), members, 0, True
    )
    upstream = cotangent.astype(F32)
    grad_two = (RESIDUAL_SCALE * upstream).astype(BF16)
    grad_two, down_all, table, first, start, _ = lax.optimization_barrier(
        (grad_two, down_all, table, first, start, normed_one)
    )
    grad_two = plane_gather(grad_two, members, 9, False)
    gate_up, grad_two = lax.optimization_barrier((gate_up, grad_two))
    gate_up_parts = rows_together(member, gate_up, CHUNKS)
    gate_up_chunks = [gather_groups(part) for part in gate_up_parts]
    packed, gate_up_parts = lax.optimization_barrier((packed, gate_up_parts))

    out_blocks = exchanged(rows_apart(member, packed, members, columns))
    query, keys, key_columns, values, mixed, lse = attention_forward(
        first, normed_one, packed, table, start, heads
    )
    mixed_then, out_blocks = lax.optimization_barrier((mixed, out_blocks))
    out_piece = columns_together(member, out_blocks)
    branch_one = product_scatter([mixed_then], [out_piece], False, members, 2, True)
    residual = inputs + RESIDUAL_SCALE * branch_one

    inverse_two = inverse_norm(residual)
    normed_two = plane_gather((residual * inverse_two).astype(BF16), members, 3, False)
    fused = group_tokens <= 2048
    hiddens = []
    grad_boths = []
    gate_up_grads = []
    for chunk in range(CHUNKS):
        both_weight = gate_up_chunks[chunk]
        hidden, grad_both = hidden_units(normed_two, grad_two, both_weight, down_all, chunk)
        hiddens.append(hidden)
        grad_boths.append(grad_both)
        if chunk < CHUNKS - 1 or not fused:
            gate_up_grad = dot_tn(normed_two, grad_both).astype(BF16)
            gate_up_grads.append(sum_over_groups(gate_up_grad))
            normed_two, grad_two, hiddens, grad_boths, _ = lax.optimization_barrier(
                (normed_two, grad_two, hiddens, grad_boths, gate_up_grad)
            )
    if fused:
        weighted_two, gate_up_grad = product_scatter(
            grad_boths, gate_up_chunks, True, members, 4, False, normed_two
        )
        gate_up_grads.append(sum_over_groups(gate_up_grad))
    else:
        weighted_two = product_scatter(grad_boths, gate_up_chunks, True, members, 4, False)
    grad_residual = (
        upstream
        + inverse_two * weighted_two
        - residual * inverse_two**3 * jnp.mean(weighted_two * residual, axis=1, keepdims=True)
    )
    gain_term_two = jnp.sum(weighted_two * residual * inverse_two, axis=0)

    grad_one, down_grad, out_high, out_kept = plane_gather(
        (RESIDUAL_SCALE * grad_residual).astype(BF16),
        members,
        5,
        True,
        (hiddens, grad_two, down_all),
    )
    down_grad = sum_over_groups(down_grad)
    gate_up_grads[0] = exchanged(
        rows_apart(member, after(gate_up_grads[0], grad_one), members)
    )
    steps = len(plane_masks(members))
    half_rows = group_tokens // 4
    out_sent = send_to(out_high, members, hopped(steps - 1, members))
    grad_projected, out_grad = attention_backward(
        first, query, keys, key_columns, values, mixed, grad_one, out_piece, lse, start, table
    )
    out_grad = lax.all_to_all(out_grad, "fsdp", split_axis=1, concat_axis=0, tiled=True)
    packed_grad = projection_grad(normed_one, grad_projected, out_grad)
    gate_up_grads[1:] = [
        exchanged(rows_apart(member, part, members))
        for part in after(gate_up_grads[1:], grad_projected)
    ]
    grad_projected, packed_grad, gate_up_grads[0], out_sent, out_kept = lax.optimization_barrier(
        (grad_projected, packed_grad, gate_up_grads[0], out_sent, out_kept)
    )
    for step in reversed(range(steps - 1)):
        half_rows //= 2
        out_next = added(out_kept[half_rows:], out_sent[half_rows:]).astype(BF16)
        out_kept = added(out_kept[:half_rows], out_sent[:half_rows])
        if step:
            out_kept = out_kept.astype(BF16)
        out_sent = send_to(out_next, members, hopped(step, members))
    packed_grad = sum_over_groups(packed_grad)
    weighted_one = product_scatter([grad_projected], [packed], True, members, 6, True, weight=1)
    weighted_one, down_grad = lax.optimization_barrier((weighted_one, down_grad))
    grad_inputs = (
        grad_residual
        + inverse_one * weighted_one
        - inputs * inverse_one**3 * jnp.mean(weighted_one * inputs, axis=1, keepdims=True)
    )
    gain_term_one = jnp.sum(weighted_one * inputs * inverse_one, axis=0)

    gains = jnp.stack(
        [
            gain_term_one.reshape(groups, members, shard),
            gain_term_two.reshape(groups, members, shard),
        ],
        axis=2,
    ).reshape(groups, members, 2 * shard)
    gains = jnp.pad(
        gains.transpose(1, 0, 2), ((0, 0), (0, (-groups) % 8), (0, (-2 * shard) % 128))
    )
    output = (residual + RESIDUAL_SCALE * added(out_kept, out_sent)).astype(BF16)

    gate_grad, up_grad, down_grad = units_together(
        member, after(gate_up_grads, weighted_one), gain_two, down_grad, members, groups
    )
    arrived, gains = finale(packed_grad, gains, groups, 8)
    query_grad, key_grad, value_grad, out_grad = heads_together(member, arrived, gain_one, heads)
    gains = lax.dynamic_slice_in_dim(gains, lax.axis_index("dp"), 1, 0)[0, : 2 * shard]
    gains = gains.reshape(2, shard)
    return (
        output,
        grad_inputs.astype(BF16),
        query_grad,
        key_grad,
        value_grad,
        out_grad,
        gate_grad,
        up_grad,
        down_grad,
        gains[0] / gain_one[:, 0],
        gains[1] / gain_two[:, 0],
    )


def solution(mesh):
    by_rows = P(("dp", "fsdp"), None)
    by_entries = P(("dp", "fsdp"))
    return jax.shard_map(
        body,
        mesh=mesh,
        in_specs=(by_rows,) * 9 + (by_entries,) * 2 + (P("dp", None),),
        out_specs=(by_rows,) * 9 + (by_entries,) * 2,
        check_vma=False,
    )
```

```python
import functools

import jax
import jax.numpy as jnp
from jax import lax
from jax.experimental import pallas as pl
from jax.experimental.pallas import tpu as pltpu
from jax.sharding import PartitionSpec as P

NH = 32
KVH = 8
HD = 64
HALF = HD // 2

EPSILON = 1e-05
RESIDUAL_SCALE = 0.22
ATTENTION_SCALE = 0.015625
ROPE_BASE = 10000000.0
MASKED = -1e30
BLOCK = 256
CHUNKS = 2
PIECES = 4
SCATTER_PIECES = 8
VMEM_BYTES = 58 * 1024 * 1024
MESH = pl.DeviceIdType.MESH
BF16 = jnp.bfloat16
F32 = jnp.float32


def dot_nn(left, right):
    return jnp.dot(left, right, preferred_element_type=F32)


def dot_nt(left, right):
    return lax.dot_general(left, right, (((1,), (1,)), ((), ())), preferred_element_type=F32)


def dot_tn(left, right):
    return lax.dot_general(left, right, (((0,), (0,)), ((), ())), preferred_element_type=F32)


def flip(index, mask):
    return index + mask * (1 - 2 * ((index // mask) % 2))


def plane_masks(member_count):
    masks = []
    mask = 2
    while mask < member_count:
        masks.append(mask)
        mask *= 2
    return masks


def hop(index, step, masks):
    core = index % 2
    return (1 - core) * flip(index, masks[step]) + core * flip(index, masks[-1 - step])


def walk(index, subset, masks):
    for step in range(len(masks)):
        if (subset >> step) & 1:
            index = hop(index, step, masks)
    return index


def greet(group, member, masks):
    barrier = pltpu.get_barrier_semaphore()
    partners = [hop(member, step, masks) for step in range(len(masks))] + [flip(member, 1)]
    for partner in partners:
        pl.semaphore_signal(barrier, inc=1, device_id=(group, partner), device_id_type=MESH)
    pl.semaphore_wait(barrier, len(partners))


def gather_kernel(member_count, in_order, count, own_ref, *refs):
    operands = refs[: count + 2] if count else ()
    refs = refs[len(operands) :]
    extra = 4 if count else 1
    all_ref, results, refs = refs[0], refs[1:extra], refs[extra:]
    link_send, link_recv, core_send, core_recv, local_sem = refs[:5]
    group = lax.axis_index("dp")
    member = lax.axis_index("fsdp")
    masks = plane_masks(member_count)
    steps = len(masks)
    rows = own_ref.shape[0]
    piece = rows // PIECES
    greet(group, member, masks)

    blocks = 1 << steps

    def place(owner, subset, side, part):
        block = walk(owner, subset, masks) if in_order else subset + side * blocks
        return all_ref.at[pl.ds(pl.multiple_of(block * rows + part * piece, piece), piece)]

    def link_copy(step, subset, part):
        number = (1 << step) - 1 + subset
        here = place(member, subset, 0, part)
        there = here if in_order else place(member, subset | (1 << step), 0, part)
        return pltpu.make_async_remote_copy(
            own_ref.at[pl.ds(part * piece, piece)] if subset == 0 else here,
            there,
            link_send.at[number, part],
            link_recv.at[number, part],
            device_id=(group, hop(member, step, masks)),
            device_id_type=MESH,
        )

    def core_copy(subset, part):
        here = place(member, subset, 0, part)
        there = here if in_order else place(member, subset, 1, part)
        return pltpu.make_async_remote_copy(
            own_ref.at[pl.ds(part * piece, piece)] if subset == 0 else here,
            there,
            core_send.at[subset, part],
            core_recv.at[subset, part],
            device_id=(group, flip(member, 1)),
            device_id_type=MESH,
        )

    for part in range(PIECES):
        for step in range(steps):
            link_copy(step, 0, part).start()
    first = pl.multiple_of(member * rows, rows) if in_order else 0
    keep = pltpu.make_async_copy(own_ref, all_ref.at[pl.ds(first, rows)], local_sem)
    keep.start()
    for part in range(PIECES):
        core_copy(0, part).start()
    tiles = []
    if count:
        hidden, gradient, down, down_grad, out_sibling, out_own, turned, out_arrived = refs[5:13]
        load_sem, store_sem, out_send, out_recv = refs[13:]
        units = operands[0].shape[1]
        targets = [hidden.at[:, pl.ds(number * units, units)] for number in range(count)]
        loads = [
            pltpu.make_async_copy(source, target, load_sem.at[number])
            for number, (source, target) in enumerate(zip(operands, (*targets, gradient, down)))
        ]
        half = out_own.shape[0]
        finished = (
            down_grad,
            out_own.at[pl.ds(half // 2, half // 2)],
            out_own.at[pl.ds(0, half // 2)],
        )
        stores = [
            pltpu.make_async_copy(source, target, store_sem.at[number])
            for number, (source, target) in enumerate(zip(finished, results))
        ]
        for load in loads:
            load.start()
        width = 256

        def out_copy(column):
            where = pl.ds(column, width)
            return pltpu.make_async_remote_copy(
                out_sibling.at[:, where],
                out_arrived.at[:, where],
                out_send.at[column // width],
                out_recv.at[column // width],
                device_id=(group, flip(member, 1)),
                device_id_type=MESH,
            )

        def sibling_tile(column):
            out_sibling[:, column : column + width] = dot_nn(
                hidden[half:, :], down[:, column : column + width]
            ).astype(BF16)
            out_copy(column).start()

        def own_tile(column):
            product = dot_nn(hidden[:half, :], down[:, column : column + width])
            out_copy(column).wait()
            out_own[:, column : column + width] = (
                product + out_arrived[:, column : column + width].astype(F32)
            ).astype(BF16)

        def turn_tile(number):
            part = slice(number * units, (number + 1) * units)
            turned[part, :] = jnp.transpose(hidden[:, part])

        def grad_tile(column):
            down_grad[:, column : column + width] = dot_nn(
                turned[...], gradient[:, column : column + width]
            ).astype(BF16)

        for load in loads[:count] + loads[count + 1 :]:
            tiles.append(load.wait)
        starts = range(0, down.shape[1], width)
        for column in starts:
            tiles.append(functools.partial(sibling_tile, column))
        for column in starts:
            tiles.append(functools.partial(own_tile, column))
        tiles += [stores[1].start, stores[2].start]
        tiles.append(loads[count].wait)
        for number in range(count):
            tiles.append(functools.partial(turn_tile, number))
        for column in starts:
            tiles.append(functools.partial(grad_tile, column))
        tiles.append(stores[0].start)
    shares = [4] * PIECES + [2, 1, 0, 0] * max(1, steps - 1)
    shares = shares[: steps * PIECES]
    ends = [-(-len(tiles) * sum(shares[: n + 1]) // sum(shares)) for n in range(len(shares))]

    turn = 0
    for step in range(steps):
        for part in range(PIECES):
            for subset in range(1 << step):
                link_copy(step, subset, part).wait_recv()
                arrived = subset | (1 << step)
                for later in range(step + 1, steps):
                    link_copy(later, arrived, part).start()
                core_copy(arrived, part).start()
            for run in tiles[ends[turn - 1] if turn else 0 : ends[turn]]:
                run()
            turn += 1
    for part in range(PIECES):
        for subset in range(1 << steps):
            core_copy(subset, part).wait()
    for part in range(PIECES):
        for step in range(steps):
            for subset in range(1 << step):
                link_copy(step, subset, part).wait_send()
    keep.wait()
    if count:
        for store in stores:
            store.wait()


def plane_gather(own, member_count, collective_id, in_order, extras=None):
    rows, width = own.shape
    steps = len(plane_masks(member_count))
    blocks = 1 << steps
    total = member_count * rows
    any_space = pl.BlockSpec(memory_space=pl.ANY)
    scratch = [
        pltpu.SemaphoreType.DMA((blocks - 1, PIECES)),
        pltpu.SemaphoreType.DMA((blocks - 1, PIECES)),
        pltpu.SemaphoreType.DMA((blocks, PIECES)),
        pltpu.SemaphoreType.DMA((blocks, PIECES)),
        pltpu.SemaphoreType.DMA,
    ]
    operands = [own]
    out_shape = [jax.ShapeDtypeStruct((total, width), own.dtype)]
    count = 0
    if extras:
        hiddens, gradient, down = extras
        count = len(hiddens)
        operands += [*hiddens, gradient, down]
        units = down.shape[0]
        scratch += [
            pltpu.VMEM((total, units), BF16),
            pltpu.VMEM(gradient.shape, BF16),
            pltpu.VMEM(down.shape, BF16),
        ]
        out_shape += [
            jax.ShapeDtypeStruct((down.shape[0], gradient.shape[1]), BF16),
            jax.ShapeDtypeStruct((total // 4, down.shape[1]), BF16),
            jax.ShapeDtypeStruct((total // 4, down.shape[1]), BF16),
        ]
        out_half = pltpu.VMEM((total // 2, down.shape[1]), BF16)
        scratch += [
            pltpu.VMEM(out_shape[1].shape, BF16),
            out_half,
            out_half,
            pltpu.VMEM((units, total), BF16),
            out_half,
            pltpu.SemaphoreType.DMA((count + 2,)),
            pltpu.SemaphoreType.DMA((3,)),
            pltpu.SemaphoreType.DMA((down.shape[1] // 256,)),
            pltpu.SemaphoreType.DMA((down.shape[1] // 256,)),
        ]
    result = pl.pallas_call(
        functools.partial(gather_kernel, member_count, in_order, count),
        out_shape=out_shape,
        in_specs=[any_space] * len(operands),
        out_specs=[any_space] * len(out_shape),
        scratch_shapes=scratch,
        compiler_params=pltpu.CompilerParams(
            collective_id=collective_id, has_side_effects=True, vmem_limit_bytes=VMEM_BYTES
        ),
        cost_estimate=pl.CostEstimate(
            flops=0, bytes_accessed=(1 if extras else 60) * total * width, transcendentals=0
        ),
        name="plane_gather",
    )(*operands)
    return result if extras else result[0]


def swap_kernel(member_count, count, *refs):
    sources, targets = refs[:count], refs[count : 2 * count]
    send_sem, recv_sem, local_sem = refs[2 * count :]
    group = lax.axis_index("dp")
    member = lax.axis_index("fsdp")
    barrier = pltpu.get_barrier_semaphore()
    for away in range(1, member_count):
        pl.semaphore_signal(
            barrier,
            inc=1,
            device_id=(group, (member + away) % member_count),
            device_id_type=MESH,
        )
    pl.semaphore_wait(barrier, member_count - 1)

    def copy(number, away):
        target = (member + away) % member_count
        return pltpu.make_async_remote_copy(
            sources[number].at[target],
            targets[number].at[member],
            send_sem.at[number, away],
            recv_sem.at[number, away],
            device_id=(group, target),
            device_id_type=MESH,
        )

    def keep(number):
        return pltpu.make_async_copy(
            sources[number].at[member], targets[number].at[member], local_sem.at[number]
        )

    for number in range(count):
        for away in range(1, member_count):
            copy(number, away).start()
        keep(number).start()
    for number in range(count):
        for away in range(1, member_count):
            copy(number, away).wait()
        keep(number).wait()


def plane_swap(values, member_count, collective_id):
    count = len(values)
    any_space = pl.BlockSpec(memory_space=pl.ANY)
    return pl.pallas_call(
        functools.partial(swap_kernel, member_count, count),
        out_shape=[jax.ShapeDtypeStruct(value.shape, value.dtype) for value in values],
        in_specs=[any_space] * count,
        out_specs=[any_space] * count,
        scratch_shapes=[
            pltpu.SemaphoreType.DMA((count, member_count)),
            pltpu.SemaphoreType.DMA((count, member_count)),
            pltpu.SemaphoreType.DMA((count,)),
        ],
        compiler_params=pltpu.CompilerParams(collective_id=collective_id, has_side_effects=True),
        cost_estimate=pl.CostEstimate(
            flops=0,
            bytes_accessed=60 * sum(value.size for value in values),
            transcendentals=0,
        ),
        name="plane_swap",
    )(*values)


def product_scatter_kernel(member_count, in_order, transposed, count, rows, with_grad, *refs):
    if with_grad:
        other_ref, grad_ref = refs[0], refs[2 * count + 2]
        held_other, held_grad, other_sem, grad_sem = refs[-4:]
        refs = refs[1 : 2 * count + 2] + refs[2 * count + 3 : -4]
    lefts, rights, sum_ref = refs[:count], refs[count : 2 * count], refs[2 * count]
    held_left, held_right = refs[2 * count + 1 : 2 * count + 3]
    depths = [left.shape[1] for left in lefts]
    offsets = [sum(depths[:number]) for number in range(count)]
    (
        outgoing,
        core_buffer,
        held,
        link_buffer,
        left_sem,
        right_sem,
        link_send,
        link_recv,
        core_send,
        core_recv,
    ) = refs[2 * count + 3 :]
    group = lax.axis_index("dp")
    member = lax.axis_index("fsdp")
    sibling = flip(member, 1)
    masks = plane_masks(member_count)
    steps = len(masks)
    blocks = 1 << steps
    pieces = SCATTER_PIECES
    piece = sum_ref.shape[1] // pieces

    def left_copy(number, side, subset):
        owner = sibling if side else member
        block = walk(owner, subset, masks) if in_order else subset + side * blocks
        return pltpu.make_async_copy(
            lefts[number].at[pl.ds(pl.multiple_of(block * rows, rows), rows)],
            held_left.at[
                pl.ds((side * blocks + subset) * rows, rows), pl.ds(offsets[number], depths[number])
            ],
            left_sem.at[number, side, subset],
        )

    def right_copy(number, index):
        where = pl.ds(pl.multiple_of(index * piece, piece), piece)
        source, there = rights[number], pl.ds(offsets[number], depths[number])
        if transposed:
            return pltpu.make_async_copy(
                source.at[where, pl.ds(0, depths[number])],
                held_right.at[where, there],
                right_sem.at[number, index],
            )
        return pltpu.make_async_copy(
            source.at[:, where], held_right.at[there, where], right_sem.at[number, index]
        )

    def load_side(side):
        for number in range(count):
            for subset in range(blocks):
                left_copy(number, side, subset).start()

    def wait_side(side):
        for number in range(count):
            for subset in range(blocks):
                left_copy(number, side, subset).wait()

    def load_right(index):
        for number in range(count):
            right_copy(number, index).start()

    load_side(1)
    load_right(0)
    greet(group, member, masks)

    def part(side, subset, where):
        left = held_left[pl.ds((side * blocks + subset) * rows, rows), :]
        if transposed:
            return dot_nt(left, held_right[where, :])
        return dot_nn(left, held_right[:, where])

    def columns(index):
        return pl.ds(pl.multiple_of(index * piece, piece), piece)

    def core_copy(index):
        return pltpu.make_async_remote_copy(
            outgoing.at[:, columns(index)],
            core_buffer.at[:, columns(index)],
            core_send.at[index],
            core_recv.at[index],
            device_id=(group, sibling),
            device_id_type=MESH,
        )

    def slot(step, kept):
        return sum(blocks >> (s + 1) for s in range(step)) + (kept >> (step + 1))

    def link_copy(step, subset, index):
        number = slot(step, subset & ~(1 << step))
        return pltpu.make_async_remote_copy(
            held.at[pl.ds(subset * rows, rows), columns(index)],
            link_buffer.at[pl.ds(number * rows, rows), columns(index)],
            link_send.at[number, index],
            link_recv.at[number, index],
            device_id=(group, hop(member, step, masks)),
            device_id_type=MESH,
        )

    order = sorted(range(blocks), key=lambda s: (-(s & 1), -s))

    def for_sibling(index):
        where = columns(index)
        for number in range(count):
            right_copy(number, index).wait()
        pl.when(index + 1 < pieces)(lambda: load_right(index + 1))
        for subset in range(blocks):
            outgoing[pl.ds(subset * rows, rows), where] = part(1, subset, where).astype(BF16)
        core_copy(index).start()

    def for_links(index):
        where = columns(index)
        core_copy(index).wait_recv()
        for subset in order:
            where_rows = pl.ds(subset * rows, rows)
            total = part(0, subset, where) + core_buffer[where_rows, where].astype(F32)
            if subset == 0:
                sum_ref[:, where] = total
            else:
                held[where_rows, where] = total.astype(BF16)
            if subset & 1:
                link_copy(0, subset, index).start()

    def for_both(index, carried):
        for_sibling(index)
        for_links(index - 1)
        return carried

    wait_side(1)
    load_side(0)
    for_sibling(0)
    wait_side(0)
    if with_grad:
        other_copy = pltpu.make_async_copy(other_ref, held_other, other_sem)
        other_copy.start()
    lax.fori_loop(1, pieces, for_both, 0)
    for_links(pieces - 1)
    if with_grad:
        other_copy.wait()
        units = held_grad.shape[1] // pieces
        late = 3 if steps > 1 else 0

    def grad_tile(index):
        where = pl.ds(pl.multiple_of(index * units, units), units)
        turned = dot_tn(
            held_left[:, pl.ds(pl.multiple_of(offsets[-1] + index * units, units), units)],
            held_other[...],
        )
        held_grad[:, where] = jnp.transpose(turned.astype(BF16))

    for step in range(steps):

        def one_step(index, carried, step=step):
            where = columns(index)
            if with_grad and step == 0:
                pl.when(index >= late)(lambda: grad_tile(index - late))
            if with_grad and step == 1:
                pl.when(index < late)(lambda: grad_tile(pieces - late + index))
            for kept in sorted(range(0, blocks, 2 << step), reverse=True):
                link_copy(step, kept | (1 << step), index).wait_recv()
                arrived = link_buffer[pl.ds(slot(step, kept) * rows, rows), where].astype(F32)
                if kept == 0:
                    sum_ref[:, where] += arrived
                else:
                    where_rows = pl.ds(kept * rows, rows)
                    held[where_rows, where] = (
                        held[where_rows, where].astype(F32) + arrived
                    ).astype(BF16)
                if (kept >> (step + 1)) & 1:
                    link_copy(step + 1, kept, index).start()
            return carried

        lax.fori_loop(0, pieces, one_step, 0)
        if with_grad and step == min(1, steps - 1):
            grad_copy = pltpu.make_async_copy(held_grad, grad_ref, grad_sem)
            grad_copy.start()

    def finish(index, carried):
        core_copy(index).wait_send()
        for step in range(steps):
            for kept in range(0, blocks, 2 << step):
                link_copy(step, kept | (1 << step), index).wait_send()
        return carried

    lax.fori_loop(0, pieces, finish, 0)
    if with_grad:
        grad_copy.wait()


def product_scatter(
    lefts, rights, transposed, member_count, collective_id, in_order, other=None, weight=60
):
    count = len(lefts)
    total = lefts[0].shape[0]
    width = rights[0].shape[0 if transposed else 1]
    rows = total // member_count
    blocks = 1 << len(plane_masks(member_count))
    depth = sum(left.shape[1] for left in lefts)
    scratch = (
        [
            pltpu.VMEM((total, depth), BF16),
            pltpu.VMEM((width, depth) if transposed else (depth, width), BF16),
        ]
        + [
            pltpu.VMEM((blocks * rows, width), BF16),
            pltpu.VMEM((blocks * rows, width), BF16),
            pltpu.VMEM((blocks * rows, width), BF16),
            pltpu.VMEM(((blocks - 1) * rows, width), BF16),
            pltpu.SemaphoreType.DMA((count, 2, blocks)),
            pltpu.SemaphoreType.DMA((count, SCATTER_PIECES)),
            pltpu.SemaphoreType.DMA((blocks - 1, SCATTER_PIECES)),
            pltpu.SemaphoreType.DMA((blocks - 1, SCATTER_PIECES)),
            pltpu.SemaphoreType.DMA((SCATTER_PIECES,)),
            pltpu.SemaphoreType.DMA((SCATTER_PIECES,)),
        ]
    )
    any_space = pl.BlockSpec(memory_space=pl.ANY)
    in_vmem = pl.BlockSpec(memory_space=pltpu.VMEM)
    operands = [*lefts, *rights]
    out_shape = [jax.ShapeDtypeStruct((rows, width), F32)]
    if other is not None:
        operands = [other] + operands
        grad_shape = (other.shape[1], lefts[-1].shape[1])
        out_shape.append(jax.ShapeDtypeStruct(grad_shape, BF16))
        scratch += [
            pltpu.VMEM(other.shape, BF16),
            pltpu.VMEM(grad_shape, BF16),
            pltpu.SemaphoreType.DMA,
            pltpu.SemaphoreType.DMA,
        ]
    result = pl.pallas_call(
        functools.partial(
            product_scatter_kernel,
            member_count,
            in_order,
            transposed,
            count,
            rows,
            other is not None,
        ),
        out_shape=out_shape,
        in_specs=[any_space] * len(operands),
        out_specs=[in_vmem] + [any_space] * (len(out_shape) - 1),
        scratch_shapes=scratch,
        compiler_params=pltpu.CompilerParams(
            collective_id=collective_id, has_side_effects=True, vmem_limit_bytes=VMEM_BYTES
        ),
        cost_estimate=pl.CostEstimate(
            flops=0, bytes_accessed=weight * total * width, transcendentals=0
        ),
        name="product_scatter",
    )(*operands)
    return result[0] if other is None else result


def finale_kernel(member_count, group_count, packed_ref, part_ref, arrived, sum_ref, *refs):
    near, held, far = refs[:3]
    packed_send, packed_recv, own_sem, near_send, near_recv, far_send, far_recv = refs[3:]
    group = lax.axis_index("dp")
    member = lax.axis_index("fsdp")
    shard = arrived.shape[1]
    barrier = pltpu.get_barrier_semaphore()
    for away in range(1, member_count):
        pl.semaphore_signal(
            barrier,
            inc=1,
            device_id=(group, (member + away) % member_count),
            device_id_type=MESH,
        )
    for away in range(1, group_count):
        pl.semaphore_signal(
            barrier, inc=1, device_id=((group + away) % group_count, member), device_id_type=MESH
        )
    pl.semaphore_wait(barrier, member_count + group_count - 2)

    def rows_of(target):
        return packed_ref.at[pl.ds(pl.multiple_of(target * shard, shard), shard)]

    def packed_copy(away):
        target = (member + away) % member_count
        return pltpu.make_async_remote_copy(
            rows_of(target),
            arrived.at[away],
            packed_send.at[away],
            packed_recv.at[away],
            device_id=(group, target),
            device_id_type=MESH,
        )

    def near_copy(away):
        target = (member + away) % member_count
        return pltpu.make_async_remote_copy(
            part_ref.at[target],
            near.at[away],
            near_send.at[away],
            near_recv.at[away],
            device_id=(group, target),
            device_id_type=MESH,
        )

    def far_copy(away):
        return pltpu.make_async_remote_copy(
            held,
            far.at[away],
            far_send.at[away],
            far_recv.at[away],
            device_id=((group + away) % group_count, member),
            device_id_type=MESH,
        )

    own_copy = pltpu.make_async_copy(rows_of(member), arrived.at[0], own_sem)
    for away in range(1, member_count):
        near_copy(away).start()
    for away in range(1, member_count):
        packed_copy(away).start()
    own_copy.start()
    total = part_ref[member]
    for away in range(1, member_count):
        near_copy(away).wait_recv()
        total = total + near[away]
    held[...] = total
    for away in range(1, group_count):
        far_copy(away).start()

    for away in range(1, member_count):
        packed_copy(away).wait_recv()
    own_copy.wait()
    for away in range(1, group_count):
        far_copy(away).wait_recv()
        total = total + far[away]
    sum_ref[...] = total
    for away in range(1, member_count):
        near_copy(away).wait_send()
        packed_copy(away).wait_send()
    for away in range(1, group_count):
        far_copy(away).wait_send()


def finale(packed, parts, group_count, collective_id):
    member_count, lines, lanes = parts.shape
    shard = packed.shape[0] // member_count
    in_vmem = pl.BlockSpec(memory_space=pltpu.VMEM)
    any_space = pl.BlockSpec(memory_space=pl.ANY)
    members_dma = pltpu.SemaphoreType.DMA((member_count,))
    groups_dma = pltpu.SemaphoreType.DMA((group_count,))
    return pl.pallas_call(
        functools.partial(finale_kernel, member_count, group_count),
        out_shape=[
            jax.ShapeDtypeStruct((member_count, shard, packed.shape[1]), BF16),
            jax.ShapeDtypeStruct((lines, lanes), F32),
        ],
        in_specs=[any_space, in_vmem],
        out_specs=[any_space, in_vmem],
        scratch_shapes=[
            pltpu.VMEM((member_count, lines, lanes), F32),
            pltpu.VMEM((lines, lanes), F32),
            pltpu.VMEM((group_count, lines, lanes), F32),
            members_dma,
            members_dma,
            pltpu.SemaphoreType.DMA,
            members_dma,
            members_dma,
            groups_dma,
            groups_dma,
        ],
        compiler_params=pltpu.CompilerParams(collective_id=collective_id, has_side_effects=True),
        cost_estimate=pl.CostEstimate(flops=0, bytes_accessed=40000000, transcendentals=0),
        name="finale",
    )(packed, parts)


def local_call(kernel, name, out_shape, *operands):
    in_vmem = pl.BlockSpec(memory_space=pltpu.VMEM)
    size = sum(value.size * value.dtype.itemsize for value in operands[1:])
    size += sum(value.size * value.dtype.itemsize for value in out_shape)
    return pl.pallas_call(
        kernel,
        grid_spec=pltpu.PrefetchScalarGridSpec(
            num_scalar_prefetch=1,
            in_specs=[in_vmem] * (len(operands) - 1),
            out_specs=[in_vmem] * len(out_shape),
            grid=(),
        ),
        out_shape=out_shape,
        compiler_params=pltpu.CompilerParams(vmem_limit_bytes=VMEM_BYTES),
        cost_estimate=pl.CostEstimate(flops=0, bytes_accessed=size, transcendentals=0),
        name=name,
    )(*operands)


def rows_apart(member, value, member_count, column=0):
    rows = value.shape[0] // member_count

    def kernel(member_ref, value_ref, *out_refs):
        for away, out_ref in enumerate(out_refs):
            other = member_ref[0] ^ away
            out_ref[...] = value_ref[pl.ds(pl.multiple_of(other * rows, rows), rows), column:]

    shape = jax.ShapeDtypeStruct((rows, value.shape[1] - column), value.dtype)
    return local_call(kernel, "rows_apart", [shape] * member_count, member, value)


def rows_together(member, blocks, chunks):
    rows, width = blocks[0].shape
    part = width // chunks
    count = len(blocks)

    def kernel(member_ref, *refs):
        for away in range(count):
            where = pl.ds(pl.multiple_of((member_ref[0] ^ away) * rows, rows), rows)
            for chunk in range(chunks):
                refs[count + chunk][where, :] = refs[away][:, chunk * part : (chunk + 1) * part]

    shape = jax.ShapeDtypeStruct((count * rows, part), blocks[0].dtype)
    return local_call(kernel, "rows_together", [shape] * chunks, member, *blocks)


def columns_together(member, blocks):
    rows, width = blocks[0].shape
    count = len(blocks)

    def kernel(member_ref, *refs):
        for away in range(count):
            where = pl.ds(pl.multiple_of((member_ref[0] ^ away) * width, width), width)
            refs[count][:, where] = refs[away][...]

    shape = jax.ShapeDtypeStruct((rows, count * width), blocks[0].dtype)
    return local_call(kernel, "columns_together", [shape], member, *blocks)[0]


def exchanged(blocks):
    return [blocks[0]] + [
        lax.ppermute(blocks[away], "fsdp", [(m, m ^ away) for m in range(len(blocks))])
        for away in range(1, len(blocks))
    ]


def added(left, right):
    return left.astype(F32) + right.astype(F32)


def send_to(value, member_count, partner):
    return lax.ppermute(value, "fsdp", [(m, partner(m)) for m in range(member_count)])


def hopped(step, member_count):
    masks = plane_masks(member_count)
    return lambda m: (m ^ masks[step]) if m % 2 == 0 else (m ^ masks[-1 - step])


def unit_strips(member_count, group_count, chunks, per):
    share = group_count // chunks
    for chunk in range(chunks):
        for side in range(2):
            for place in range(share):
                group = chunk * share + place
                yield chunk, side, (side * share + place) * per, group * member_count * per


def units_apart(member, gate, up, gain, member_count, group_count, chunks):
    shard, width = gate.shape
    per = width // (member_count * group_count)
    columns = 2 * group_count * per
    strips = list(unit_strips(member_count, group_count, chunks, per))
    shape = jax.ShapeDtypeStruct((shard, columns), BF16)
    if per % 128:
        scaled = [(value * gain).astype(BF16) for value in (gate, up)]

        def block(away):
            other = member[0] ^ away
            return jnp.concatenate(
                [
                    lax.dynamic_slice_in_dim(scaled[side], base + other * per, per, 1)
                    for chunk, side, column, base in strips
                ],
                axis=1,
            )

        return [block(away) for away in range(member_count)]

    def kernel(member_ref, gate_ref, up_ref, gain_ref, *out_refs):
        for away, out_ref in enumerate(out_refs):
            other = member_ref[0] ^ away
            for chunk, side, column, base in strips:
                where = pl.ds(pl.multiple_of(base + other * per, per), per)
                source = (gate_ref, up_ref)[side][:, where].astype(F32)
                column += chunk * (columns // chunks)
                out_ref[:, column : column + per] = (source * gain_ref[...]).astype(BF16)

    return local_call(kernel, "units_apart", [shape] * member_count, member, gate, up, gain)


def units_together(member, chunk_blocks, gain, down, member_count, group_count):
    chunks = len(chunk_blocks)
    shard, columns = chunk_blocks[0][0].shape
    per = columns * chunks // (2 * group_count)
    width = per * member_count * group_count
    strips = list(unit_strips(member_count, group_count, chunks, per))
    blocks = [block for group in chunk_blocks for block in group]
    if per % 128:
        results = []
        for side in range(2):
            result = jnp.zeros((shard, width), F32)
            for away in range(member_count):
                other = member[0] ^ away
                for chunk, this, column, base in strips:
                    if this == side:
                        piece = chunk_blocks[chunk][away][:, column : column + per]
                        result = lax.dynamic_update_slice_in_dim(
                            result, piece.astype(F32) * gain, base + other * per, 1
                        )
            results.append(result)
        return *results, down.astype(F32)

    def kernel(member_ref, gain_ref, down_ref, *refs):
        outs = refs[len(blocks) :]
        outs[2][...] = down_ref[...].astype(F32)
        for away in range(member_count):
            other = member_ref[0] ^ away
            for chunk, side, column, base in strips:
                where = pl.ds(pl.multiple_of(base + other * per, per), per)
                piece = refs[chunk * member_count + away][:, column : column + per]
                outs[side][:, where] = piece.astype(F32) * gain_ref[...]

    shape = jax.ShapeDtypeStruct((shard, width), F32)
    shapes = [shape, shape, jax.ShapeDtypeStruct(down.shape, F32)]
    return local_call(kernel, "units_together", shapes, member, gain, down, *blocks)


def heads_together(member, arrived, gain, heads):
    count, shard, columns = arrived.shape
    width = heads * HD
    out_width = columns - width - 2 * HD
    copies = count // KVH

    def kernel(member_ref, arrived_ref, gain_ref, query_out, key_out, value_out, out_out):
        row = lax.broadcasted_iota(jnp.int32, (width, width), 0)
        column = lax.broadcasted_iota(jnp.int32, (width, width), 1)
        source = column % HD // HALF * (HALF * heads) + column // HD * HALF + column % HALF
        order = (row == source).astype(BF16)
        pair_row = lax.broadcasted_iota(jnp.int32, (2 * HD, KVH * HD), 0)
        pair_column = lax.broadcasted_iota(jnp.int32, (2 * HD, KVH * HD), 1)
        gain_here = gain_ref[...]
        keys = jnp.zeros((shard, KVH * HD), F32)
        values = jnp.zeros((shard, KVH * HD), F32)
        for away in range(count):
            other = (member_ref[0] + count - away) % count
            where = pl.ds(pl.multiple_of(other * width, width), width)
            query_out[:, where] = dot_nn(arrived_ref[away, :, :width], order) * gain_here
            pair = arrived_ref[away, :, width : width + 2 * HD]
            first = other // copies * HD
            to_keys = (pair_column == pair_row + first) & (pair_row < HD)
            to_values = (pair_column == pair_row - HD + first) & (pair_row >= HD)
            keys = keys + dot_nn(pair, to_keys.astype(BF16))
            values = values + dot_nn(pair, to_values.astype(BF16))
            out_where = pl.ds(pl.multiple_of(other * out_width, out_width), out_width)
            out_out[:, out_where] = arrived_ref[away, :, width + 2 * HD :].astype(F32)
        key_out[...] = keys * gain_here
        value_out[...] = values * gain_here

    shapes = [
        jax.ShapeDtypeStruct((shard, size), F32)
        for size in (count * width, KVH * HD, KVH * HD, count * out_width)
    ]
    return local_call(kernel, "heads_together", shapes, member, arrived, gain)


def units_kernel(normed_ref, gradient_ref, both_ref, down_ref, hidden_ref, grad_ref):
    units = down_ref.shape[0]
    normed = normed_ref[...]
    gradient = gradient_ref[...]
    part = min(256, units)
    for first in range(0, units, part):
        where = slice(first, first + part)
        past = slice(units + first, units + first + part)
        gate = dot_nn(normed, both_ref[:, where])
        up = dot_nn(normed, both_ref[:, past])
        upstream = dot_nt(gradient, down_ref[where, :])
        sigmoid = jax.nn.sigmoid(gate)
        active = gate * sigmoid
        hidden_ref[:, where] = (active * up).astype(BF16)
        grad_ref[:, where] = (
            upstream * up * sigmoid * (1.0 + gate * (1.0 - sigmoid))
        ).astype(BF16)
        grad_ref[:, past] = (upstream * active).astype(BF16)


def hidden_units(normed, gradient, both, down, chunk):
    tokens, model = normed.shape
    units = both.shape[1] // 2
    tile = 512
    by_tile = pl.BlockSpec((tile, model), lambda i: (i, 0))
    return pl.pallas_call(
        units_kernel,
        grid=(tokens // tile,),
        in_specs=[
            by_tile,
            by_tile,
            pl.BlockSpec(both.shape, lambda i: (0, 0)),
            pl.BlockSpec((units, model), lambda i: (chunk, 0)),
        ],
        out_specs=[
            pl.BlockSpec((tile, units), lambda i: (i, 0)),
            pl.BlockSpec((tile, 2 * units), lambda i: (i, 0)),
        ],
        out_shape=[
            jax.ShapeDtypeStruct((tokens, units), BF16),
            jax.ShapeDtypeStruct((tokens, 2 * units), BF16),
        ],
        compiler_params=pltpu.CompilerParams(vmem_limit_bytes=VMEM_BYTES),
        cost_estimate=pl.CostEstimate(
            flops=6 * tokens * model * units,
            bytes_accessed=4 * tokens * model + 6 * units * model,
            transcendentals=tokens * units,
        ),
        name="hidden_units",
    )(normed, gradient, both, down)


def half_group(shape, heads):
    return (lax.broadcasted_iota(jnp.int32, shape, 1) // HALF) % heads


def full_group(shape):
    return lax.broadcasted_iota(jnp.int32, shape, 1) // HD


def spread_keys(width):
    heads = width // HD
    row = lax.broadcasted_iota(jnp.int32, (2 * HD, width), 0)
    column = lax.broadcasted_iota(jnp.int32, (2 * HD, width), 1)
    source = column // (HALF * heads) * HALF + column % HALF
    return (row == source).astype(F32)


def spread_values(width):
    row = lax.broadcasted_iota(jnp.int32, (2 * HD, width), 0)
    column = lax.broadcasted_iota(jnp.int32, (2 * HD, width), 1)
    return (row == HD + column % HD).astype(F32)


def split(value):
    high = value.astype(BF16)
    return high, (value - high.astype(F32)).astype(BF16)


def exact(value, choice):
    high, low = split(value)
    choice = choice.astype(BF16)
    return dot_nn(high, choice) + dot_nn(low, choice)


def tables(table, width):
    half = width // 2
    row = lax.broadcasted_iota(jnp.int32, (2 * HALF, half), 0)
    column = lax.broadcasted_iota(jnp.int32, (2 * HALF, half), 1) % HALF
    return (
        exact(table, row == column),
        exact(table, row == column + HALF),
    )


def turn(values, cosine, sine):
    half = cosine.shape[1]
    first = values[:, :half]
    second = values[:, half:]
    return jnp.concatenate([first * cosine - second * sine, second * cosine + first * sine], axis=1)


def forward_kernel(
    heads,
    first_ref,
    normed_ref,
    weight_ref,
    table_ref,
    start_ref,
    query_ref,
    key_ref,
    key_columns_ref,
    value_ref,
    mixed_ref,
    lse_ref,
    value_columns,
    top,
    total,
    acc,
):
    step = pl.program_id(0)
    width = heads * HD
    start = start_ref[...]
    cosine, sine = tables(table_ref[...], width)
    projected = dot_nn(normed_ref[...], weight_ref[:, : width + 2 * HD])
    query = turn(projected[:, :width], cosine, sine).astype(BF16) * ATTENTION_SCALE
    pair = projected[:, width:]
    keys_here = turn(exact(pair, spread_keys(width)), cosine, sine).astype(BF16)
    own_rows = pl.ds(pl.multiple_of(step * BLOCK, BLOCK), BLOCK)
    query_ref[...] = query
    key_ref[own_rows, :] = keys_here
    turned_keys = jnp.transpose(keys_here.astype(F32)).astype(BF16)
    key_columns_ref[:HALF, :] = turned_keys[:HALF, :]
    key_columns_ref[HALF:, :] = turned_keys[width // 2 : width // 2 + HALF, :]
    value_ref[...] = dot_nn(pair.astype(BF16), spread_values(width).astype(BF16)).astype(BF16)
    value_columns[:, own_rows] = jnp.transpose(pair)[HD:, :].astype(BF16)
    token = step * BLOCK + lax.broadcasted_iota(jnp.int32, (BLOCK, BLOCK), 1)
    within = lax.broadcasted_iota(jnp.int32, (BLOCK, BLOCK), 0)
    lane_head = half_group((BLOCK, width), heads)
    top[...] = jnp.full_like(top, MASKED)
    total[...] = jnp.zeros_like(total)
    acc[...] = jnp.zeros_like(acc)

    def one_block(block, carried):
        offset = pl.multiple_of(block * BLOCK, BLOCK)
        keys = key_ref[pl.ds(offset, BLOCK), :]
        values = value_columns[:, pl.ds(offset, BLOCK)]
        place = offset + within
        visible = (place >= start) & (place <= token)
        for head in range(heads):
            own_keys = jnp.where(lane_head == head, keys, jnp.zeros_like(keys))
            scores = jnp.where(visible, dot_nt(own_keys, query), MASKED)
            old = top[head : head + 1, :]
            new = jnp.maximum(old, jnp.max(scores, axis=0, keepdims=True))
            weights = jnp.exp(scores - new)
            fade = jnp.exp(old - new)
            top[head : head + 1, :] = new
            total[head : head + 1, :] = total[head : head + 1, :] * fade + jnp.sum(
                weights, axis=0, keepdims=True
            )
            acc[head * HD : (head + 1) * HD, :] = acc[
                head * HD : (head + 1) * HD, :
            ] * fade + dot_nn(values, weights.astype(BF16))
        return carried

    lax.fori_loop(first_ref[step], step + 1, one_block, 0)
    for head in range(heads):
        acc[head * HD : (head + 1) * HD, :] = (
            acc[head * HD : (head + 1) * HD, :] / total[head : head + 1, :]
        )
    mixed_ref[...] = jnp.transpose(acc[...]).astype(BF16)
    lse_ref[...] = top[...] + jnp.log(total[...])


def attention_forward(first, normed, weight, table, start, heads):
    tokens, model = normed.shape
    width = heads * HD
    by_block = pl.BlockSpec((BLOCK, width), lambda i, first: (i, 0))
    whole = pl.BlockSpec((tokens, width), lambda i, first: (0, 0))
    return pl.pallas_call(
        functools.partial(forward_kernel, heads),
        grid_spec=pltpu.PrefetchScalarGridSpec(
            num_scalar_prefetch=1,
            grid=(tokens // BLOCK,),
            in_specs=[
                pl.BlockSpec((BLOCK, model), lambda i, first: (i, 0)),
                pl.BlockSpec(weight.shape, lambda i, first: (0, 0)),
                pl.BlockSpec((BLOCK, 2 * HALF), lambda i, first: (i, 0)),
                pl.BlockSpec((1, BLOCK), lambda i, first: (0, i)),
            ],
            out_specs=[
                by_block,
                whole,
                pl.BlockSpec((HD, BLOCK), lambda i, first: (0, i)),
                by_block,
                by_block,
                pl.BlockSpec((heads, BLOCK), lambda i, first: (0, i)),
            ],
            scratch_shapes=[
                pltpu.VMEM((HD, tokens), BF16),
                pltpu.VMEM((heads, BLOCK), F32),
                pltpu.VMEM((heads, BLOCK), F32),
                pltpu.VMEM((width, BLOCK), F32),
            ],
        ),
        out_shape=[jax.ShapeDtypeStruct((tokens, width), BF16)] * 2
        + [jax.ShapeDtypeStruct((HD, tokens), BF16)]
        + [jax.ShapeDtypeStruct((tokens, width), BF16)] * 2
        + [jax.ShapeDtypeStruct((heads, tokens), F32)],
        compiler_params=pltpu.CompilerParams(vmem_limit_bytes=VMEM_BYTES),
        cost_estimate=pl.CostEstimate(
            flops=64 * tokens * BLOCK * width, bytes_accessed=8 * tokens * width, transcendentals=0
        ),
        name="attention_forward",
    )(first, normed, weight, table, start)


def backward_kernel(
    heads,
    first_ref,
    query_ref,
    key_ref,
    key_columns_ref,
    value_ref,
    mixed_ref,
    grad_ref,
    weight_ref,
    lse_ref,
    start_ref,
    table_ref,
    out_ref,
    weight_grad_ref,
    dquery,
    dkey,
    dvalue,
    weight_grad,
):
    step = pl.program_id(0)
    query = query_ref[...]
    grad_one = grad_ref[...]
    grad = dot_nt(grad_one, weight_ref[...]).astype(BF16)
    start = start_ref[...]
    width = query.shape[1]
    token = step * BLOCK + lax.broadcasted_iota(jnp.int32, (BLOCK, BLOCK), 1)
    within = lax.broadcasted_iota(jnp.int32, (BLOCK, BLOCK), 0)
    half_head = half_group((BLOCK, width), heads)
    full_head = full_group((BLOCK, width))
    zero = jnp.zeros((BLOCK, width), BF16)
    product = grad.astype(F32) * mixed_ref[...].astype(F32)
    chooser = (
        lax.broadcasted_iota(jnp.int32, (8, width), 0)
        == lax.broadcasted_iota(jnp.int32, (8, width), 1) // HD
    ).astype(BF16)
    high, low = split(product)
    correction = dot_nt(chooser, high) + dot_nt(chooser, low)

    @pl.when(step == 0)
    def _():
        dkey[...] = jnp.zeros_like(dkey)
        dvalue[...] = jnp.zeros_like(dvalue)
        weight_grad[...] = jnp.zeros_like(weight_grad)

    weight_grad[...] += dot_tn(mixed_ref[...], grad_one)
    dquery[...] = jnp.zeros_like(dquery)

    def one_block(block, carried):
        offset = pl.multiple_of(block * BLOCK, BLOCK)
        rows = pl.ds(offset, BLOCK)
        keys = key_ref[rows, :]
        values = value_ref[rows, :]
        key_columns = key_columns_ref[:, rows]
        place = offset + within
        visible = (place >= start) & (place <= token)
        new_key = dkey[rows, :]
        new_value = dvalue[rows, :]
        for head in range(heads):
            own_keys = jnp.where(half_head == head, keys, zero)
            own_values = jnp.where(full_head == head, values, zero)
            scores = dot_nt(own_keys, query)
            probs = jnp.where(visible, jnp.exp(scores - lse_ref[head : head + 1, :]), 0.0)
            pressure = dot_nt(own_values, grad)
            dscores = (probs * (pressure - correction[head : head + 1, :])).astype(BF16)
            new_value = new_value + dot_nn(
                probs.astype(BF16), jnp.where(full_head == head, grad, zero)
            )
            new_key = new_key + dot_nn(dscores, jnp.where(half_head == head, query, zero))
            term = dot_nn(key_columns, dscores)
            low = slice(head * HALF, (head + 1) * HALF)
            high = slice(width // 2 + head * HALF, width // 2 + (head + 1) * HALF)
            dquery[low, :] += term[:HALF]
            dquery[high, :] += term[HALF:]
        dkey[rows, :] = new_key
        dvalue[rows, :] = new_value
        return carried

    lax.fori_loop(first_ref[step], step + 1, one_block, 0)
    own_rows = pl.ds(pl.multiple_of(step * BLOCK, BLOCK), BLOCK)
    cosine, sine = tables(table_ref[own_rows, :], width)
    out_ref[own_rows, :width] = (
        turn(jnp.transpose(dquery[...]), cosine, -sine) * ATTENTION_SCALE
    ).astype(BF16)

    @pl.when(step == pl.num_programs(0) - 1)
    def _():
        def fold(block, carried):
            rows = pl.ds(pl.multiple_of(block * BLOCK, BLOCK), BLOCK)
            cosine, sine = tables(table_ref[rows, :], width)
            turned = turn(dkey[rows, :], cosine, -sine)
            out_ref[rows, width:] = (
                dot_nt(turned.astype(BF16), spread_keys(width).astype(BF16))
                + dot_nt(dvalue[rows, :].astype(BF16), spread_values(width).astype(BF16))
            ).astype(BF16)
            return carried

        lax.fori_loop(0, pl.num_programs(0), fold, 0)
        weight_grad_ref[...] = weight_grad[...].astype(BF16)


def attention_backward(
    first, query, keys, key_columns, values, mixed, grad, weight, lse, start, table
):
    tokens, width = query.shape
    model = grad.shape[1]
    heads = width // HD
    columns = width + 2 * HD
    by_block = pl.BlockSpec((BLOCK, width), lambda i, first: (i, 0))
    whole = pl.BlockSpec((tokens, width), lambda i, first: (0, 0))
    return pl.pallas_call(
        functools.partial(backward_kernel, heads),
        grid_spec=pltpu.PrefetchScalarGridSpec(
            num_scalar_prefetch=1,
            grid=(tokens // BLOCK,),
            in_specs=[
                by_block,
                whole,
                pl.BlockSpec((HD, tokens), lambda i, first: (0, 0)),
                whole,
                by_block,
                pl.BlockSpec((BLOCK, model), lambda i, first: (i, 0)),
                pl.BlockSpec((width, model), lambda i, first: (0, 0)),
                pl.BlockSpec((heads, BLOCK), lambda i, first: (0, i)),
                pl.BlockSpec((1, BLOCK), lambda i, first: (0, i)),
                pl.BlockSpec((tokens, 2 * HALF), lambda i, first: (0, 0)),
            ],
            out_specs=[
                pl.BlockSpec((tokens, columns), lambda i, first: (0, 0)),
                pl.BlockSpec((width, model), lambda i, first: (0, 0)),
            ],
            scratch_shapes=[
                pltpu.VMEM((width, BLOCK), F32),
                pltpu.VMEM((tokens, width), F32),
                pltpu.VMEM((tokens, width), F32),
                pltpu.VMEM((width, model), F32),
            ],
        ),
        out_shape=[
            jax.ShapeDtypeStruct((tokens, columns), BF16),
            jax.ShapeDtypeStruct((width, model), BF16),
        ],
        compiler_params=pltpu.CompilerParams(vmem_limit_bytes=VMEM_BYTES),
        cost_estimate=pl.CostEstimate(
            flops=0, bytes_accessed=tokens * width, transcendentals=0
        ),
        name="attention_backward",
    )(first, query, keys, key_columns, values, mixed, grad, weight, lse, start, table)


def projection_grad(normed, grad, out_grad=None):
    tokens, model = normed.shape
    beside = () if out_grad is None else (out_grad,)
    columns, more = grad.shape[1], sum(value.shape[1] for value in beside)
    tile = 512

    def kernel(normed_ref, grad_ref, *refs):
        refs[-1][:, :columns] = dot_tn(normed_ref[...], grad_ref[...]).astype(BF16)
        if more:
            refs[-1][:, columns:] = refs[0][...]

    return pl.pallas_call(
        kernel,
        grid=(model // tile,),
        in_specs=[
            pl.BlockSpec((tokens, tile), lambda i: (0, i)),
            pl.BlockSpec((tokens, columns), lambda i: (0, 0)),
        ]
        + [pl.BlockSpec((tile, more), lambda i: (i, 0))] * len(beside),
        out_specs=pl.BlockSpec((tile, columns + more), lambda i: (i, 0)),
        out_shape=jax.ShapeDtypeStruct((model, columns + more), BF16),
        compiler_params=pltpu.CompilerParams(vmem_limit_bytes=VMEM_BYTES),
        cost_estimate=pl.CostEstimate(
            flops=2 * tokens * model * columns, bytes_accessed=2 * tokens * model, transcendentals=0
        ),
        name="projection_grad",
    )(normed, grad, *beside)


def token_starts(lengths_row, group_tokens):
    count = lengths_row.shape[0]
    order = jnp.arange(count, dtype=jnp.int32)
    finish = jnp.sum(jnp.where(order[None, :] <= order[:, None], lengths_row[None, :], 0), axis=1)
    place = jnp.arange(group_tokens, dtype=jnp.int32)
    passed = place[:, None] >= finish[None, :]
    return jnp.max(jnp.where(passed, finish[None, :], 0), axis=1), place


def inverse_norm(values):
    return lax.rsqrt(jnp.mean(values * values, axis=1, keepdims=True) + EPSILON)


def after(value, *earlier):
    return lax.optimization_barrier((value, *earlier))[0]


def sum_over_groups(value):
    return lax.psum_scatter(value, "dp", scatter_dimension=0, tiled=True)


def gather_groups(value):
    return lax.all_gather(value, "dp", axis=0, tiled=True)


def body(
    tokens,
    cotangent,
    query_weight,
    key_weight,
    value_weight,
    output_weight,
    gate_weight,
    up_weight,
    down_weight,
    attention_gain,
    feedforward_gain,
    lengths,
):
    members = lax.axis_size("fsdp")
    groups = lax.axis_size("dp")
    rows, model = tokens.shape
    group_tokens = rows * members
    shard = query_weight.shape[0]
    heads = NH // members
    width = heads * HD
    columns = width + 2 * HD
    copies = members // KVH
    out_columns = model // members
    down_rows = down_weight.shape[0]
    units = groups * down_rows // CHUNKS
    gain_one = attention_gain.astype(F32)[:, None]
    gain_two = feedforward_gain.astype(F32)[:, None]
    member = lax.axis_index("fsdp").astype(jnp.int32)[None]

    scaled_query = (query_weight * gain_one).astype(BF16)
    scaled_key = (key_weight * gain_one).astype(BF16)
    scaled_value = (value_weight * gain_one).astype(BF16)
    packed_in = jnp.concatenate(
        [
            scaled_query.reshape(shard, members, heads, 2, HALF)
            .transpose(1, 0, 3, 2, 4)
            .reshape(members, shard, width),
            jnp.repeat(
                scaled_key.reshape(shard, KVH, HD).transpose(1, 0, 2), copies, axis=0
            ),
            jnp.repeat(
                scaled_value.reshape(shard, KVH, HD).transpose(1, 0, 2), copies, axis=0
            ),
            output_weight.reshape(shard, members, out_columns).transpose(1, 0, 2),
        ],
        axis=2,
    )
    [packed_in] = plane_swap([packed_in], members, 1)
    packed_in = packed_in.reshape(members * shard, columns + out_columns)
    inputs = tokens.astype(F32)
    inverse_one = inverse_norm(inputs)
    start, place = token_starts(lengths[0], group_tokens)
    first = start[::BLOCK] // BLOCK
    frequency = ROPE_BASE ** (-(2.0 * jnp.arange(HALF, dtype=F32)) / HD)
    angles = (place - start).astype(F32)[:, None] * frequency[None, :]
    table = jnp.concatenate([jnp.cos(angles), jnp.sin(angles)], axis=1)
    start = start[None, :]

    gate_up = exchanged(
        units_apart(
            member, after(gate_weight, packed_in), up_weight, gain_two, members, groups, CHUNKS
        )
    )
    packed = gather_groups(packed_in)
    down_all = gather_groups(down_weight)
    normed_one = plane_gather(
        after((inputs * inverse_one).astype(BF16), packed_in), members, 0, True
    )
    upstream = cotangent.astype(F32)
    grad_two = (RESIDUAL_SCALE * upstream).astype(BF16)
    grad_two, down_all, table, first, start, _ = lax.optimization_barrier(
        (grad_two, down_all, table, first, start, normed_one)
    )
    grad_two = plane_gather(grad_two, members, 9, False)
    gate_up, grad_two = lax.optimization_barrier((gate_up, grad_two))
    gate_up_parts = rows_together(member, gate_up, CHUNKS)
    gate_up_chunks = [gather_groups(part) for part in gate_up_parts]
    packed, gate_up_parts = lax.optimization_barrier((packed, gate_up_parts))

    out_blocks = exchanged(rows_apart(member, packed, members, columns))
    query, keys, key_columns, values, mixed, lse = attention_forward(
        first, normed_one, packed, table, start, heads
    )
    mixed_then, out_blocks = lax.optimization_barrier((mixed, out_blocks))
    out_piece = columns_together(member, out_blocks)
    branch_one = product_scatter([mixed_then], [out_piece], False, members, 2, True)
    residual = inputs + RESIDUAL_SCALE * branch_one

    inverse_two = inverse_norm(residual)
    normed_two = plane_gather((residual * inverse_two).astype(BF16), members, 3, False)
    fused = group_tokens <= 2048
    hiddens = []
    grad_boths = []
    gate_up_grads = []
    for chunk in range(CHUNKS):
        both_weight = gate_up_chunks[chunk]
        hidden, grad_both = hidden_units(normed_two, grad_two, both_weight, down_all, chunk)
        hiddens.append(hidden)
        grad_boths.append(grad_both)
        if chunk < CHUNKS - 1 or not fused:
            gate_up_grad = projection_grad(normed_two, grad_both)
            gate_up_grads.append(sum_over_groups(gate_up_grad))
            normed_two, grad_two, hiddens, grad_boths, _ = lax.optimization_barrier(
                (normed_two, grad_two, hiddens, grad_boths, gate_up_grad)
            )
    if fused:
        weighted_two, gate_up_grad = product_scatter(
            grad_boths, gate_up_chunks, True, members, 4, False, normed_two
        )
        gate_up_grads.append(sum_over_groups(gate_up_grad))
    else:
        weighted_two = product_scatter(grad_boths, gate_up_chunks, True, members, 4, False)
    grad_residual = (
        upstream
        + inverse_two * weighted_two
        - residual * inverse_two**3 * jnp.mean(weighted_two * residual, axis=1, keepdims=True)
    )
    gain_term_two = jnp.sum(weighted_two * residual * inverse_two, axis=0)

    grad_one, down_grad, out_high, out_kept = plane_gather(
        (RESIDUAL_SCALE * grad_residual).astype(BF16),
        members,
        5,
        True,
        (hiddens, grad_two, down_all),
    )
    down_grad = sum_over_groups(down_grad)
    gate_up_grads[0] = exchanged(
        rows_apart(member, after(gate_up_grads[0], grad_one), members)
    )
    steps = len(plane_masks(members))
    half_rows = group_tokens // 4
    out_sent = send_to(out_high, members, hopped(steps - 1, members))
    grad_projected, out_grad = attention_backward(
        first, query, keys, key_columns, values, mixed, grad_one, out_piece, lse, start, table
    )
    out_grad = lax.all_to_all(out_grad, "fsdp", split_axis=1, concat_axis=0, tiled=True)
    packed_grad = projection_grad(normed_one, grad_projected, out_grad)
    gate_up_grads[1:] = [
        exchanged(rows_apart(member, part, members))
        for part in after(gate_up_grads[1:], grad_projected)
    ]
    grad_projected, packed_grad, gate_up_grads[0], out_sent, out_kept = lax.optimization_barrier(
        (grad_projected, packed_grad, gate_up_grads[0], out_sent, out_kept)
    )
    for step in reversed(range(steps - 1)):
        half_rows //= 2
        out_next = added(out_kept[half_rows:], out_sent[half_rows:]).astype(BF16)
        out_kept = added(out_kept[:half_rows], out_sent[:half_rows])
        if step:
            out_kept = out_kept.astype(BF16)
        out_sent = send_to(out_next, members, hopped(step, members))
    packed_grad = sum_over_groups(packed_grad)
    weighted_one = product_scatter([grad_projected], [packed], True, members, 6, True, weight=1)
    weighted_one, down_grad = lax.optimization_barrier((weighted_one, down_grad))
    grad_inputs = (
        grad_residual
        + inverse_one * weighted_one
        - inputs * inverse_one**3 * jnp.mean(weighted_one * inputs, axis=1, keepdims=True)
    )
    gain_term_one = jnp.sum(weighted_one * inputs * inverse_one, axis=0)

    gains = jnp.stack(
        [
            gain_term_one.reshape(groups, members, shard),
            gain_term_two.reshape(groups, members, shard),
        ],
        axis=2,
    ).reshape(groups, members, 2 * shard)
    gains = jnp.pad(
        gains.transpose(1, 0, 2), ((0, 0), (0, (-groups) % 8), (0, (-2 * shard) % 128))
    )
    output = (residual + RESIDUAL_SCALE * added(out_kept, out_sent)).astype(BF16)

    gate_grad, up_grad, down_grad = units_together(
        member, after(gate_up_grads, weighted_one), gain_two, down_grad, members, groups
    )
    arrived, gains = finale(packed_grad, gains, groups, 8)
    query_grad, key_grad, value_grad, out_grad = heads_together(member, arrived, gain_one, heads)
    gains = lax.dynamic_slice_in_dim(gains, lax.axis_index("dp"), 1, 0)[0, : 2 * shard]
    gains = gains.reshape(2, shard)
    return (
        output,
        grad_inputs.astype(BF16),
        query_grad,
        key_grad,
        value_grad,
        out_grad,
        gate_grad,
        up_grad,
        down_grad,
        gains[0] / gain_one[:, 0],
        gains[1] / gain_two[:, 0],
    )


def solution(mesh):
    by_rows = P(("dp", "fsdp"), None)
    by_entries = P(("dp", "fsdp"))
    return jax.shard_map(
        body,
        mesh=mesh,
        in_specs=(by_rows,) * 9 + (by_entries,) * 2 + (P("dp", None),),
        out_specs=(by_rows,) * 9 + (by_entries,) * 2,
        check_vma=False,
    )
```
